256 devices in a mesh: grp: 8 (over z), head: 32 (over y, x, core).
Axes of the slice: x: 4, y: 4, z: 8, core: 2. Of those that a mesh axis runs over, the one named last changes fastest.
Arguments:
- prefill_rows: bfloat16 [4096, 8192], P(('grp', 'head')), may hold values from -300 to 300
- row_group: int32 [4096], P(('grp', 'head')), may hold values from 0 to 7, as said below
- lengths: int32 [8, 16], replicated, may hold values from 1 to 128, 512 in all within a row
- decode_state: float32 [128, 8192], P('grp'), may hold values from -300 to 300
- norm_gain: float32 [8192], replicated, may hold values from 0.1 to 1.9
- w_query: bfloat16 [8192, 4096], P(None, 'head'), may hold values from -1 to 1
- w_key: bfloat16 [8192, 4096], P(None, 'head'), may hold values from -1 to 1
- w_value: bfloat16 [8192, 4096], P(None, 'head'), may hold values from -0.0625 to 0.0625
- w_out: bfloat16 [4096, 8192], P('head'), may hold values from -0.09375 to 0.09375
Outputs:
- final_state: float32 [128, 8192], P('grp', 'head')
The draws below stay inside these ranges and needn't reach their ends.
Inputs may be any that keep to these rules, and one draw needn't show every extreme that they name: `row_group`: each device's 16 rows name any one group at most 3 times, and some device names some group exactly 3 times; over all devices every group is named exactly 512 times.
All inputs are finite; a program needn't handle non-finite values.
Results may differ from the reference program's by a relative error of at most 0.006.
Values may be sent and summed in bfloat16 or wider, within the bound.
No kernel may reach another device: no remote copies, remote signals or barrier semaphores. Data moves between devices by JAX's collectives and lax.ppermute only.
A program may use at most 64 MiB of HBM per device.

```python
import math
import jax
import jax.numpy as jnp
import numpy as np
from jax import lax

D = 8192
HD = 128
PF_DEV = 16
REQ_GRP = 16
STEPS = 4
HEADS = 32
PF = 4096
GROUP_ROWS = 512
MAXLEN = 128
NREQ = 128
N_GRP = 8


def drawn_rows(key, row_count):
    first = jax.random.fold_in(key, 0)
    values = jax.random.normal(first, (row_count, D), jnp.float32)
    return values


def drawn_weight(key):
    values = jax.random.normal(key, (D, HEADS * HD), jnp.float32) * D ** (-0.5)
    return values.astype(jnp.bfloat16)


def draw_prefill_rows(key, part):
    key = jax.random.fold_in(key, 1)
    return drawn_rows(key, PF).astype(jnp.bfloat16)


def draw_decode_state(key, part):
    key = jax.random.fold_in(key, 2)
    return drawn_rows(key, NREQ)


def draw_w_query(key, part):
    key = jax.random.fold_in(key, 3)
    return drawn_weight(key)


def draw_w_key(key, part):
    key = jax.random.fold_in(key, 4)
    return drawn_weight(key)


def draw_row_group(key, part):
    key = jax.random.fold_in(key, 5)
    first, second, third, fourth = jax.random.split(key, 4)
    device_count = PF // PF_DEV
    pair_count = device_count // 2
    base_count = PF_DEV // N_GRP
    spread_most = base_count // 2
    raised = jax.random.randint(first, (pair_count,), 0, N_GRP)
    lowered = (raised + 1 + jax.random.randint(second, (pair_count,), 0, N_GRP - 1)) % N_GRP
    amounts = jax.random.randint(third, (pair_count,), 0, spread_most + 1)
    amounts = amounts.at[0].set(spread_most)
    group_ids = jnp.arange(N_GRP, dtype=jnp.int32)
    change = amounts[:, None] * ((group_ids[None, :] == raised[:, None]).astype(jnp.int32) - (group_ids[None, :] == lowered[:, None]).astype(jnp.int32))
    counts = base_count + jnp.stack([change, -change], axis=1).reshape(device_count, N_GRP)
    bounds = jnp.cumsum(counts, axis=1)
    slots = jnp.arange(PF_DEV, dtype=jnp.int32)
    labels = jnp.sum((bounds[:, None, :] <= slots[None, :, None]).astype(jnp.int32), axis=-1)
    scores = jax.random.randint(fourth, (device_count, PF_DEV), 0, 1 << 20) * PF_DEV + slots[None, :]
    order = jnp.argsort(scores, axis=1, stable=True)
    labels = jnp.take_along_axis(labels, order, axis=1)
    return labels.reshape(PF).astype(jnp.int32)


def levels(own_key, extent, pieces, low, largest):
    gain, own = 1.0, jax.random.fold_in(own_key, 6)
    for dim, parts in pieces:
        steps = jnp.exp(jax.random.uniform(jax.random.fold_in(own, dim), (parts,), jnp.float32, low / len(pieces), largest / len(pieces)))
        gain = gain * jnp.repeat(steps, extent[dim] // parts).reshape([-1 if axis == dim else 1 for axis in range(len(extent))])
    return gain


def split_up(number_of, total, reach, lean):
    portions = [(1 << 20) // math.isqrt(grade ** lean) + 1 for grade in range(2, number_of + 1)]
    surplus, given = total - reach - (number_of - 1), [1] * (number_of - 1)
    while surplus > 0:
        candidates = [i for i in range(number_of - 1) if given[i] < reach]
        pool, remaining = sum([portions[i] for i in candidates]), surplus
        for i in candidates:
            addition = min(reach - given[i], max(1, remaining * portions[i] // pool), surplus)
            given[i] = given[i] + addition
            surplus = surplus - addition
    return np.array([reach] + given)


def uneven(key, number_of, total, reach, lean):
    if number_of == 2:
        one = jax.random.randint(key, (), max(1, total - reach), min(reach, total - 1) + 1)
        return jnp.stack([one, total - one])
    sizes = jnp.asarray(split_up(number_of, total, reach, lean), jnp.int32)
    twos = (number_of - 1) // 2
    giver, taker = sizes[1:1 + 2 * twos:2], sizes[2:2 + 2 * twos:2]
    slack = jnp.minimum(giver - 1, reach - taker)
    shifted = jax.random.randint(jax.random.fold_in(key, 1), (twos,), 0, 1 << 20) % (slack + 1)
    sizes = sizes.at[1:1 + 2 * twos:2].set(giver - shifted).at[2:2 + 2 * twos:2].set(taker + shifted)
    return sizes[jax.random.permutation(jax.random.fold_in(key, 2), number_of)]


def bell_draw(own_key, dims, width, limit, cuts=(), held_as=jnp.bfloat16):
    values = width * jax.random.normal(own_key, dims, jnp.float32)
    if cuts:
        values = values * levels(own_key, dims, cuts, -0.22, 0.18)
    return jnp.clip(values, -limit, limit).astype(held_as)


def setup_inputs(seed: int = 0) -> dict:
    key_list = jax.random.split(jax.random.key(seed), 10)
    return {
        "prefill_rows": draw_prefill_rows(jax.random.fold_in(key_list[9], 71), 0),
        "row_group": draw_row_group(jax.random.fold_in(key_list[9], 71), 0),
        "lengths": jax.vmap(lambda own: uneven(own, REQ_GRP, GROUP_ROWS, MAXLEN, 2))(jax.random.split(key_list[2], N_GRP)).reshape((N_GRP, REQ_GRP)).astype(jnp.int32),
        "decode_state": draw_decode_state(jax.random.fold_in(key_list[9], 71), 0),
        "norm_gain": jnp.clip(1.0 + 0.18 * jax.random.normal(key_list[4], (D,), jnp.float32), 0.1, 1.9),
        "w_query": draw_w_query(jax.random.fold_in(key_list[9], 71), 0),
        "w_key": draw_w_key(jax.random.fold_in(key_list[9], 71), 0),
        "w_value": bell_draw(key_list[7], (D, HEADS * HD), D ** -0.5, 0.0625, ((1, 32),)),
        "w_out": bell_draw(key_list[8], (HEADS * HD, D), (HEADS * HD) ** -0.5, 0.09375, ((0, 32),)),
    }


EPSILON = 1e-05
ROPE_BASE = 10000.0
MASKED = -1e+30

def normed(values, norm_gain):
    widened = values.astype(jnp.float32)
    factor = lax.rsqrt(lax.optimization_barrier(jnp.mean(widened * widened, axis=-1, keepdims=True)) + EPSILON)
    return (widened * factor * norm_gain).astype(jnp.bfloat16)

def rotary(values, positions):
    head_size = HD
    half_size = head_size // 2
    shaped = values.reshape(values.shape[:-1] + (values.shape[-1] // head_size, head_size))
    frequency = jnp.exp(jnp.arange(half_size, dtype=jnp.float32) * (-2.0 * math.log(ROPE_BASE) / head_size))
    angles = positions.astype(jnp.float32)[..., None] * frequency
    cosine = jnp.cos(angles)[..., None, :]
    sine_part = jnp.sin(angles)[..., None, :]
    first_half = shaped[..., :half_size]
    second_half = shaped[..., half_size:]
    turned = jnp.concatenate([first_half * cosine - second_half * sine_part, second_half * cosine + first_half * sine_part], axis=-1)
    return turned.reshape(values.shape)

def locate(groups, cell_ids, row_starts, row_ends):
    group_count = row_starts.shape[0]
    picked = groups[..., None] == jnp.arange(group_count, dtype=jnp.int32)
    first_cells = lax.optimization_barrier(jnp.sum(jnp.where(picked[..., None], row_starts, 0), axis=-2))
    last_cells = lax.optimization_barrier(jnp.sum(jnp.where(picked[..., None], row_ends, 0), axis=-2))
    inside = (cell_ids[..., None] >= first_cells) & (cell_ids[..., None] < last_cells)
    return lax.optimization_barrier(jnp.sum(jnp.where(inside, cell_ids[..., None] - first_cells, 0), axis=-1)).astype(jnp.int32)

def reference(prefill_rows, row_group, lengths, decode_state, norm_gain, w_query, w_key, w_value, w_out):
    group_ids = jnp.arange(N_GRP, dtype=jnp.int32)
    matches = (row_group[:, None] == group_ids[None, :]).astype(jnp.int32)
    earlier = jnp.cumsum(matches, axis=0) - matches
    cell_ids = lax.optimization_barrier(jnp.sum(earlier * matches, axis=1)).astype(jnp.int32)
    row_ends = jnp.cumsum(lengths, axis=1).astype(jnp.int32)
    row_starts = row_ends - lengths
    places = locate(row_group, cell_ids, row_starts, row_ends)

    def project(block):
        rows_block, where_at = block
        normal_rows = normed(rows_block, norm_gain)
        keys = rotary(jnp.dot(normal_rows, w_key, preferred_element_type=jnp.float32), where_at).astype(jnp.bfloat16)
        values = jnp.dot(normal_rows, w_value, preferred_element_type=jnp.float32).astype(jnp.bfloat16)
        return (keys, values)
    keys, values = lax.map(project, (prefill_rows.reshape(N_GRP, GROUP_ROWS, D), places.reshape(N_GRP, GROUP_ROWS)))
    width_all = HEADS * HD
    cache_keys = jnp.zeros((N_GRP, GROUP_ROWS, width_all), jnp.bfloat16).at[row_group, cell_ids].set(keys.reshape(PF, width_all))
    cache_values = jnp.zeros((N_GRP, GROUP_ROWS, width_all), jnp.bfloat16).at[row_group, cell_ids].set(values.reshape(PF, width_all))
    cache_keys = cache_keys.reshape(N_GRP, GROUP_ROWS, HEADS, HD).astype(jnp.float32)
    cache_values = cache_values.reshape(N_GRP, GROUP_ROWS, HEADS, HD).astype(jnp.float32)
    segment = lax.optimization_barrier(jnp.sum((row_ends[:, None, :] <= jnp.arange(GROUP_ROWS, dtype=jnp.int32)[None, :, None]).astype(jnp.int32), axis=-1))
    cache_mask = (segment[:, None, :] == jnp.arange(REQ_GRP, dtype=jnp.int32)[None, :, None])[:, :, None, :]
    current = decode_state.reshape(N_GRP, REQ_GRP, D)
    new_keys = jnp.zeros((N_GRP, STEPS, REQ_GRP, HEADS, HD), jnp.float32)
    new_values = jnp.zeros((N_GRP, STEPS, REQ_GRP, HEADS, HD), jnp.float32)
    step_ids = jnp.arange(STEPS, dtype=jnp.int32)
    scale = HD ** (-0.5)
    for step in range(STEPS):
        positions_now = (lengths + step).reshape(-1)
        decode_rows = normed(current.reshape(NREQ, D), norm_gain)
        query = rotary(jnp.dot(decode_rows, w_query, preferred_element_type=jnp.float32), positions_now).astype(jnp.bfloat16)
        new_key = rotary(jnp.dot(decode_rows, w_key, preferred_element_type=jnp.float32), positions_now).astype(jnp.bfloat16)
        new_value = jnp.dot(decode_rows, w_value, preferred_element_type=jnp.float32).astype(jnp.bfloat16)
        query = lax.optimization_barrier(query).astype(jnp.float32).reshape(N_GRP, REQ_GRP, HEADS, HD)
        new_key = lax.optimization_barrier(new_key).astype(jnp.float32).reshape(N_GRP, REQ_GRP, HEADS, HD)
        new_value = lax.optimization_barrier(new_value).astype(jnp.float32).reshape(N_GRP, REQ_GRP, HEADS, HD)
        new_keys = new_keys.at[:, step].set(new_key)
        new_values = new_values.at[:, step].set(new_value)
        cache_scores = jnp.einsum('grhd,gchd->grhc', query, cache_keys) * scale
        fresh_scores = jnp.einsum('grhd,gsrhd->grhs', query, new_keys) * scale
        fresh_mask = step_ids <= step
        peak = jnp.maximum(lax.optimization_barrier(jnp.max(jnp.where(cache_mask, cache_scores, MASKED), axis=-1)), lax.optimization_barrier(jnp.max(jnp.where(fresh_mask, fresh_scores, MASKED), axis=-1)))
        cache_exp = jnp.where(cache_mask, jnp.exp(cache_scores - peak[..., None]), 0.0)
        fresh_exp = jnp.where(fresh_mask, jnp.exp(fresh_scores - peak[..., None]), 0.0)
        total = lax.optimization_barrier(jnp.sum(cache_exp, axis=-1)) + lax.optimization_barrier(jnp.sum(fresh_exp, axis=-1))
        cache_weights = lax.optimization_barrier((cache_exp / total[..., None]).astype(jnp.bfloat16)).astype(jnp.float32)
        fresh_weights = lax.optimization_barrier((fresh_exp / total[..., None]).astype(jnp.bfloat16)).astype(jnp.float32)
        attended = (jnp.einsum('grhc,gchd->grhd', cache_weights, cache_values) + jnp.einsum('grhs,gsrhd->grhd', fresh_weights, new_values)).astype(jnp.bfloat16)
        current = current + jnp.dot(attended.reshape(NREQ, HEADS * HD), w_out, preferred_element_type=jnp.float32).reshape(N_GRP, REQ_GRP, D)
    return current.reshape(NREQ, D)
```

```python
import math

import jax
import jax.numpy as jnp
from jax import lax
from jax.sharding import PartitionSpec as P

HD = 128
STEPS = 4
EPSILON = 1e-05
ROPE_BASE = 10000.0
MASKED = -1e30


def normed(values, norm_gain):
    widened = values.astype(jnp.float32)
    factor = lax.rsqrt(jnp.mean(widened * widened, axis=-1, keepdims=True) + EPSILON)
    return (widened * factor * norm_gain).astype(jnp.bfloat16)


def angles_of(positions):
    half = HD // 2
    frequency = jnp.exp(
        jnp.arange(half, dtype=jnp.float32) * (-2.0 * math.log(ROPE_BASE) / HD)
    )
    angles = positions.astype(jnp.float32)[..., None] * frequency
    cosine = jnp.cos(angles)
    sine = jnp.sin(angles)
    return (
        jnp.concatenate([cosine, cosine], axis=-1),
        jnp.concatenate([-sine, sine], axis=-1),
    )


def turned(values, cosine, sine):
    half = HD // 2
    swapped = jnp.concatenate([values[..., half:], values[..., :half]], axis=-1)
    return values * cosine + swapped * sine


def per_device(
    prefill_rows, row_group, lengths, decode_state, norm_gain, w_query, w_key, w_value, w_out
):
    groups = lax.axis_size("grp")
    heads = lax.axis_size("head")
    rows_local, width = prefill_rows.shape
    plane_rows = rows_local * heads
    cap = (rows_local // groups + rows_local // groups // 2) * heads
    requests = lengths.shape[1]
    my_group = lax.axis_index("grp")
    my_head = lax.axis_index("head")
    share = width // heads
    f32, bf16 = jnp.float32, jnp.bfloat16

    group_ids = jnp.arange(groups, dtype=jnp.int32)
    row_ends = jnp.cumsum(lengths, axis=1)
    row_starts = row_ends - lengths

    with jax.named_scope("rows"):
        normal_rows = normed(prefill_rows, norm_gain)
        plane = lax.all_gather(normal_rows, "head", axis=0, tiled=True)
    weights = jnp.concatenate([w_key, w_value, w_query], axis=1)

    with jax.named_scope("ids"):
        ids = lax.all_to_all(
            jnp.broadcast_to(row_group[None, :], (heads, rows_local)),
            "head", split_axis=0, concat_axis=0, tiled=True,
        ).reshape(plane_rows)
        match = ids[:, None] == group_ids[None, :]
        plane_counts = jnp.sum(match.astype(jnp.int32), axis=0)
        counts = lax.all_to_all(
            jnp.broadcast_to(plane_counts[None, :], (groups, groups)),
            "grp", split_axis=0, concat_axis=0, tiled=True,
        )
        first = jnp.cumsum(counts, axis=0) - counts
        lower = jnp.arange(plane_rows)[:, None] > jnp.arange(plane_rows)[None, :]
        order = jnp.dot(
            lower.astype(bf16), match.astype(bf16), preferred_element_type=f32
        ).astype(jnp.int32)
        order = jnp.sum(jnp.where(match, order, 0), axis=1)
        my_first = jnp.sum(jnp.where(group_ids[:, None] == my_group, first, 0), axis=0)
        cell = order + jnp.sum(jnp.where(match, my_first[None, :], 0), axis=1)
        starts = jnp.sum(jnp.where(match[:, :, None], row_starts[None], 0), axis=1)
        ends = jnp.sum(jnp.where(match[:, :, None], row_ends[None], 0), axis=1)
        inside = (cell[:, None] >= starts) & (cell[:, None] < ends)
        places = jnp.sum(jnp.where(inside, cell[:, None] - starts, 0), axis=1)
        slots = jnp.arange(cap, dtype=jnp.int32)
        pick = (
            (ids[None, None, :] == group_ids[:, None, None])
            & (order[None, None, :] == slots[None, :, None])
        ).astype(bf16)
        cosine, sine = angles_of(places)

    with jax.named_scope("project"):
        both = jnp.dot(plane, weights[:, : 2 * HD], preferred_element_type=f32)
        keys = turned(both[:, :HD], cosine, sine)
        packed = jnp.concatenate([keys, both[:, HD:]], axis=1).astype(bf16)
        outgoing = jnp.dot(
            pick.reshape(groups * cap, plane_rows), packed, preferred_element_type=f32
        ).astype(bf16)
        cache = lax.all_to_all(
            outgoing.reshape(groups, cap, 2 * HD), "grp", split_axis=0, concat_axis=0, tiled=True
        ).reshape(groups * cap, 2 * HD)

    mine = group_ids == my_group
    from_counts = jnp.sum(jnp.where(mine[None, :], counts, 0), axis=1)
    from_first = jnp.sum(jnp.where(mine[None, :], first, 0), axis=1)
    my_lengths = jnp.sum(jnp.where(mine[:, None], lengths, 0), axis=0)
    my_ends = jnp.sum(jnp.where(mine[:, None], row_ends, 0), axis=0)
    my_starts = my_ends - my_lengths
    slot_cell = jnp.where(
        slots[None, :] < from_counts[:, None], from_first[:, None] + slots[None, :], -1
    ).reshape(-1)
    mask = (slot_cell[None, :] >= my_starts[:, None]) & (slot_cell[None, :] < my_ends[:, None])
    cache_keys = cache[:, :HD]
    cache_values = cache[:, HD:]

    scale = HD ** (-0.5)
    new_keys, new_values = [], []
    current = lax.dynamic_slice_in_dim(decode_state, my_head * share, share, 1)
    my_gain = lax.dynamic_slice_in_dim(norm_gain, my_head * share, share, 0)
    inverse = 1.0 / norm_gain
    decode_rows = normed(decode_state, norm_gain)
    factor = None
    for step in range(STEPS):
        with jax.named_scope("decode"):
            projected = jnp.dot(decode_rows, weights, preferred_element_type=f32)
            if factor is not None:
                projected = projected * factor
            cos_now, sin_now = angles_of(my_lengths + step)
            new_key = turned(projected[:, :HD], cos_now, sin_now).astype(bf16)
            new_value = projected[:, HD : 2 * HD].astype(bf16)
            query = turned(projected[:, 2 * HD :], cos_now, sin_now).astype(bf16)
            new_keys.append(new_key)
            new_values.append(new_value)
            scores = jnp.einsum("rd,cd->rc", query, cache_keys, preferred_element_type=f32) * scale
            wide = query.astype(f32)
            fresh = jnp.stack(
                [jnp.sum(wide * k.astype(f32), axis=1) * scale for k in new_keys], axis=1
            )
            peak = jnp.maximum(
                jnp.max(jnp.where(mask, scores, MASKED), axis=1), jnp.max(fresh, axis=1)
            )
            cache_exp = jnp.where(mask, jnp.exp(scores - peak[:, None]), 0.0)
            fresh_exp = jnp.exp(fresh - peak[:, None])
            total = jnp.sum(cache_exp, axis=1) + jnp.sum(fresh_exp, axis=1)
            cache_weights = (cache_exp / total[:, None]).astype(bf16)
            fresh_weights = (fresh_exp / total[:, None]).astype(bf16).astype(f32)
            attended = jnp.dot(cache_weights, cache_values, preferred_element_type=f32)
            for back, value in enumerate(new_values):
                attended = attended + fresh_weights[:, back : back + 1] * value.astype(f32)
            term = jnp.dot(attended.astype(bf16), w_out, preferred_element_type=f32).astype(bf16)
        with jax.named_scope("sum"):
            parts = lax.all_to_all(
                term.reshape(requests, heads, share), "head", split_axis=1, concat_axis=1, tiled=True
            )
            current = current + jnp.sum(parts.astype(f32), axis=1)
        if step + 1 < STEPS:
            with jax.named_scope("spread"):
                piece = (current * my_gain[None, :]).astype(bf16)
                decode_rows = lax.all_to_all(
                    jnp.broadcast_to(piece[:, None, :], (requests, heads, share)),
                    "head", split_axis=1, concat_axis=1, tiled=True,
                ).reshape(requests, width)
                plain = decode_rows.astype(f32) * inverse
                factor = lax.rsqrt(jnp.mean(plain * plain, axis=1, keepdims=True) + EPSILON)
    return current


def solution(mesh):
    return jax.shard_map(
        per_device,
        mesh=mesh,
        in_specs=(
            P(("grp", "head"), None),
            P(("grp", "head")),
            P(),
            P("grp", None),
            P(),
            P(None, "head"),
            P(None, "head"),
            P(None, "head"),
            P("head", None),
        ),
        out_specs=P("grp", "head"),
        check_vma=False,
    )
```

```python
import math

import jax
import jax.numpy as jnp
from jax import lax
from jax.sharding import PartitionSpec as P

HD = 128
STEPS = 4
EPSILON = 1e-05
ROPE_BASE = 10000.0
MASKED = -1e30


def normed(values, norm_gain):
    widened = values.astype(jnp.float32)
    factor = lax.rsqrt(jnp.mean(widened * widened, axis=-1, keepdims=True) + EPSILON)
    return (widened * factor * norm_gain).astype(jnp.bfloat16)


def angles_of(positions):
    half = HD // 2
    frequency = jnp.exp(
        jnp.arange(half, dtype=jnp.float32) * (-2.0 * math.log(ROPE_BASE) / HD)
    )
    angles = positions.astype(jnp.float32)[..., None] * frequency
    cosine = jnp.cos(angles)
    sine = jnp.sin(angles)
    return (
        jnp.concatenate([cosine, cosine], axis=-1),
        jnp.concatenate([-sine, sine], axis=-1),
    )


def turned(values, cosine, sine):
    half = HD // 2
    swapped = jnp.concatenate([values[..., half:], values[..., :half]], axis=-1)
    return values * cosine + swapped * sine


NX = 4
NY = 4


def head_pairs(move):
    pairs = []
    for y in range(NY):
        for x in range(NX):
            for c in range(2):
                ty, tx, tc = move(y, x, c)
                pairs.append(((y * NX + x) * 2 + c, (ty * NX + tx) * 2 + tc))
    return pairs


def lane(first, second):
    return head_pairs(
        lambda y, x, c: (y ^ second, x ^ first, c) if c == 0 else (y ^ first, x ^ second, c)
    )


CORE = head_pairs(lambda y, x, c: (y, x, c ^ 1))


def send(values, pairs):
    return lax.ppermute(values, "head", pairs)


def gather_lane(normal_rows, core):
    half = normal_rows.shape[1] // 2
    n = normal_rows.shape[0]
    low, high = normal_rows[:, :half], normal_rows[:, half:]
    kept = jnp.where(core == 0, low, high)
    given = jnp.where(core == 0, high, low)
    start = jnp.concatenate([kept, send(given, CORE)])
    f1 = send(start, lane(1, 0))
    f3 = send(start, lane(3, 0))
    f2 = jnp.concatenate([send(f3[:n], lane(1, 0)), send(f1[n:], lane(3, 0))])
    line = jnp.concatenate([start, f1, f2, f3])
    s1 = send(line, lane(0, 1))
    s3 = send(line, lane(0, 3))
    early = s3.reshape(NX, 2, n, half)[:, 0].reshape(NX * n, half)
    late = s1.reshape(NX, 2, n, half)[:, 1].reshape(NX * n, half)
    s2 = jnp.concatenate([send(early, lane(0, 1)), send(late, lane(0, 3))])
    return line, s1, s3, s2


def per_device(
    prefill_rows, row_group, lengths, decode_state, norm_gain, w_query, w_key, w_value, w_out
):
    groups = lax.axis_size("grp")
    heads = lax.axis_size("head")
    rows_local, width = prefill_rows.shape
    plane_rows = rows_local * heads
    cap = (rows_local // groups + rows_local // groups // 2) * heads
    requests = lengths.shape[1]
    my_group = lax.axis_index("grp")
    my_head = lax.axis_index("head")
    share = width // heads
    f32, bf16 = jnp.float32, jnp.bfloat16

    group_ids = jnp.arange(groups, dtype=jnp.int32)
    row_ends = jnp.cumsum(lengths, axis=1)
    row_starts = row_ends - lengths

    core = my_head % 2
    half = width // 2
    with jax.named_scope("rows"):
        normal_rows = normed(prefill_rows, norm_gain)
        line, s1, s3, s2 = gather_lane(normal_rows, core)
    with jax.named_scope("weights"):
        kv = jnp.concatenate([w_key, w_value], axis=1)
        kept = jnp.where(core == 0, kv[:half], kv[half:])
        given = jnp.where(core == 0, kv[half:], kv[:half])
        half_weights = jnp.concatenate([kept, send(given, CORE)], axis=1)
        weights = jnp.concatenate([kv, w_query], axis=1)

    with jax.named_scope("ids"):
        ids = lax.all_to_all(
            jnp.broadcast_to(row_group[None, :], (heads, rows_local)),
            "head", split_axis=0, concat_axis=0, tiled=True,
        ).reshape(plane_rows)
        match = ids[:, None] == group_ids[None, :]
        plane_counts = jnp.sum(match.astype(jnp.int32), axis=0)
        counts = lax.all_to_all(
            jnp.broadcast_to(plane_counts[None, :], (groups, groups)),
            "grp", split_axis=0, concat_axis=0, tiled=True,
        )
        first = jnp.cumsum(counts, axis=0) - counts
        lower = jnp.arange(plane_rows)[:, None] > jnp.arange(plane_rows)[None, :]
        order = jnp.dot(
            lower.astype(bf16), match.astype(bf16), preferred_element_type=f32
        ).astype(jnp.int32)
        order = jnp.sum(jnp.where(match, order, 0), axis=1)
        my_first = jnp.sum(jnp.where(group_ids[:, None] == my_group, first, 0), axis=0)
        cell = order + jnp.sum(jnp.where(match, my_first[None, :], 0), axis=1)
        starts = jnp.sum(jnp.where(match[:, :, None], row_starts[None], 0), axis=1)
        ends = jnp.sum(jnp.where(match[:, :, None], row_ends[None], 0), axis=1)
        inside = (cell[:, None] >= starts) & (cell[:, None] < ends)
        places = jnp.sum(jnp.where(inside, cell[:, None] - starts, 0), axis=1)
        slots = jnp.arange(cap, dtype=jnp.int32)
        block = jnp.arange(heads, dtype=jnp.int32)
        d_second, d_first, d_core = block // (2 * NX), (block // 2) % NX, block % 2
        dy = jnp.where(core == 0, d_second, d_first)
        dx = jnp.where(core == 0, d_first, d_second)
        source = (
            ((my_head // (2 * NX)) ^ dy) * 2 * NX
            + (((my_head // 2) % NX) ^ dx) * 2
            + (core ^ d_core)
        )
        from_block = source[:, None] == block[None, :]

        def here(values):
            blocks = values.reshape(1, heads, rows_local)
            return jnp.sum(jnp.where(from_block[:, :, None], blocks, 0), axis=1).reshape(-1)

        ids, order, places = here(ids), here(order), here(places)
        pick = (
            (ids[None, None, :] == group_ids[:, None, None])
            & (order[None, None, :] == slots[None, :, None])
        ).astype(bf16)
        cosine, sine = angles_of(places)

    with jax.named_scope("project"):
        parts = [jnp.dot(r, half_weights, preferred_element_type=f32) for r in (line, s1, s2, s3)]
        parts[2] = parts[2].reshape(2, NX, rows_local, 4 * HD).swapaxes(0, 1).reshape(parts[1].shape)
        parts = jnp.stack(parts).reshape(NY, NX, 2, rows_local, 4 * HD)
        theirs = parts[..., 2 * HD :].swapaxes(0, 1)[:, :, ::-1]
        theirs = send(theirs.reshape(plane_rows, 2 * HD), CORE)
        both = parts[..., : 2 * HD].reshape(plane_rows, 2 * HD) + theirs
        keys = turned(both[:, :HD], cosine, sine)
        packed = jnp.concatenate([keys, both[:, HD:]], axis=1).astype(bf16)
        outgoing = jnp.dot(
            pick.reshape(groups * cap, plane_rows), packed, preferred_element_type=f32
        ).astype(bf16)
        cache = lax.all_to_all(
            outgoing.reshape(groups, cap, 2 * HD), "grp", split_axis=0, concat_axis=0, tiled=True
        ).reshape(groups * cap, 2 * HD)

    mine = group_ids == my_group
    from_counts = jnp.sum(jnp.where(mine[None, :], counts, 0), axis=1)
    from_first = jnp.sum(jnp.where(mine[None, :], first, 0), axis=1)
    my_lengths = jnp.sum(jnp.where(mine[:, None], lengths, 0), axis=0)
    my_ends = jnp.sum(jnp.where(mine[:, None], row_ends, 0), axis=0)
    my_starts = my_ends - my_lengths
    slot_cell = jnp.where(
        slots[None, :] < from_counts[:, None], from_first[:, None] + slots[None, :], -1
    ).reshape(-1)
    mask = (slot_cell[None, :] >= my_starts[:, None]) & (slot_cell[None, :] < my_ends[:, None])
    cache_keys = cache[:, :HD]
    cache_values = cache[:, HD:]

    scale = HD ** (-0.5)
    new_keys, new_values = [], []
    current = lax.dynamic_slice_in_dim(decode_state, my_head * share, share, 1)
    my_gain = lax.dynamic_slice_in_dim(norm_gain, my_head * share, share, 0)
    inverse = 1.0 / norm_gain
    decode_rows = normed(decode_state, norm_gain)
    factor = None
    for step in range(STEPS):
        with jax.named_scope("decode"):
            projected = jnp.dot(decode_rows, weights, preferred_element_type=f32)
            if factor is not None:
                projected = projected * factor
            cos_now, sin_now = angles_of(my_lengths + step)
            new_key = turned(projected[:, :HD], cos_now, sin_now).astype(bf16)
            new_value = projected[:, HD : 2 * HD].astype(bf16)
            query = turned(projected[:, 2 * HD :], cos_now, sin_now).astype(bf16)
            new_keys.append(new_key)
            new_values.append(new_value)
            scores = jnp.einsum("rd,cd->rc", query, cache_keys, preferred_element_type=f32) * scale
            wide = query.astype(f32)
            fresh = jnp.stack(
                [jnp.sum(wide * k.astype(f32), axis=1) * scale for k in new_keys], axis=1
            )
            peak = jnp.maximum(
                jnp.max(jnp.where(mask, scores, MASKED), axis=1), jnp.max(fresh, axis=1)
            )
            cache_exp = jnp.where(mask, jnp.exp(scores - peak[:, None]), 0.0)
            fresh_exp = jnp.exp(fresh - peak[:, None])
            total = jnp.sum(cache_exp, axis=1) + jnp.sum(fresh_exp, axis=1)
            cache_weights = (cache_exp / total[:, None]).astype(bf16)
            fresh_weights = (fresh_exp / total[:, None]).astype(bf16).astype(f32)
            attended = jnp.dot(cache_weights, cache_values, preferred_element_type=f32)
            for back, value in enumerate(new_values):
                attended = attended + fresh_weights[:, back : back + 1] * value.astype(f32)
            term = jnp.dot(attended.astype(bf16), w_out, preferred_element_type=f32).astype(bf16)
        with jax.named_scope("sum"):
            parts = lax.all_to_all(
                term.reshape(requests, heads, share), "head", split_axis=1, concat_axis=1, tiled=True
            )
            current = current + jnp.sum(parts.astype(f32), axis=1)
        if step + 1 < STEPS:
            with jax.named_scope("spread"):
                piece = (current * my_gain[None, :]).astype(bf16)
                decode_rows = lax.all_to_all(
                    jnp.broadcast_to(piece[:, None, :], (requests, heads, share)),
                    "head", split_axis=1, concat_axis=1, tiled=True,
                ).reshape(requests, width)
                plain = decode_rows.astype(f32) * inverse
                factor = lax.rsqrt(jnp.mean(plain * plain, axis=1, keepdims=True) + EPSILON)
    return current


def solution(mesh):
    return jax.shard_map(
        per_device,
        mesh=mesh,
        in_specs=(
            P(("grp", "head"), None),
            P(("grp", "head")),
            P(),
            P("grp", None),
            P(),
            P(None, "head"),
            P(None, "head"),
            P(None, "head"),
            P("head", None),
        ),
        out_specs=P("grp", "head"),
        check_vma=False,
    )
```

```python
import math

import jax
import jax.numpy as jnp
from jax import lax
from jax.experimental import pallas as pl
from jax.experimental.pallas import tpu as pltpu
from jax.sharding import PartitionSpec as P

HD = 128
STEPS = 4
EPSILON = 1e-05
ROPE_BASE = 10000.0
MASKED = -1e30


def normed(values, norm_gain):
    widened = values.astype(jnp.float32)
    factor = lax.rsqrt(jnp.mean(widened * widened, axis=-1, keepdims=True) + EPSILON)
    return (widened * factor * norm_gain).astype(jnp.bfloat16)


def angles_of(positions):
    half = HD // 2
    frequency = jnp.exp(
        jnp.arange(half, dtype=jnp.float32) * (-2.0 * math.log(ROPE_BASE) / HD)
    )
    angles = positions.astype(jnp.float32)[..., None] * frequency
    cosine = jnp.cos(angles)
    sine = jnp.sin(angles)
    return (
        jnp.concatenate([cosine, cosine], axis=-1),
        jnp.concatenate([-sine, sine], axis=-1),
    )


def turned(values, cosine, sine):
    half = HD // 2
    swapped = jnp.concatenate([values[..., half:], values[..., :half]], axis=-1)
    return values * cosine + swapped * sine


NX = 4
NY = 4
HELD = ((0, 0), (0, 1), (1, 0), (1, 1), (3, 0), (3, 1), (2, 0), (2, 1))
EARLY = 6
EMPTY = 1e30


def head_pairs(move):
    pairs = []
    for y in range(NY):
        for x in range(NX):
            for c in range(2):
                ty, tx, tc = move(y, x, c)
                pairs.append(((y * NX + x) * 2 + c, (ty * NX + tx) * 2 + tc))
    return pairs


def lane(first, second):
    return head_pairs(
        lambda y, x, c: (y ^ second, x ^ first, c) if c == 0 else (y ^ first, x ^ second, c)
    )


CORE = head_pairs(lambda y, x, c: (y, x, c ^ 1))


def send(values, pairs):
    return lax.ppermute(values, "head", pairs)


def after(values, piece):
    return values + (piece[0, 0].astype(jnp.float32) * 0.0).astype(values.dtype)


def params(mib):
    return pltpu.CompilerParams(vmem_limit_bytes=mib * 1024 * 1024)


def norm_split_kernel(group_ref, rows_ref, gain_ref, kept_ref, given_ref):
    n, half = rows_ref.shape[0], rows_ref.shape[1] // 2
    core = lax.rem(lax.axis_index("head"), 2)
    rows = rows_ref[...].astype(jnp.float32)
    factor = lax.rsqrt(jnp.mean(rows * rows, axis=1, keepdims=True) + EPSILON)
    result = (rows * factor * gain_ref[...]).astype(jnp.bfloat16)
    row = lax.broadcasted_iota(jnp.int32, (n, HD), 0)
    ids = jnp.zeros((n, HD), jnp.int32)
    for j in range(n):
        ids = jnp.where(row == j, group_ref[j], ids)
    ids = ids.astype(jnp.float32).astype(jnp.bfloat16)
    kept_ref[:, half:] = ids
    given_ref[:, half:] = ids

    @pl.when(core == 0)
    def _():
        kept_ref[:, :half] = result[:, :half]
        given_ref[:, :half] = result[:, half:]

    @pl.when(core == 1)
    def _():
        kept_ref[:, :half] = result[:, half:]
        given_ref[:, :half] = result[:, :half]


def norm_split(groups, rows, gain):
    shape = jax.ShapeDtypeStruct((rows.shape[0], rows.shape[1] // 2 + HD), jnp.bfloat16)
    whole = pl.BlockSpec(memory_space=pltpu.VMEM)
    return pl.pallas_call(
        norm_split_kernel,
        out_shape=(shape, shape),
        in_specs=[pl.BlockSpec(memory_space=pltpu.SMEM), whole, whole],
        compiler_params=params(8),
        name="norm_split",
    )(groups, rows, gain.reshape(1, -1))


def other_half_kernel(key_ref, value_ref, dep_ref, out_ref, sems):
    half = out_ref.shape[0]
    core = lax.rem(lax.axis_index("head"), 2)
    rows = pl.ds(pl.multiple_of((1 - core) * half, half), half)
    one = pltpu.make_async_copy(key_ref.at[rows], out_ref.at[:, :HD], sems.at[0])
    two = pltpu.make_async_copy(value_ref.at[rows], out_ref.at[:, HD:], sems.at[1])
    one.start()
    two.start()
    one.wait()
    two.wait()


def other_half(w_key, w_value, dep):
    anywhere = pl.BlockSpec(memory_space=pl.ANY)
    return pl.pallas_call(
        other_half_kernel,
        out_shape=jax.ShapeDtypeStruct((w_key.shape[0] // 2, 2 * HD), jnp.bfloat16),
        in_specs=[anywhere] * 3,
        out_specs=anywhere,
        scratch_shapes=[pltpu.SemaphoreType.DMA((2,))],
        compiler_params=params(4),
        name="other_half",
    )(w_key, w_value, dep)


CHUNKS = 4


def project_kernel(count, *refs):
    pieces = refs[:count]
    key_ref, value_ref, their_ref, own_ref, other_ref, ids_ref, x, w, piece_sems, weight_sems = refs[count:]
    size = pieces[0].shape[0]
    half = w.shape[0]
    depth = half // CHUNKS
    core = lax.rem(lax.axis_index("head"), 2)
    loads = []
    for k in range(CHUNKS):
        mine = pl.ds(pl.multiple_of(core * half + k * depth, depth), depth)
        here = slice(k * depth, (k + 1) * depth)
        loads.append(
            [
                pltpu.make_async_copy(key_ref.at[mine], w.at[here, :HD], weight_sems.at[k, 0]),
                pltpu.make_async_copy(
                    value_ref.at[mine], w.at[here, HD : 2 * HD], weight_sems.at[k, 1]
                ),
                pltpu.make_async_copy(
                    their_ref.at[here], w.at[here, 2 * HD :], weight_sems.at[k, 2]
                ),
            ]
        )
    rows = [
        pltpu.make_async_copy(p, x.at[i * size : (i + 1) * size], piece_sems.at[i])
        for i, p in enumerate(pieces)
    ]
    for load in loads[0]:
        load.start()
    for row in rows:
        row.start()
    for k in range(1, CHUNKS):
        for load in loads[k]:
            load.start()
    for row in rows:
        row.wait()
    ids_ref[...] = x[:, half:]
    for k in range(CHUNKS):
        for load in loads[k]:
            load.wait()
        here = slice(k * depth, (k + 1) * depth)
        term = jnp.dot(x[:, here], w[here, :], preferred_element_type=jnp.float32)
        if k == 0:
            own_ref[...] = term[:, : 2 * HD]
            other_ref[...] = term[:, 2 * HD :]
        else:
            own_ref[...] += term[:, : 2 * HD]
            other_ref[...] += term[:, 2 * HD :]


def project(pieces, w_key, w_value, their_half):
    count = len(pieces)
    size, wide = pieces[0].shape
    half = wide - HD
    rows = count * size
    anywhere = pl.BlockSpec(memory_space=pl.ANY)
    shape = jax.ShapeDtypeStruct((rows, 2 * HD), jnp.float32)
    return pl.pallas_call(
        lambda *refs: project_kernel(count, *refs),
        out_shape=(shape, shape, jax.ShapeDtypeStruct((rows, HD), jnp.bfloat16)),
        in_specs=[anywhere] * (count + 3),
        scratch_shapes=[
            pltpu.VMEM((rows, wide), jnp.bfloat16),
            pltpu.VMEM((half, 4 * HD), jnp.bfloat16),
            pltpu.SemaphoreType.DMA((count,)),
            pltpu.SemaphoreType.DMA((CHUNKS, 3)),
        ],
        compiler_params=params(16),
        name="project",
    )(*pieces, w_key, w_value, their_half)


def origin(shape, dim, head):
    at = lax.broadcasted_iota(jnp.int32, shape, dim)
    block, row = at >> 4, at & 15
    turn = block >> 3
    d_second, d_first, d_core = turn ^ (turn >> 1), block & 3, (block >> 2) & 1
    core = head & 1
    dy = jnp.where(core == 0, d_second, d_first)
    dx = jnp.where(core == 0, d_first, d_second)
    y, x, c = (head >> 3) ^ dy, ((head >> 1) & 3) ^ dx, core ^ d_core
    return (((y * NX + x) * 2 + c) << 4) + row


def finish_kernel(groups, own_a, own_b, their_a, their_b, ids_a, ids_b, out_ref, packed):
    total = packed.shape[0]
    n = total // (len(HELD) * NX)
    early = EARLY * NX
    head = lax.axis_index("head")
    cap = out_ref.shape[0] // groups

    def block(first, second, i):
        return first[i * n : (i + 1) * n] if i < early else second[(i - early) * n : (i - early + 1) * n]

    for at, (d_second, d_core) in enumerate(HELD):
        for d_first in range(NX):
            i = at * NX + d_first
            j = HELD.index((d_first, 1 - d_core)) * NX + d_second
            both = block(own_a, own_b, i) + block(their_a, their_b, j)
            packed[i * n : (i + 1) * n, :] = both.astype(jnp.bfloat16)
    ids = jnp.concatenate([ids_a[...], ids_b[...]], axis=0).astype(jnp.float32)
    lanes = lax.broadcasted_iota(jnp.int32, (total, HD), 1).astype(jnp.float32)
    match = jnp.where(ids == lanes, 1.0, 0.0)
    earlier = origin((total, total), 1, head) < origin((total, total), 0, head)
    ranks = jnp.dot(
        jnp.where(earlier, 1.0, 0.0).astype(jnp.bfloat16),
        match.astype(jnp.bfloat16),
        preferred_element_type=jnp.float32,
    )
    order = jnp.sum(ranks * match, axis=1, keepdims=True)
    slot = ids[:, :1] * cap + order
    slots = lax.broadcasted_iota(jnp.int32, (total, groups * cap), 1).astype(jnp.float32)
    pick = jnp.where(slots == slot, 1.0, 0.0).astype(jnp.bfloat16)
    routed = lax.dot_general(
        pick, packed[...], (((0,), (0,)), ((), ())), preferred_element_type=jnp.float32
    )
    counts = jnp.sum(match, axis=0, keepdims=True)
    step = lax.broadcasted_iota(jnp.int32, (cap, HD), 0).astype(jnp.float32)
    for g in range(groups):
        rows = slice(g * cap, (g + 1) * cap)
        filled = step < counts[:, g : g + 1]
        out_ref[rows, :HD] = jnp.where(filled, routed[rows, :HD], EMPTY).astype(jnp.bfloat16)
        out_ref[rows, HD:] = routed[rows, HD:].astype(jnp.bfloat16)


def finish(groups, slots, own_a, own_b, their_a, their_b, ids_a, ids_b):
    return pl.pallas_call(
        lambda *refs: finish_kernel(groups, *refs),
        out_shape=jax.ShapeDtypeStruct((slots, 2 * HD), jnp.bfloat16),
        scratch_shapes=[pltpu.VMEM((own_a.shape[0] + own_b.shape[0], 2 * HD), jnp.bfloat16)],
        compiler_params=params(24),
        name="finish",
    )(own_a, own_b, their_a, their_b, ids_a, ids_b)


def settle_kernel(groups, cache_ref, edge_row, edge_col, high_ref, low_ref, key_ref, bias_ref, hot):
    slots = cache_ref.shape[0]
    cap = slots // groups
    starts, ends = edge_row[0:1, :], edge_row[1:2, :]
    lanes = lax.broadcasted_iota(jnp.int32, (cap, HD), 1).astype(jnp.float32)
    step = lax.broadcasted_iota(jnp.int32, (cap, 1), 0).astype(jnp.float32)
    across = lax.broadcasted_iota(jnp.int32, (1, slots), 1).astype(jnp.float32)
    cells = across
    open_slots = across < 0.0
    base = jnp.zeros((1, 1), jnp.float32)
    for g in range(groups):
        rows = slice(g * cap, (g + 1) * cap)
        full = cache_ref[rows, :HD].astype(jnp.float32) < EMPTY / 2
        count = jnp.sum(jnp.where(full, 1.0, 0.0), axis=0, keepdims=True)[:, :1]
        cell = base + step
        inside = (cell >= starts) & (cell < ends)
        place = cell - jnp.sum(jnp.where(inside, starts, 0.0), axis=1, keepdims=True)
        hot[rows, :] = jnp.where(lanes == place, 1.0, 0.0).astype(jnp.bfloat16)
        here = (across >= g * cap) & (across < (g + 1) * cap)
        cells = jnp.where(here, across - g * cap + base, cells)
        open_slots = open_slots | (here & (across - g * cap < count))
        base = base + count
    low_edge, high_edge = edge_col[:, 0:1], edge_col[:, HD : HD + 1]
    mine = (cells >= low_edge) & (cells < high_edge) & open_slots
    bias_ref[...] = jnp.where(mine, 0.0, MASKED)
    trig = jnp.dot(hot[...], high_ref[...], preferred_element_type=jnp.float32)
    trig = trig + jnp.dot(hot[...], low_ref[...], preferred_element_type=jnp.float32)
    keys = cache_ref[:, :HD].astype(jnp.float32)
    keys = jnp.where(keys < EMPTY / 2, keys, 0.0)
    key_ref[...] = (keys * trig[:, :HD] + pltpu.roll(keys, HD // 2, 1) * trig[:, HD:]).astype(
        jnp.bfloat16
    )


def settle(groups, cache, edge_row, edge_col, high, low):
    slots = cache.shape[0]
    return pl.pallas_call(
        lambda *refs: settle_kernel(groups, *refs),
        out_shape=(
            jax.ShapeDtypeStruct((slots, HD), jnp.bfloat16),
            jax.ShapeDtypeStruct((edge_col.shape[0], slots), jnp.float32),
        ),
        scratch_shapes=[pltpu.VMEM((slots, HD), jnp.bfloat16)],
        compiler_params=params(16),
        name="settle",
    )(cache, edge_row, edge_col, high, low)


def per_device(
    prefill_rows, row_group, lengths, decode_state, norm_gain, w_query, w_key, w_value, w_out
):
    groups = lax.axis_size("grp")
    heads = lax.axis_size("head")
    rows_local, width = prefill_rows.shape
    plane_rows = rows_local * heads
    cap = (rows_local // groups + rows_local // groups // 2) * heads
    requests = lengths.shape[1]
    my_group = lax.axis_index("grp")
    my_head = lax.axis_index("head")
    share = width // heads
    f32, bf16 = jnp.float32, jnp.bfloat16

    core = my_head % 2
    with jax.named_scope("rows"):
        n = rows_local
        kept, given = norm_split(row_group, prefill_rows, norm_gain)
        got = send(given, CORE)
        start = jnp.concatenate([kept, got])
        f2 = send(start, lane(2, 0))
        f1 = send(start, lane(1, 0))
        f3 = send(start, lane(3, 0))
        l0 = jnp.concatenate([kept, f1[:n], f2[:n], f3[:n]])
        l1 = jnp.concatenate([got, f1[n:], f2[n:], f3[n:]])
        s11 = send(l1, lane(0, 1))
        s30 = send(l0, lane(0, 3))
        s10 = send(l0, lane(0, 1))
        s31 = send(l1, lane(0, 3))
        s20 = send(s30, lane(0, 1))
        s21 = send(s11, lane(0, 3))
    with jax.named_scope("weights"):
        their_half = send(other_half(w_key, w_value, f1), CORE)

    with jax.named_scope("places"):
        group_ids = jnp.arange(groups, dtype=jnp.int32)
        late_lengths = after(lengths, f1)
        my_lengths = jnp.sum(
            jnp.where((group_ids == my_group)[:, None], late_lengths, 0), axis=0
        )
        request = jnp.arange(requests, dtype=jnp.int32)
        my_ends = jnp.sum(jnp.where(request[None, :] <= request[:, None], my_lengths[None, :], 0), axis=1)
        my_starts = my_ends - my_lengths
        edges = jnp.stack([my_starts, my_ends]).astype(f32)
        edge_row = jnp.pad(edges, ((0, 0), (0, HD - requests)), constant_values=1e9)
        edge_col = jnp.repeat(edges, HD, axis=0).T.reshape(requests, 2 * HD)
        spots = jnp.arange(HD, dtype=jnp.int32) + 0 * my_lengths[0]
        table = jnp.concatenate(angles_of(spots), axis=1)
        table_high = table.astype(bf16)
        table_low = (table - table_high.astype(f32)).astype(bf16)

    with jax.named_scope("project"):
        own_a, other_a, ids_a = project([l0, l1, s10, s11, s30, s31], w_key, w_value, their_half)
        own_b, other_b, ids_b = project([s20, s21], w_key, w_value, their_half)
        outgoing = finish(
            groups, groups * cap, own_a, own_b, send(other_a, CORE), send(other_b, CORE), ids_a, ids_b
        )
        cache = lax.all_to_all(
            outgoing.reshape(groups, cap, 2 * HD), "grp", split_axis=0, concat_axis=0, tiled=True
        ).reshape(groups * cap, 2 * HD)
        cache_keys, bias = settle(groups, cache, edge_row, edge_col, table_high, table_low)
        cache_values = cache[:, HD:]

    scale = HD ** (-0.5)
    new_keys, new_values = [], []
    current = lax.dynamic_slice_in_dim(decode_state, my_head * share, share, 1)
    my_gain = lax.dynamic_slice_in_dim(norm_gain, my_head * share, share, 0)
    inverse = 1.0 / norm_gain
    decode_rows = normed(after(decode_state, f1), norm_gain)
    factor = None
    for step in range(STEPS):
        with jax.named_scope("decode"):
            scaled = 1.0 if factor is None else factor
            key_now = jnp.dot(decode_rows, w_key, preferred_element_type=f32) * scaled
            value_now = jnp.dot(decode_rows, w_value, preferred_element_type=f32) * scaled
            query_now = jnp.dot(decode_rows, w_query, preferred_element_type=f32) * scaled
            cos_now, sin_now = angles_of(my_lengths + step)
            new_key = turned(key_now, cos_now, sin_now).astype(bf16)
            new_value = value_now.astype(bf16)
            query = turned(query_now, cos_now, sin_now).astype(bf16)
            new_keys.append(new_key)
            new_values.append(new_value)
            scores = jnp.einsum("rd,cd->rc", query, cache_keys, preferred_element_type=f32) * scale
            wide = query.astype(f32)
            fresh = jnp.stack(
                [jnp.sum(wide * k.astype(f32), axis=1) * scale for k in new_keys], axis=1
            )
            scores = scores + bias
            peak = jnp.maximum(jnp.max(scores, axis=1), jnp.max(fresh, axis=1))
            cache_exp = jnp.exp(scores - peak[:, None])
            fresh_exp = jnp.exp(fresh - peak[:, None])
            total = jnp.sum(cache_exp, axis=1) + jnp.sum(fresh_exp, axis=1)
            cache_weights = (cache_exp / total[:, None]).astype(bf16)
            fresh_weights = (fresh_exp / total[:, None]).astype(bf16).astype(f32)
            attended = jnp.dot(cache_weights, cache_values, preferred_element_type=f32)
            for back, value in enumerate(new_values):
                attended = attended + fresh_weights[:, back : back + 1] * value.astype(f32)
            term = jnp.dot(attended.astype(bf16), w_out, preferred_element_type=f32).astype(bf16)
        with jax.named_scope("sum"):
            parts = lax.all_to_all(
                term.reshape(requests, heads, share), "head", split_axis=1, concat_axis=1, tiled=True
            )
            current = current + jnp.sum(parts.astype(f32), axis=1)
        if step + 1 < STEPS:
            with jax.named_scope("spread"):
                piece = (current * my_gain[None, :]).astype(bf16)
                decode_rows = lax.all_to_all(
                    jnp.broadcast_to(piece[:, None, :], (requests, heads, share)),
                    "head", split_axis=1, concat_axis=1, tiled=True,
                ).reshape(requests, width)
                plain = decode_rows.astype(f32) * inverse
                factor = lax.rsqrt(jnp.mean(plain * plain, axis=1, keepdims=True) + EPSILON)
    return current


def solution(mesh):
    return jax.shard_map(
        per_device,
        mesh=mesh,
        in_specs=(
            P(("grp", "head"), None),
            P(("grp", "head")),
            P(),
            P("grp", None),
            P(),
            P(None, "head"),
            P(None, "head"),
            P(None, "head"),
            P("head", None),
        ),
        out_specs=P("grp", "head"),
        check_vma=False,
    )
```

```python
import math

import jax
import jax.numpy as jnp
from jax import lax
from jax.experimental import pallas as pl
from jax.experimental.pallas import tpu as pltpu
from jax.sharding import PartitionSpec as P

HD = 128
STEPS = 4
EPSILON = 1e-05
ROPE_BASE = 10000.0
MASKED = -1e30


def normed(values, norm_gain):
    widened = values.astype(jnp.float32)
    factor = lax.rsqrt(jnp.mean(widened * widened, axis=-1, keepdims=True) + EPSILON)
    return (widened * factor * norm_gain).astype(jnp.bfloat16)


def angles_of(positions):
    half = HD // 2
    frequency = jnp.exp(
        jnp.arange(half, dtype=jnp.float32) * (-2.0 * math.log(ROPE_BASE) / HD)
    )
    angles = positions.astype(jnp.float32)[..., None] * frequency
    cosine = jnp.cos(angles)
    sine = jnp.sin(angles)
    return (
        jnp.concatenate([cosine, cosine], axis=-1),
        jnp.concatenate([-sine, sine], axis=-1),
    )


def turned(values, cosine, sine):
    half = HD // 2
    swapped = jnp.concatenate([values[..., half:], values[..., :half]], axis=-1)
    return values * cosine + swapped * sine


NX = 4
NY = 4
HELD = ((0, 0), (0, 1), (1, 0), (1, 1), (3, 0), (3, 1), (2, 0), (2, 1))
EARLY = 6
EMPTY = 1e30


def head_pairs(move):
    pairs = []
    for y in range(NY):
        for x in range(NX):
            for c in range(2):
                ty, tx, tc = move(y, x, c)
                pairs.append(((y * NX + x) * 2 + c, (ty * NX + tx) * 2 + tc))
    return pairs


def lane(first, second):
    return head_pairs(
        lambda y, x, c: (y ^ second, x ^ first, c) if c == 0 else (y ^ first, x ^ second, c)
    )


CORE = head_pairs(lambda y, x, c: (y, x, c ^ 1))


def send(values, pairs):
    return lax.ppermute(values, "head", pairs)


def after(values, piece):
    return values + (piece[0, 0].astype(jnp.float32) * 0.0).astype(values.dtype)


def params(mib):
    return pltpu.CompilerParams(vmem_limit_bytes=mib * 1024 * 1024)


def norm_split_kernel(group_ref, rows_ref, gain_ref, kept_ref, given_ref):
    n, half = rows_ref.shape[0], rows_ref.shape[1] // 2
    core = lax.rem(lax.axis_index("head"), 2)
    rows = rows_ref[...].astype(jnp.float32)
    factor = lax.rsqrt(jnp.mean(rows * rows, axis=1, keepdims=True) + EPSILON)
    result = (rows * factor * gain_ref[...]).astype(jnp.bfloat16)
    row = lax.broadcasted_iota(jnp.int32, (n, HD), 0)
    ids = jnp.zeros((n, HD), jnp.int32)
    for j in range(n):
        ids = jnp.where(row == j, group_ref[j], ids)
    ids = ids.astype(jnp.float32).astype(jnp.bfloat16)
    kept_ref[:, half:] = ids
    given_ref[:, half:] = ids

    @pl.when(core == 0)
    def _():
        kept_ref[:, :half] = result[:, :half]
        given_ref[:, :half] = result[:, half:]

    @pl.when(core == 1)
    def _():
        kept_ref[:, :half] = result[:, half:]
        given_ref[:, :half] = result[:, :half]


def norm_split(groups, rows, gain):
    shape = jax.ShapeDtypeStruct((rows.shape[0], rows.shape[1] // 2 + HD), jnp.bfloat16)
    whole = pl.BlockSpec(memory_space=pltpu.VMEM)
    return pl.pallas_call(
        norm_split_kernel,
        out_shape=(shape, shape),
        in_specs=[pl.BlockSpec(memory_space=pltpu.SMEM), whole, whole],
        compiler_params=params(8),
        name="norm_split",
    )(groups, rows, gain.reshape(1, -1))


def other_half_kernel(key_ref, value_ref, dep_ref, out_ref, sems):
    half = out_ref.shape[0]
    core = lax.rem(lax.axis_index("head"), 2)
    rows = pl.ds(pl.multiple_of((1 - core) * half, half), half)
    one = pltpu.make_async_copy(key_ref.at[rows], out_ref.at[:, :HD], sems.at[0])
    two = pltpu.make_async_copy(value_ref.at[rows], out_ref.at[:, HD:], sems.at[1])
    one.start()
    two.start()
    one.wait()
    two.wait()


def other_half(w_key, w_value, dep):
    anywhere = pl.BlockSpec(memory_space=pl.ANY)
    return pl.pallas_call(
        other_half_kernel,
        out_shape=jax.ShapeDtypeStruct((w_key.shape[0] // 2, 2 * HD), jnp.bfloat16),
        in_specs=[anywhere] * 3,
        out_specs=anywhere,
        scratch_shapes=[pltpu.SemaphoreType.DMA((2,))],
        compiler_params=params(4),
        name="other_half",
    )(w_key, w_value, dep)


CHUNKS = 4


def project_kernel(count, *refs):
    pieces = refs[:count]
    key_ref, value_ref, their_ref, own_ref, other_ref, ids_ref, x, w, piece_sems, weight_sems = refs[count:]
    size = pieces[0].shape[0]
    half = w.shape[0]
    depth = half // CHUNKS
    core = lax.rem(lax.axis_index("head"), 2)
    loads = []
    for k in range(CHUNKS):
        mine = pl.ds(pl.multiple_of(core * half + k * depth, depth), depth)
        here = slice(k * depth, (k + 1) * depth)
        loads.append(
            [
                pltpu.make_async_copy(key_ref.at[mine], w.at[here, :HD], weight_sems.at[k, 0]),
                pltpu.make_async_copy(
                    value_ref.at[mine], w.at[here, HD : 2 * HD], weight_sems.at[k, 1]
                ),
                pltpu.make_async_copy(
                    their_ref.at[here], w.at[here, 2 * HD :], weight_sems.at[k, 2]
                ),
            ]
        )
    rows = [
        pltpu.make_async_copy(p, x.at[i * size : (i + 1) * size], piece_sems.at[i])
        for i, p in enumerate(pieces)
    ]
    for load in loads[0]:
        load.start()
    for row in rows:
        row.start()
    for k in range(1, CHUNKS):
        for load in loads[k]:
            load.start()
    for row in rows:
        row.wait()
    ids_ref[...] = x[:, half:]
    for k in range(CHUNKS):
        for load in loads[k]:
            load.wait()
        here = slice(k * depth, (k + 1) * depth)
        term = jnp.dot(x[:, here], w[here, :], preferred_element_type=jnp.float32)
        if k == 0:
            own_ref[...] = term[:, : 2 * HD]
            other_ref[...] = term[:, 2 * HD :]
        else:
            own_ref[...] += term[:, : 2 * HD]
            other_ref[...] += term[:, 2 * HD :]


def project(pieces, w_key, w_value, their_half):
    count = len(pieces)
    size, wide = pieces[0].shape
    half = wide - HD
    rows = count * size
    anywhere = pl.BlockSpec(memory_space=pl.ANY)
    shape = jax.ShapeDtypeStruct((rows, 2 * HD), jnp.float32)
    return pl.pallas_call(
        lambda *refs: project_kernel(count, *refs),
        out_shape=(shape, shape, jax.ShapeDtypeStruct((rows, HD), jnp.bfloat16)),
        in_specs=[anywhere] * (count + 3),
        scratch_shapes=[
            pltpu.VMEM((rows, wide), jnp.bfloat16),
            pltpu.VMEM((half, 4 * HD), jnp.bfloat16),
            pltpu.SemaphoreType.DMA((count,)),
            pltpu.SemaphoreType.DMA((CHUNKS, 3)),
        ],
        compiler_params=params(16),
        name="project",
    )(*pieces, w_key, w_value, their_half)


def origin(shape, dim, head):
    at = lax.broadcasted_iota(jnp.int32, shape, dim)
    block, row = at >> 4, at & 15
    turn = block >> 3
    d_second, d_first, d_core = turn ^ (turn >> 1), block & 3, (block >> 2) & 1
    core = head & 1
    dy = jnp.where(core == 0, d_second, d_first)
    dx = jnp.where(core == 0, d_first, d_second)
    y, x, c = (head >> 3) ^ dy, ((head >> 1) & 3) ^ dx, core ^ d_core
    return (((y * NX + x) * 2 + c) << 4) + row


def finish_kernel(groups, own_a, own_b, their_a, their_b, ids_a, ids_b, out_ref, packed):
    total = packed.shape[0]
    n = total // (len(HELD) * NX)
    early = EARLY * NX
    head = lax.axis_index("head")
    cap = out_ref.shape[0] // groups

    def block(first, second, i):
        return first[i * n : (i + 1) * n] if i < early else second[(i - early) * n : (i - early + 1) * n]

    for at, (d_second, d_core) in enumerate(HELD):
        for d_first in range(NX):
            i = at * NX + d_first
            j = HELD.index((d_first, 1 - d_core)) * NX + d_second
            both = block(own_a, own_b, i) + block(their_a, their_b, j)
            packed[i * n : (i + 1) * n, :] = both.astype(jnp.bfloat16)
    ids = jnp.concatenate([ids_a[...], ids_b[...]], axis=0).astype(jnp.float32)
    lanes = lax.broadcasted_iota(jnp.int32, (total, HD), 1).astype(jnp.float32)
    match = jnp.where(ids == lanes, 1.0, 0.0)
    earlier = origin((total, total), 1, head) < origin((total, total), 0, head)
    ranks = jnp.dot(
        jnp.where(earlier, 1.0, 0.0).astype(jnp.bfloat16),
        match.astype(jnp.bfloat16),
        preferred_element_type=jnp.float32,
    )
    order = jnp.sum(ranks * match, axis=1, keepdims=True)
    slot = ids[:, :1] * cap + order
    slots = lax.broadcasted_iota(jnp.int32, (total, groups * cap), 1).astype(jnp.float32)
    pick = jnp.where(slots == slot, 1.0, 0.0).astype(jnp.bfloat16)
    routed = lax.dot_general(
        pick, packed[...], (((0,), (0,)), ((), ())), preferred_element_type=jnp.float32
    )
    counts = jnp.sum(match, axis=0, keepdims=True)
    step = lax.broadcasted_iota(jnp.int32, (cap, HD), 0).astype(jnp.float32)
    for g in range(groups):
        rows = slice(g * cap, (g + 1) * cap)
        filled = step < counts[:, g : g + 1]
        out_ref[rows, :HD] = jnp.where(filled, routed[rows, :HD], EMPTY).astype(jnp.bfloat16)
        out_ref[rows, HD:] = routed[rows, HD:].astype(jnp.bfloat16)


def finish(groups, slots, own_a, own_b, their_a, their_b, ids_a, ids_b):
    return pl.pallas_call(
        lambda *refs: finish_kernel(groups, *refs),
        out_shape=jax.ShapeDtypeStruct((slots, 2 * HD), jnp.bfloat16),
        scratch_shapes=[pltpu.VMEM((own_a.shape[0] + own_b.shape[0], 2 * HD), jnp.bfloat16)],
        compiler_params=params(24),
        name="finish",
    )(own_a, own_b, their_a, their_b, ids_a, ids_b)


def settle_kernel(groups, cache_ref, edge_row, edge_col, high_ref, low_ref, key_ref, bias_ref, hot):
    slots = cache_ref.shape[0]
    cap = slots // groups
    starts, ends = edge_row[0:1, :], edge_row[1:2, :]
    lanes = lax.broadcasted_iota(jnp.int32, (cap, HD), 1).astype(jnp.float32)
    step = lax.broadcasted_iota(jnp.int32, (cap, 1), 0).astype(jnp.float32)
    across = lax.broadcasted_iota(jnp.int32, (1, slots), 1).astype(jnp.float32)
    cells = across
    open_slots = across < 0.0
    base = jnp.zeros((1, 1), jnp.float32)
    for g in range(groups):
        rows = slice(g * cap, (g + 1) * cap)
        full = cache_ref[rows, :HD].astype(jnp.float32) < EMPTY / 2
        count = jnp.sum(jnp.where(full, 1.0, 0.0), axis=0, keepdims=True)[:, :1]
        cell = base + step
        inside = (cell >= starts) & (cell < ends)
        place = cell - jnp.sum(jnp.where(inside, starts, 0.0), axis=1, keepdims=True)
        hot[rows, :] = jnp.where(lanes == place, 1.0, 0.0).astype(jnp.bfloat16)
        here = (across >= g * cap) & (across < (g + 1) * cap)
        cells = jnp.where(here, across - g * cap + base, cells)
        open_slots = open_slots | (here & (across - g * cap < count))
        base = base + count
    low_edge, high_edge = edge_col[:, 0:1], edge_col[:, HD : HD + 1]
    mine = (cells >= low_edge) & (cells < high_edge) & open_slots
    bias_ref[...] = jnp.where(mine, 0.0, MASKED)
    trig = jnp.dot(hot[...], high_ref[...], preferred_element_type=jnp.float32)
    trig = trig + jnp.dot(hot[...], low_ref[...], preferred_element_type=jnp.float32)
    keys = cache_ref[:, :HD].astype(jnp.float32)
    keys = jnp.where(keys < EMPTY / 2, keys, 0.0)
    key_ref[...] = (keys * trig[:, :HD] + pltpu.roll(keys, HD // 2, 1) * trig[:, HD:]).astype(
        jnp.bfloat16
    )


def settle(groups, cache, edge_row, edge_col, high, low):
    slots = cache.shape[0]
    return pl.pallas_call(
        lambda *refs: settle_kernel(groups, *refs),
        out_shape=(
            jax.ShapeDtypeStruct((slots, HD), jnp.bfloat16),
            jax.ShapeDtypeStruct((edge_col.shape[0], slots), jnp.float32),
        ),
        scratch_shapes=[pltpu.VMEM((slots, HD), jnp.bfloat16)],
        compiler_params=params(16),
        name="settle",
    )(cache, edge_row, edge_col, high, low)


def rotated(values, turn):
    return values * turn[:, :HD] + pltpu.roll(values, HD // 2, 1) * turn[:, HD:]


def attend_kernel(step, *refs):
    f32, bf16 = jnp.float32, jnp.bfloat16
    turn_ref, key_ref, cache_ref, bias_ref, out_weight, *rest = refs
    turn = turn_ref[step]
    olds = [(rest[2 * i], rest[2 * i + 1]) for i in range(step)]
    rest = rest[2 * step :]
    if step:
        row_ref, inverse_ref, wq_ref, wk_ref, wv_ref, term_ref, new_key_ref, new_value_ref = rest
        blocks, n, share = row_ref.shape
        squares = jnp.zeros((n, share), f32)
        for i in range(blocks):
            plain = row_ref[i].astype(f32) * inverse_ref[:, i * share : (i + 1) * share]
            squares = squares + plain * plain
        mean = jnp.sum(squares, axis=1, keepdims=True) * (1.0 / (blocks * share))
        factor = lax.rsqrt(mean + EPSILON)
        rows = jnp.concatenate([row_ref[i] for i in range(blocks)], axis=1)
        query = jnp.dot(rows, wq_ref[...], preferred_element_type=f32) * factor
        key = jnp.dot(rows, wk_ref[...], preferred_element_type=f32) * factor
        value = jnp.dot(rows, wv_ref[...], preferred_element_type=f32) * factor
    else:
        query_ref, first_key, first_value, _, _, _, term_ref, new_key_ref, new_value_ref = rest
        query, key, value = query_ref[...], first_key[...], first_value[...]
    query = rotated(query, turn).astype(bf16)
    key = rotated(key, turn).astype(bf16)
    value = value.astype(bf16)
    new_key_ref[...] = key
    new_value_ref[...] = value
    scale = HD ** (-0.5)
    scores = lax.dot_general(
        query, key_ref[...], (((1,), (1,)), ((), ())), preferred_element_type=f32
    )
    scores = scores * scale + bias_ref[...]
    wide = query.astype(f32)
    pairs = [(k[...], v[...]) for k, v in olds] + [(key, value)]
    fresh = [jnp.sum(wide * k.astype(f32), axis=1, keepdims=True) * scale for k, _ in pairs]
    peak = jnp.max(scores, axis=1, keepdims=True)
    for f in fresh:
        peak = jnp.maximum(peak, f)
    cache_exp = jnp.exp(scores - peak)
    fresh_exp = [jnp.exp(f - peak) for f in fresh]
    total = jnp.sum(cache_exp, axis=1, keepdims=True)
    for f in fresh_exp:
        total = total + f
    weights = (cache_exp / total).astype(bf16)
    attended = jnp.dot(weights, cache_ref[:, HD:], preferred_element_type=f32)
    for f, (_, v) in zip(fresh_exp, pairs):
        attended = attended + (f / total).astype(bf16).astype(f32) * v.astype(f32)
    attended = attended.astype(bf16)
    blocks, _, share = term_ref.shape
    wide_share = 4 * share
    for j in range(blocks // 4):
        term = jnp.dot(
            attended, out_weight[:, j * wide_share : (j + 1) * wide_share], preferred_element_type=f32
        ).astype(bf16)
        for i in range(4):
            term_ref[4 * j + i] = term[:, i * share : (i + 1) * share]


def attend(step, blocks, turns, keys, cache, bias, w_out, olds, extra):
    n = bias.shape[0]
    share = w_out.shape[1] // blocks
    flat = [x for pair in olds for x in pair]
    small = jax.ShapeDtypeStruct((n, HD), jnp.bfloat16)
    return pl.pallas_call(
        lambda *refs: attend_kernel(step, *refs),
        out_shape=(jax.ShapeDtypeStruct((blocks, n, share), jnp.bfloat16), small, small),
        compiler_params=params(20),
        name="attend",
    )(turns, keys, cache, bias, w_out, *flat, *extra)


def spread_kernel(last, part_ref, current_ref, gain_ref, next_ref, *out):
    total = current_ref[...]
    for i in range(part_ref.shape[0]):
        total = total + part_ref[i].astype(jnp.float32)
    next_ref[...] = total
    if not last:
        piece = (total * gain_ref[...]).astype(jnp.bfloat16)
        for i in range(part_ref.shape[0]):
            out[0][i] = piece


def spread(last, parts, current, gain):
    shapes = [jax.ShapeDtypeStruct(current.shape, jnp.float32)]
    if not last:
        shapes.append(jax.ShapeDtypeStruct(parts.shape, jnp.bfloat16))
    return pl.pallas_call(
        lambda *refs: spread_kernel(last, *refs),
        out_shape=tuple(shapes),
        compiler_params=params(4),
        name="spread",
    )(parts, current, gain)


def per_device(
    prefill_rows, row_group, lengths, decode_state, norm_gain, w_query, w_key, w_value, w_out
):
    groups = lax.axis_size("grp")
    heads = lax.axis_size("head")
    rows_local, width = prefill_rows.shape
    plane_rows = rows_local * heads
    cap = (rows_local // groups + rows_local // groups // 2) * heads
    requests = lengths.shape[1]
    my_group = lax.axis_index("grp")
    my_head = lax.axis_index("head")
    share = width // heads
    f32, bf16 = jnp.float32, jnp.bfloat16

    core = my_head % 2
    with jax.named_scope("rows"):
        n = rows_local
        kept, given = norm_split(row_group, prefill_rows, norm_gain)
        got = send(given, CORE)
        start = jnp.concatenate([kept, got])
        f2 = send(start, lane(2, 0))
        f1 = send(start, lane(1, 0))
        f3 = send(start, lane(3, 0))
        l0 = jnp.concatenate([kept, f1[:n], f2[:n], f3[:n]])
        l1 = jnp.concatenate([got, f1[n:], f2[n:], f3[n:]])
        s11 = send(l1, lane(0, 1))
        s30 = send(l0, lane(0, 3))
        s10 = send(l0, lane(0, 1))
        s31 = send(l1, lane(0, 3))
        s20 = send(s30, lane(0, 1))
        s21 = send(s11, lane(0, 3))
    with jax.named_scope("weights"):
        their_half = send(other_half(w_key, w_value, f1), CORE)

    with jax.named_scope("places"):
        group_ids = jnp.arange(groups, dtype=jnp.int32)
        late_lengths = after(lengths, f1)
        my_lengths = jnp.sum(
            jnp.where((group_ids == my_group)[:, None], late_lengths, 0), axis=0
        )
        request = jnp.arange(requests, dtype=jnp.int32)
        my_ends = jnp.sum(jnp.where(request[None, :] <= request[:, None], my_lengths[None, :], 0), axis=1)
        my_starts = my_ends - my_lengths
        edges = jnp.stack([my_starts, my_ends]).astype(f32)
        edge_row = jnp.pad(edges, ((0, 0), (0, HD - requests)), constant_values=1e9)
        edge_col = jnp.repeat(edges, HD, axis=0).T.reshape(requests, 2 * HD)
        spots = jnp.arange(HD, dtype=jnp.int32) + 0 * my_lengths[0]
        table = jnp.concatenate(angles_of(spots), axis=1)
        table_high = table.astype(bf16)
        table_low = (table - table_high.astype(f32)).astype(bf16)

    with jax.named_scope("project"):
        own_a, other_a, ids_a = project([l0, l1, s10, s11, s30, s31], w_key, w_value, their_half)
        own_b, other_b, ids_b = project([s20, s21], w_key, w_value, their_half)
        outgoing = finish(
            groups, groups * cap, own_a, own_b, send(other_a, CORE), send(other_b, CORE), ids_a, ids_b
        )
        cache = lax.all_to_all(
            outgoing.reshape(groups, cap, 2 * HD), "grp", split_axis=0, concat_axis=0, tiled=True
        ).reshape(groups * cap, 2 * HD)
        cache_keys, bias = settle(groups, cache, edge_row, edge_col, table_high, table_low)

    with jax.named_scope("first"):
        late_state = after(decode_state, f1)
        current = lax.dynamic_slice_in_dim(late_state, my_head * share, share, 1)
        late_gain = after(norm_gain, f1)
        my_gain = lax.dynamic_slice_in_dim(late_gain, my_head * share, share, 0)[None, :]
        inverse = (1.0 / late_gain)[None, :]
        decode_rows = normed(late_state, norm_gain)
        extra = [
            jnp.dot(decode_rows, w, preferred_element_type=f32) for w in (w_query, w_key, w_value)
        ]
        at_step = my_lengths[None, :] + jnp.arange(STEPS, dtype=jnp.int32)[:, None]
        turns = jnp.concatenate(angles_of(at_step), axis=-1)
        extra += [current, my_gain, inverse]
    olds = []
    for step in range(STEPS):
        term, new_key, new_value = attend(
            step, heads, turns, cache_keys, cache, bias, w_out, olds, extra
        )
        olds.append((new_key, new_value))
        parts = lax.all_to_all(term, "head", split_axis=0, concat_axis=0, tiled=True)
        last = step + 1 == STEPS
        current, *spreading = spread(last, parts, current, my_gain)
        if not last:
            rows = lax.all_to_all(spreading[0], "head", split_axis=0, concat_axis=0, tiled=True)
            extra = [rows, inverse, w_query, w_key, w_value]
    return current


def solution(mesh):
    return jax.shard_map(
        per_device,
        mesh=mesh,
        in_specs=(
            P(("grp", "head"), None),
            P(("grp", "head")),
            P(),
            P("grp", None),
            P(),
            P(None, "head"),
            P(None, "head"),
            P(None, "head"),
            P("head", None),
        ),
        out_specs=P("grp", "head"),
        check_vma=False,
    )
```

```python
import math

import jax
import jax.numpy as jnp
from jax import lax
from jax.experimental import pallas as pl
from jax.experimental.pallas import tpu as pltpu
from jax.sharding import PartitionSpec as P

HD = 128
STEPS = 4
EPSILON = 1e-05
ROPE_BASE = 10000.0
MASKED = -1e30


def normed(values, norm_gain):
    widened = values.astype(jnp.float32)
    factor = lax.rsqrt(jnp.mean(widened * widened, axis=-1, keepdims=True) + EPSILON)
    return (widened * factor * norm_gain).astype(jnp.bfloat16)


def angles_of(positions):
    half = HD // 2
    frequency = jnp.exp(
        jnp.arange(half, dtype=jnp.float32) * (-2.0 * math.log(ROPE_BASE) / HD)
    )
    angles = positions.astype(jnp.float32)[..., None] * frequency
    cosine = jnp.cos(angles)
    sine = jnp.sin(angles)
    return (
        jnp.concatenate([cosine, cosine], axis=-1),
        jnp.concatenate([-sine, sine], axis=-1),
    )


def turned(values, cosine, sine):
    half = HD // 2
    swapped = jnp.concatenate([values[..., half:], values[..., :half]], axis=-1)
    return values * cosine + swapped * sine


NX = 4
NY = 4
HELD = ((0, 0), (0, 1), (1, 0), (1, 1), (3, 0), (3, 1), (2, 0), (2, 1))
EARLY = 6
EMPTY = 1e30


def head_pairs(move):
    pairs = []
    for y in range(NY):
        for x in range(NX):
            for c in range(2):
                ty, tx, tc = move(y, x, c)
                pairs.append(((y * NX + x) * 2 + c, (ty * NX + tx) * 2 + tc))
    return pairs


def lane(first, second):
    return head_pairs(
        lambda y, x, c: (y ^ second, x ^ first, c) if c == 0 else (y ^ first, x ^ second, c)
    )


CORE = head_pairs(lambda y, x, c: (y, x, c ^ 1))


def send(values, pairs):
    return lax.ppermute(values, "head", pairs)


def after(values, piece):
    return values + (piece[0, 0].astype(jnp.float32) * 0.0).astype(values.dtype)


def params(mib):
    return pltpu.CompilerParams(vmem_limit_bytes=mib * 1024 * 1024)


def norm_split_kernel(group_ref, rows_ref, gain_ref, kept_ref, given_ref):
    n, half = rows_ref.shape[0], rows_ref.shape[1] // 2
    core = lax.rem(lax.axis_index("head"), 2)
    rows = rows_ref[...].astype(jnp.float32)
    factor = lax.rsqrt(jnp.mean(rows * rows, axis=1, keepdims=True) + EPSILON)
    result = (rows * factor * gain_ref[...]).astype(jnp.bfloat16)
    row = lax.broadcasted_iota(jnp.int32, (n, HD), 0)
    ids = jnp.zeros((n, HD), jnp.int32)
    for j in range(n):
        ids = jnp.where(row == j, group_ref[j], ids)
    ids = ids.astype(jnp.float32).astype(jnp.bfloat16)
    kept_ref[:, half:] = ids
    given_ref[:, half:] = ids

    @pl.when(core == 0)
    def _():
        kept_ref[:, :half] = result[:, :half]
        given_ref[:, :half] = result[:, half:]

    @pl.when(core == 1)
    def _():
        kept_ref[:, :half] = result[:, half:]
        given_ref[:, :half] = result[:, :half]


def norm_split(groups, rows, gain):
    shape = jax.ShapeDtypeStruct((rows.shape[0], rows.shape[1] // 2 + HD), jnp.bfloat16)
    whole = pl.BlockSpec(memory_space=pltpu.VMEM)
    return pl.pallas_call(
        norm_split_kernel,
        out_shape=(shape, shape),
        in_specs=[pl.BlockSpec(memory_space=pltpu.SMEM), whole, whole],
        compiler_params=params(56),
        name="norm_split",
    )(groups, rows, gain.reshape(1, -1))


def other_half_kernel(key_ref, value_ref, dep_ref, out_ref, sems):
    half = out_ref.shape[0]
    core = lax.rem(lax.axis_index("head"), 2)
    rows = pl.ds(pl.multiple_of((1 - core) * half, half), half)
    one = pltpu.make_async_copy(key_ref.at[rows], out_ref.at[:, :HD], sems.at[0])
    two = pltpu.make_async_copy(value_ref.at[rows], out_ref.at[:, HD:], sems.at[1])
    one.start()
    two.start()
    one.wait()
    two.wait()


def other_half(w_key, w_value, dep):
    anywhere = pl.BlockSpec(memory_space=pl.ANY)
    return pl.pallas_call(
        other_half_kernel,
        out_shape=jax.ShapeDtypeStruct((w_key.shape[0] // 2, 2 * HD), jnp.bfloat16),
        in_specs=[anywhere] * 3,
        out_specs=anywhere,
        scratch_shapes=[pltpu.SemaphoreType.DMA((2,))],
        compiler_params=params(4),
        name="other_half",
    )(w_key, w_value, dep)


CHUNKS = 4


def project_kernel(count, *refs):
    pieces = refs[:count]
    key_ref, value_ref, their_ref, own_ref, other_ref, ids_ref, w, x, piece_sems, weight_sems = refs[
        count:
    ]
    size = pieces[0].shape[0]
    half = w.shape[0]
    depth = half // CHUNKS
    core = lax.rem(lax.axis_index("head"), 2)
    loads = []
    for k in range(CHUNKS):
        mine = pl.ds(pl.multiple_of(core * half + k * depth, depth), depth)
        here = slice(k * depth, (k + 1) * depth)
        loads.append(
            [
                pltpu.make_async_copy(key_ref.at[mine], w.at[here, :HD], weight_sems.at[k, 0]),
                pltpu.make_async_copy(
                    value_ref.at[mine], w.at[here, HD : 2 * HD], weight_sems.at[k, 1]
                ),
                pltpu.make_async_copy(
                    their_ref.at[here], w.at[here, 2 * HD :], weight_sems.at[k, 2]
                ),
            ]
        )
    rows = [
        pltpu.make_async_copy(p, x.at[i * size : (i + 1) * size], piece_sems.at[i])
        for i, p in enumerate(pieces)
    ]
    for load in loads[0]:
        load.start()
    for row in rows:
        row.start()
    for k in range(1, CHUNKS):
        for load in loads[k]:
            load.start()
    for row in rows:
        row.wait()
    ids_ref[...] = x[:, half:]
    for k in range(CHUNKS):
        for load in loads[k]:
            load.wait()
        here = slice(k * depth, (k + 1) * depth)
        term = jnp.dot(x[:, here], w[here, :], preferred_element_type=jnp.float32)
        if k == 0:
            own_ref[...] = term[:, : 2 * HD]
            other_ref[...] = term[:, 2 * HD :]
        else:
            own_ref[...] += term[:, : 2 * HD]
            other_ref[...] += term[:, 2 * HD :]


def project(pieces, w_key, w_value, their_half):
    count = len(pieces)
    size, wide = pieces[0].shape
    half = wide - HD
    rows = count * size
    anywhere = pl.BlockSpec(memory_space=pl.ANY)
    shape = jax.ShapeDtypeStruct((rows, 2 * HD), jnp.float32)
    return pl.pallas_call(
        lambda *refs: project_kernel(count, *refs),
        out_shape=(
            shape,
            shape,
            jax.ShapeDtypeStruct((rows, HD), jnp.bfloat16),
            jax.ShapeDtypeStruct((half, 4 * HD), jnp.bfloat16),
        ),
        in_specs=[anywhere] * (count + 3),
        scratch_shapes=[
            pltpu.VMEM((rows, wide), jnp.bfloat16),
            pltpu.SemaphoreType.DMA((count,)),
            pltpu.SemaphoreType.DMA((CHUNKS, 3)),
        ],
        compiler_params=params(14),
        name="project",
    )(*pieces, w_key, w_value, their_half)


def project_last_kernel(first, second, w, own_ref, other_ref, ids_ref):
    n, half = first.shape[0], w.shape[0]
    x = jnp.concatenate([first[...], second[...]], axis=0)
    ids_ref[...] = x[:, half:]
    term = jnp.dot(x[:, :half], w[...], preferred_element_type=jnp.float32)
    own_ref[...] = term[:, : 2 * HD]
    other_ref[...] = term[:, 2 * HD :]


def project_last(first, second, weights):
    rows = 2 * first.shape[0]
    shape = jax.ShapeDtypeStruct((rows, 2 * HD), jnp.float32)
    return pl.pallas_call(
        project_last_kernel,
        out_shape=(shape, shape, jax.ShapeDtypeStruct((rows, HD), jnp.bfloat16)),
        compiler_params=params(10),
        name="project_last",
    )(first, second, weights)


def origin(shape, dim, head):
    at = lax.broadcasted_iota(jnp.int32, shape, dim)
    block, row = at >> 4, at & 15
    turn = block >> 3
    d_second, d_first, d_core = turn ^ (turn >> 1), block & 3, (block >> 2) & 1
    core = head & 1
    dy = jnp.where(core == 0, d_second, d_first)
    dx = jnp.where(core == 0, d_first, d_second)
    y, x, c = (head >> 3) ^ dy, ((head >> 1) & 3) ^ dx, core ^ d_core
    return (((y * NX + x) * 2 + c) << 4) + row


def finish_kernel(groups, cap, own_a, own_b, their_a, their_b, ids_a, ids_b, *refs):
    outs, packed = refs[:groups], refs[groups]
    total = packed.shape[0]
    n = total // (len(HELD) * NX)
    early = EARLY * NX
    head = lax.axis_index("head")
    group = lax.axis_index("grp").astype(jnp.float32)

    def block(first, second, i):
        return first[i * n : (i + 1) * n] if i < early else second[(i - early) * n : (i - early + 1) * n]

    for at, (d_second, d_core) in enumerate(HELD):
        for d_first in range(NX):
            i = at * NX + d_first
            j = HELD.index((d_first, 1 - d_core)) * NX + d_second
            both = block(own_a, own_b, i) + block(their_a, their_b, j)
            packed[i * n : (i + 1) * n, :] = both.astype(jnp.bfloat16)
    hop = jnp.concatenate([ids_a[...], ids_b[...]], axis=0).astype(jnp.float32) - group
    hop = jnp.where(hop < 0.0, hop + groups, hop)
    lanes = lax.broadcasted_iota(jnp.int32, (1, HD), 1).astype(jnp.float32)
    match = jnp.where(hop == lanes, 1.0, 0.0)
    earlier = origin((1, total), 1, head) < origin((total, 1), 0, head)
    ranks = jnp.dot(
        jnp.where(earlier, 1.0, 0.0).astype(jnp.bfloat16),
        match.astype(jnp.bfloat16),
        preferred_element_type=jnp.float32,
    )
    order = jnp.sum(ranks * match, axis=1, keepdims=True)
    slot = hop[:, :1] * cap + order
    slots = lax.broadcasted_iota(jnp.int32, (1, groups * cap), 1).astype(jnp.float32)
    pick = jnp.where(slots == slot, 1.0, 0.0).astype(jnp.bfloat16)
    routed = lax.dot_general(
        pick, packed[...], (((0,), (0,)), ((), ())), preferred_element_type=jnp.float32
    )
    counts = jnp.sum(match, axis=0, keepdims=True)
    step = lax.broadcasted_iota(jnp.int32, (cap, 1), 0).astype(jnp.float32)
    for g in range(groups):
        rows = slice(g * cap, (g + 1) * cap)
        filled = step < counts[:, g : g + 1]
        outs[g][:, :HD] = jnp.where(filled, routed[rows, :HD], EMPTY).astype(jnp.bfloat16)
        outs[g][:, HD:] = routed[rows, HD:].astype(jnp.bfloat16)


def finish(groups, cap, own_a, own_b, their_a, their_b, ids_a, ids_b):
    shape = jax.ShapeDtypeStruct((cap, 2 * HD), jnp.bfloat16)
    return pl.pallas_call(
        lambda *refs: finish_kernel(groups, cap, *refs),
        out_shape=(shape,) * groups,
        scratch_shapes=[pltpu.VMEM((own_a.shape[0] + own_b.shape[0], 2 * HD), jnp.bfloat16)],
        compiler_params=params(12),
        name="finish",
    )(own_a, own_b, their_a, their_b, ids_a, ids_b)


def settle_kernel(groups, edge_row, edge_col, high_ref, low_ref, *refs):
    parts = refs[:groups]
    key_ref, value_ref, bias_ref, hot = refs[groups:]
    cap = parts[0].shape[0]
    slots = groups * cap
    me = lax.axis_index("grp")
    sources = [lax.rem(me + groups - g, groups) for g in range(groups)]
    starts, ends = edge_row[0:1, :], edge_row[1:2, :]
    lanes = lax.broadcasted_iota(jnp.int32, (1, HD), 1).astype(jnp.float32)
    step = lax.broadcasted_iota(jnp.int32, (cap, 1), 0).astype(jnp.float32)
    across = lax.broadcasted_iota(jnp.int32, (1, slots), 1).astype(jnp.float32)
    counts = []
    for part in parts:
        full = part[:, :HD].astype(jnp.float32) < EMPTY / 2
        counts.append(jnp.sum(jnp.where(full, 1.0, 0.0), axis=0, keepdims=True)[:, :1])
    cells = across
    open_slots = across < 0.0
    for g in range(groups):
        base = jnp.zeros((1, 1), jnp.float32)
        for other in range(groups):
            if other != g:
                before = jnp.where(sources[other] < sources[g], 1.0, 0.0)
                base = base + counts[other] * before
        rows = slice(g * cap, (g + 1) * cap)
        cell = base + step
        inside = (cell >= starts) & (cell < ends)
        place = cell - jnp.sum(jnp.where(inside, starts, 0.0), axis=1, keepdims=True)
        hot[rows, :] = jnp.where(lanes == place, 1.0, 0.0).astype(jnp.bfloat16)
        here = (across >= g * cap) & (across < (g + 1) * cap)
        cells = jnp.where(here, across - g * cap + base, cells)
        open_slots = open_slots | (here & (across - g * cap < counts[g]))
        value_ref[rows, :] = parts[g][:, HD:]
    low_edge, high_edge = edge_col[:, 0:1], edge_col[:, HD : HD + 1]
    mine = (cells >= low_edge) & (cells < high_edge) & open_slots
    bias_ref[...] = jnp.where(mine, 0.0, MASKED)
    trig = jnp.dot(hot[...], high_ref[...], preferred_element_type=jnp.float32)
    trig = trig + jnp.dot(hot[...], low_ref[...], preferred_element_type=jnp.float32)
    for g in range(groups):
        rows = slice(g * cap, (g + 1) * cap)
        keys = parts[g][:, :HD].astype(jnp.float32)
        keys = jnp.where(keys < EMPTY / 2, keys, 0.0)
        turned_keys = keys * trig[rows, :HD] + pltpu.roll(keys, HD // 2, 1) * trig[rows, HD:]
        key_ref[rows, :] = turned_keys.astype(jnp.bfloat16)


def settle(edge_row, edge_col, high, low, parts):
    slots = len(parts) * parts[0].shape[0]
    wide = jax.ShapeDtypeStruct((slots, HD), jnp.bfloat16)
    return pl.pallas_call(
        lambda *refs: settle_kernel(len(parts), *refs),
        out_shape=(wide, wide, jax.ShapeDtypeStruct((edge_col.shape[0], slots), jnp.float32)),
        scratch_shapes=[pltpu.VMEM((slots, HD), jnp.bfloat16)],
        compiler_params=params(8),
        name="settle",
    )(edge_row, edge_col, high, low, *parts)


def hold_kernel(count, *refs):
    sems = refs[-1]
    copies = [
        pltpu.make_async_copy(refs[i], refs[count + 1 + i], sems.at[i]) for i in range(count)
    ]
    for copy in copies:
        copy.start()
    for copy in copies:
        copy.wait()


def hold(arrays, dep):
    count = len(arrays)
    return pl.pallas_call(
        lambda *refs: hold_kernel(count, *refs),
        out_shape=tuple(jax.ShapeDtypeStruct(a.shape, a.dtype) for a in arrays),
        in_specs=[pl.BlockSpec(memory_space=pl.ANY)] * (count + 1),
        out_specs=(pl.BlockSpec(memory_space=pltpu.VMEM),) * count,
        scratch_shapes=[pltpu.SemaphoreType.DMA((count,))],
        compiler_params=params(10),
        name="hold",
    )(*arrays, dep)


def rotated(values, turn):
    return values * turn[:, :HD] + pltpu.roll(values, HD // 2, 1) * turn[:, HD:]


def attend_kernel(step, *refs):
    f32, bf16 = jnp.float32, jnp.bfloat16
    turn_ref, key_ref, cache_ref, bias_ref, out_weight, *rest = refs
    turn = turn_ref[step]
    olds = [(rest[2 * i], rest[2 * i + 1]) for i in range(step)]
    rest = rest[2 * step :]
    if step:
        row_ref, inverse_ref, wq_ref, wk_ref, wv_ref, term_ref, new_key_ref, new_value_ref = rest
        blocks, n, share = row_ref.shape
        squares = jnp.zeros((n, share), f32)
        for i in range(blocks):
            plain = row_ref[i].astype(f32) * inverse_ref[:, i * share : (i + 1) * share]
            squares = squares + plain * plain
        mean = jnp.sum(squares, axis=1, keepdims=True) * (1.0 / (blocks * share))
        factor = lax.rsqrt(mean + EPSILON)
        rows = jnp.concatenate([row_ref[i] for i in range(blocks)], axis=1)
        query = jnp.dot(rows, wq_ref[...], preferred_element_type=f32) * factor
        key = jnp.dot(rows, wk_ref[...], preferred_element_type=f32) * factor
        value = jnp.dot(rows, wv_ref[...], preferred_element_type=f32) * factor
    else:
        query_ref, first_key, first_value, _, _, _, term_ref, new_key_ref, new_value_ref = rest
        query, key, value = query_ref[...], first_key[...], first_value[...]
    query = rotated(query, turn).astype(bf16)
    key = rotated(key, turn).astype(bf16)
    value = value.astype(bf16)
    new_key_ref[...] = key
    new_value_ref[...] = value
    scale = HD ** (-0.5)
    scores = lax.dot_general(
        query, key_ref[...], (((1,), (1,)), ((), ())), preferred_element_type=f32
    )
    scores = scores * scale + bias_ref[...]
    wide = query.astype(f32)
    pairs = [(k[...], v[...]) for k, v in olds] + [(key, value)]
    fresh = [jnp.sum(wide * k.astype(f32), axis=1, keepdims=True) * scale for k, _ in pairs]
    peak = jnp.max(scores, axis=1, keepdims=True)
    for f in fresh:
        peak = jnp.maximum(peak, f)
    cache_exp = jnp.exp(scores - peak)
    fresh_exp = [jnp.exp(f - peak) for f in fresh]
    total = jnp.sum(cache_exp, axis=1, keepdims=True)
    for f in fresh_exp:
        total = total + f
    weights = (cache_exp / total).astype(bf16)
    attended = jnp.dot(weights, cache_ref[...], preferred_element_type=f32)
    for f, (_, v) in zip(fresh_exp, pairs):
        attended = attended + (f / total).astype(bf16).astype(f32) * v.astype(f32)
    attended = attended.astype(bf16)
    blocks, _, share = term_ref.shape
    wide_share = 4 * share
    for j in range(blocks // 4):
        term = jnp.dot(
            attended, out_weight[:, j * wide_share : (j + 1) * wide_share], preferred_element_type=f32
        ).astype(bf16)
        for i in range(4):
            term_ref[4 * j + i] = term[:, i * share : (i + 1) * share]


def attend(step, blocks, turns, keys, cache, bias, w_out, olds, extra):
    n = bias.shape[0]
    share = w_out.shape[1] // blocks
    flat = [x for pair in olds for x in pair]
    small = jax.ShapeDtypeStruct((n, HD), jnp.bfloat16)
    return pl.pallas_call(
        lambda *refs: attend_kernel(step, *refs),
        out_shape=(jax.ShapeDtypeStruct((blocks, n, share), jnp.bfloat16), small, small),
        compiler_params=params(10),
        name="attend",
    )(turns, keys, cache, bias, w_out, *flat, *extra)


def spread_kernel(last, part_ref, current_ref, gain_ref, *refs):
    next_ref, *out = refs[-1:] if last else refs[-2:]
    total = current_ref[...]
    for i in range(part_ref.shape[0]):
        total = total + part_ref[i].astype(jnp.float32)
    next_ref[...] = total
    if not last:
        piece = (total * gain_ref[...]).astype(jnp.bfloat16)
        for i in range(part_ref.shape[0]):
            out[0][i] = piece


def spread(last, parts, current, gain, held):
    shapes = [jax.ShapeDtypeStruct(current.shape, jnp.float32)]
    if not last:
        shapes.append(jax.ShapeDtypeStruct(parts.shape, jnp.bfloat16))
    return pl.pallas_call(
        lambda *refs: spread_kernel(last, *refs),
        out_shape=tuple(shapes),
        compiler_params=params(4),
        name="spread",
    )(parts, current, gain, *held)


def per_device(
    prefill_rows, row_group, lengths, decode_state, norm_gain, w_query, w_key, w_value, w_out
):
    groups = lax.axis_size("grp")
    heads = lax.axis_size("head")
    rows_local, width = prefill_rows.shape
    plane_rows = rows_local * heads
    cap = (rows_local // groups + rows_local // groups // 2) * heads
    requests = lengths.shape[1]
    my_group = lax.axis_index("grp")
    my_head = lax.axis_index("head")
    share = width // heads
    f32, bf16 = jnp.float32, jnp.bfloat16

    core = my_head % 2
    with jax.named_scope("rows"):
        n = rows_local
        kept, given = norm_split(row_group, prefill_rows, norm_gain)
        got = send(given, CORE)
        start = jnp.concatenate([kept, got])
        f2 = send(start, lane(2, 0))
        f1 = send(start, lane(1, 0))
        f3 = send(start, lane(3, 0))
        l0 = jnp.concatenate([kept, f1[:n], f2[:n], f3[:n]])
        l1 = jnp.concatenate([got, f1[n:], f2[n:], f3[n:]])
        s11 = send(l1, lane(0, 1))
        s30 = send(l0, lane(0, 3))
        s10 = send(l0, lane(0, 1))
        s31 = send(l1, lane(0, 3))
        s20 = send(s30, lane(0, 1))
        s21 = send(s11, lane(0, 3))
    with jax.named_scope("weights"):
        their_half = send(other_half(w_key, w_value, f1), CORE)

    with jax.named_scope("places"):
        group_ids = jnp.arange(groups, dtype=jnp.int32)
        late_lengths = after(lengths, f1)
        my_lengths = jnp.sum(
            jnp.where((group_ids == my_group)[:, None], late_lengths, 0), axis=0
        )
        request = jnp.arange(requests, dtype=jnp.int32)
        my_ends = jnp.sum(jnp.where(request[None, :] <= request[:, None], my_lengths[None, :], 0), axis=1)
        my_starts = my_ends - my_lengths
        edges = jnp.stack([my_starts, my_ends]).astype(f32)
        edge_row = jnp.pad(edges, ((0, 0), (0, HD - requests)), constant_values=1e9)
        edge_col = jnp.repeat(edges, HD, axis=0).T.reshape(requests, 2 * HD)
        spots = jnp.arange(HD, dtype=jnp.int32) + 0 * my_lengths[0]
        table = jnp.concatenate(angles_of(spots), axis=1)
        table_high = table.astype(bf16)
        table_low = (table - table_high.astype(f32)).astype(bf16)

    with jax.named_scope("project"):
        own_a, other_a, ids_a, half_weights = project(
            [l0, l1, s10, s11, s30, s31], w_key, w_value, their_half
        )
        own_b, other_b, ids_b = project_last(s20, s21, half_weights)
        leaving = finish(
            groups, cap, own_a, own_b, send(other_a, CORE), send(other_b, CORE), ids_a, ids_b
        )
        arrived = [leaving[0]]
        for hop in range(1, groups):
            pairs = [(g, (g + hop) % groups) for g in range(groups)]
            arrived.append(lax.ppermute(leaving[hop], "grp", pairs))
        (w_out,) = hold([w_out], leaving[0])
        cache_keys, cache_values, bias = settle(edge_row, edge_col, table_high, table_low, arrived)

    with jax.named_scope("first"):
        late_state = after(decode_state, f1)
        current = lax.dynamic_slice_in_dim(late_state, my_head * share, share, 1)
        late_gain = after(norm_gain, f1)
        my_gain = lax.dynamic_slice_in_dim(late_gain, my_head * share, share, 0)[None, :]
        inverse = (1.0 / late_gain)[None, :]
        decode_rows = normed(late_state, norm_gain)
        extra = [
            jnp.dot(decode_rows, w, preferred_element_type=f32) for w in (w_query, w_key, w_value)
        ]
        at_step = my_lengths[None, :] + jnp.arange(STEPS, dtype=jnp.int32)[:, None]
        turns = jnp.concatenate(angles_of(at_step), axis=-1)
        extra += [current, my_gain, inverse]
    held = [w_query, w_key, w_value, w_out]
    olds = []
    for step in range(STEPS):
        term, new_key, new_value = attend(
            step, heads, turns, cache_keys, cache_values, bias, w_out, olds, extra
        )
        olds.append((new_key, new_value))
        parts = lax.all_to_all(term, "head", split_axis=0, concat_axis=0, tiled=True)
        last = step + 1 == STEPS
        current, *spreading = spread(last, parts, current, my_gain, [] if last else held)
        if not last:
            rows = lax.all_to_all(spreading[0], "head", split_axis=0, concat_axis=0, tiled=True)
            extra = [rows, inverse, w_query, w_key, w_value]
    return current


def solution(mesh):
    return jax.shard_map(
        per_device,
        mesh=mesh,
        in_specs=(
            P(("grp", "head"), None),
            P(("grp", "head")),
            P(),
            P("grp", None),
            P(),
            P(None, "head"),
            P(None, "head"),
            P(None, "head"),
            P("head", None),
        ),
        out_specs=P("grp", "head"),
        check_vma=False,
    )
```

```python
import math

import jax
import jax.numpy as jnp
from jax import lax
from jax.experimental import pallas as pl
from jax.experimental.pallas import tpu as pltpu
from jax.sharding import PartitionSpec as P

HD = 128
STEPS = 4
EPSILON = 1e-05
ROPE_BASE = 10000.0
MASKED = -1e30


def normed(values, norm_gain):
    widened = values.astype(jnp.float32)
    factor = lax.rsqrt(jnp.mean(widened * widened, axis=-1, keepdims=True) + EPSILON)
    return (widened * factor * norm_gain).astype(jnp.bfloat16)


def angles_of(positions):
    half = HD // 2
    frequency = jnp.exp(
        jnp.arange(half, dtype=jnp.float32) * (-2.0 * math.log(ROPE_BASE) / HD)
    )
    angles = positions.astype(jnp.float32)[..., None] * frequency
    cosine = jnp.cos(angles)
    sine = jnp.sin(angles)
    return (
        jnp.concatenate([cosine, cosine], axis=-1),
        jnp.concatenate([-sine, sine], axis=-1),
    )


def turned(values, cosine, sine):
    half = HD // 2
    swapped = jnp.concatenate([values[..., half:], values[..., :half]], axis=-1)
    return values * cosine + swapped * sine


NX = 4
NY = 4
HELD = ((0, 0), (0, 1), (1, 0), (1, 1), (3, 0), (3, 1), (2, 0), (2, 1))
EARLY = 6
EMPTY = 1e30


def head_pairs(move):
    pairs = []
    for y in range(NY):
        for x in range(NX):
            for c in range(2):
                ty, tx, tc = move(y, x, c)
                pairs.append(((y * NX + x) * 2 + c, (ty * NX + tx) * 2 + tc))
    return pairs


def lane(first, second):
    return head_pairs(
        lambda y, x, c: (y ^ second, x ^ first, c) if c == 0 else (y ^ first, x ^ second, c)
    )


CORE = head_pairs(lambda y, x, c: (y, x, c ^ 1))


def send(values, pairs):
    return lax.ppermute(values, "head", pairs)


def after(values, piece):
    return values + (piece[0, 0].astype(jnp.float32) * 0.0).astype(values.dtype)


def params(mib):
    return pltpu.CompilerParams(vmem_limit_bytes=mib * 1024 * 1024)


def norm_split_kernel(group_ref, rows_ref, gain_ref, kept_ref, given_ref):
    n, half = rows_ref.shape[0], rows_ref.shape[1] // 2
    core = lax.rem(lax.axis_index("head"), 2)
    rows = rows_ref[...].astype(jnp.float32)
    factor = lax.rsqrt(jnp.mean(rows * rows, axis=1, keepdims=True) + EPSILON)
    result = (rows * factor * gain_ref[...]).astype(jnp.bfloat16)
    row = lax.broadcasted_iota(jnp.int32, (n, HD), 0)
    ids = jnp.zeros((n, HD), jnp.int32)
    for j in range(n):
        ids = jnp.where(row == j, group_ref[j], ids)
    ids = ids.astype(jnp.float32).astype(jnp.bfloat16)
    kept_ref[:, half:] = ids
    given_ref[:, half:] = ids

    @pl.when(core == 0)
    def _():
        kept_ref[:, :half] = result[:, :half]
        given_ref[:, :half] = result[:, half:]

    @pl.when(core == 1)
    def _():
        kept_ref[:, :half] = result[:, half:]
        given_ref[:, :half] = result[:, :half]


def norm_split(groups, rows, gain):
    shape = jax.ShapeDtypeStruct((rows.shape[0], rows.shape[1] // 2 + HD), jnp.bfloat16)
    whole = pl.BlockSpec(memory_space=pltpu.VMEM)
    return pl.pallas_call(
        norm_split_kernel,
        out_shape=(shape, shape),
        in_specs=[pl.BlockSpec(memory_space=pltpu.SMEM), whole, whole],
        compiler_params=params(56),
        name="norm_split",
    )(groups, rows, gain.reshape(1, -1))


def other_half_kernel(key_ref, value_ref, dep_ref, out_ref, sems):
    half = out_ref.shape[0]
    core = lax.rem(lax.axis_index("head"), 2)
    rows = pl.ds(pl.multiple_of((1 - core) * half, half), half)
    one = pltpu.make_async_copy(key_ref.at[rows], out_ref.at[:, :HD], sems.at[0])
    two = pltpu.make_async_copy(value_ref.at[rows], out_ref.at[:, HD:], sems.at[1])
    one.start()
    two.start()
    one.wait()
    two.wait()


def other_half(w_key, w_value, dep):
    anywhere = pl.BlockSpec(memory_space=pl.ANY)
    return pl.pallas_call(
        other_half_kernel,
        out_shape=jax.ShapeDtypeStruct((w_key.shape[0] // 2, 2 * HD), jnp.bfloat16),
        in_specs=[anywhere] * 3,
        out_specs=anywhere,
        scratch_shapes=[pltpu.SemaphoreType.DMA((2,))],
        compiler_params=params(4),
        name="other_half",
    )(w_key, w_value, dep)


def lines_kernel(kept, got, f1, f2, f3, l0_ref, l1_ref):
    n = kept.shape[0]
    for i, (first, second) in enumerate(
        [(kept[...], got[...])] + [(f[:n, :], f[n:, :]) for f in (f1, f2, f3)]
    ):
        l0_ref[i * n : (i + 1) * n, :] = first
        l1_ref[i * n : (i + 1) * n, :] = second


def lines(kept, got, f1, f2, f3):
    shape = jax.ShapeDtypeStruct((NX * kept.shape[0], kept.shape[1]), kept.dtype)
    return pl.pallas_call(
        lines_kernel, out_shape=(shape, shape), compiler_params=params(6), name="lines"
    )(kept, got, f1, f2, f3)


CHUNKS = 4


def project_kernel(count, *refs):
    pieces = refs[:count]
    key_ref, value_ref, their_ref, own_ref, other_ref, ids_ref, w, x, piece_sems, weight_sems = refs[
        count:
    ]
    size = pieces[0].shape[0]
    half = w.shape[0]
    depth = half // CHUNKS
    core = lax.rem(lax.axis_index("head"), 2)
    loads = []
    for k in range(CHUNKS):
        mine = pl.ds(pl.multiple_of(core * half + k * depth, depth), depth)
        here = slice(k * depth, (k + 1) * depth)
        loads.append(
            [
                pltpu.make_async_copy(key_ref.at[mine], w.at[here, :HD], weight_sems.at[k, 0]),
                pltpu.make_async_copy(
                    value_ref.at[mine], w.at[here, HD : 2 * HD], weight_sems.at[k, 1]
                ),
                pltpu.make_async_copy(
                    their_ref.at[here], w.at[here, 2 * HD :], weight_sems.at[k, 2]
                ),
            ]
        )
    rows = [
        pltpu.make_async_copy(p, x.at[i * size : (i + 1) * size], piece_sems.at[i])
        for i, p in enumerate(pieces)
    ]
    for load in loads[0]:
        load.start()
    for row in rows:
        row.start()
    for k in range(1, CHUNKS):
        for load in loads[k]:
            load.start()
    for row in rows:
        row.wait()
    ids_ref[...] = x[:, half:]
    for k in range(CHUNKS):
        for load in loads[k]:
            load.wait()
        here = slice(k * depth, (k + 1) * depth)
        term = jnp.dot(x[:, here], w[here, :], preferred_element_type=jnp.float32)
        if k == 0:
            own_ref[...] = term[:, : 2 * HD]
            other_ref[...] = term[:, 2 * HD :]
        else:
            own_ref[...] += term[:, : 2 * HD]
            other_ref[...] += term[:, 2 * HD :]


def project(pieces, w_key, w_value, their_half):
    count = len(pieces)
    size, wide = pieces[0].shape
    half = wide - HD
    rows = count * size
    anywhere = pl.BlockSpec(memory_space=pl.ANY)
    shape = jax.ShapeDtypeStruct((rows, 2 * HD), jnp.float32)
    return pl.pallas_call(
        lambda *refs: project_kernel(count, *refs),
        out_shape=(
            shape,
            shape,
            jax.ShapeDtypeStruct((rows, HD), jnp.bfloat16),
            jax.ShapeDtypeStruct((half, 4 * HD), jnp.bfloat16),
        ),
        in_specs=[anywhere] * (count + 3),
        scratch_shapes=[
            pltpu.VMEM((rows, wide), jnp.bfloat16),
            pltpu.SemaphoreType.DMA((count,)),
            pltpu.SemaphoreType.DMA((CHUNKS, 3)),
        ],
        compiler_params=params(14),
        name="project",
    )(*pieces, w_key, w_value, their_half)


def project_last_kernel(first, second, w, own_ref, other_ref, ids_ref):
    n, half = first.shape[0], w.shape[0]
    x = jnp.concatenate([first[...], second[...]], axis=0)
    ids_ref[...] = x[:, half:]
    term = jnp.dot(x[:, :half], w[...], preferred_element_type=jnp.float32)
    own_ref[...] = term[:, : 2 * HD]
    other_ref[...] = term[:, 2 * HD :]


def project_last(first, second, weights):
    rows = 2 * first.shape[0]
    shape = jax.ShapeDtypeStruct((rows, 2 * HD), jnp.float32)
    return pl.pallas_call(
        project_last_kernel,
        out_shape=(shape, shape, jax.ShapeDtypeStruct((rows, HD), jnp.bfloat16)),
        compiler_params=params(10),
        name="project_last",
    )(first, second, weights)


def origin(shape, dim, head):
    at = lax.broadcasted_iota(jnp.int32, shape, dim)
    block, row = at >> 4, at & 15
    turn = block >> 3
    d_second, d_first, d_core = turn ^ (turn >> 1), block & 3, (block >> 2) & 1
    core = head & 1
    dy = jnp.where(core == 0, d_second, d_first)
    dx = jnp.where(core == 0, d_first, d_second)
    y, x, c = (head >> 3) ^ dy, ((head >> 1) & 3) ^ dx, core ^ d_core
    return (((y * NX + x) * 2 + c) << 4) + row


def finish_kernel(groups, cap, own_a, own_b, their_a, their_b, ids_a, ids_b, *refs):
    outs, packed = refs[:groups], refs[groups]
    total = packed.shape[0]
    n = total // (len(HELD) * NX)
    early = EARLY * NX
    head = lax.axis_index("head")
    group = lax.axis_index("grp").astype(jnp.float32)

    def block(first, second, i):
        return first[i * n : (i + 1) * n] if i < early else second[(i - early) * n : (i - early + 1) * n]

    for at, (d_second, d_core) in enumerate(HELD):
        for d_first in range(NX):
            i = at * NX + d_first
            j = HELD.index((d_first, 1 - d_core)) * NX + d_second
            both = block(own_a, own_b, i) + block(their_a, their_b, j)
            packed[i * n : (i + 1) * n, :] = both.astype(jnp.bfloat16)
    hop = jnp.concatenate([ids_a[...], ids_b[...]], axis=0).astype(jnp.float32) - group
    hop = jnp.where(hop < 0.0, hop + groups, hop)
    lanes = lax.broadcasted_iota(jnp.int32, (1, HD), 1).astype(jnp.float32)
    match = jnp.where(hop == lanes, 1.0, 0.0)
    earlier = origin((1, total), 1, head) < origin((total, 1), 0, head)
    ranks = jnp.dot(
        jnp.where(earlier, 1.0, 0.0).astype(jnp.bfloat16),
        match.astype(jnp.bfloat16),
        preferred_element_type=jnp.float32,
    )
    order = jnp.sum(ranks * match, axis=1, keepdims=True)
    slot = hop[:, :1] * cap + order
    slots = lax.broadcasted_iota(jnp.int32, (1, groups * cap), 1).astype(jnp.float32)
    pick = jnp.where(slots == slot, 1.0, 0.0).astype(jnp.bfloat16)
    routed = lax.dot_general(
        pick, packed[...], (((0,), (0,)), ((), ())), preferred_element_type=jnp.float32
    )
    counts = jnp.sum(match, axis=0, keepdims=True)
    step = lax.broadcasted_iota(jnp.int32, (cap, 1), 0).astype(jnp.float32)
    for g in range(groups):
        rows = slice(g * cap, (g + 1) * cap)
        filled = step < counts[:, g : g + 1]
        outs[g][:, :HD] = jnp.where(filled, routed[rows, :HD], EMPTY).astype(jnp.bfloat16)
        outs[g][:, HD:] = routed[rows, HD:].astype(jnp.bfloat16)


def finish(groups, cap, own_a, own_b, their_a, their_b, ids_a, ids_b):
    shape = jax.ShapeDtypeStruct((cap, 2 * HD), jnp.bfloat16)
    return pl.pallas_call(
        lambda *refs: finish_kernel(groups, cap, *refs),
        out_shape=(shape,) * groups,
        scratch_shapes=[pltpu.VMEM((own_a.shape[0] + own_b.shape[0], 2 * HD), jnp.bfloat16)],
        compiler_params=params(12),
        name="finish",
    )(own_a, own_b, their_a, their_b, ids_a, ids_b)


def settle_kernel(groups, edge_row, edge_col, high_ref, low_ref, *refs):
    parts = refs[:groups]
    key_ref, value_ref, bias_ref, hot = refs[groups:]
    cap = parts[0].shape[0]
    slots = groups * cap
    me = lax.axis_index("grp")
    sources = [lax.rem(me + groups - g, groups) for g in range(groups)]
    starts, ends = edge_row[0:1, :], edge_row[1:2, :]
    lanes = lax.broadcasted_iota(jnp.int32, (1, HD), 1).astype(jnp.float32)
    step = lax.broadcasted_iota(jnp.int32, (cap, 1), 0).astype(jnp.float32)
    across = lax.broadcasted_iota(jnp.int32, (1, slots), 1).astype(jnp.float32)
    counts = []
    for part in parts:
        full = part[:, :HD].astype(jnp.float32) < EMPTY / 2
        counts.append(jnp.sum(jnp.where(full, 1.0, 0.0), axis=0, keepdims=True)[:, :1])
    cells = across
    open_slots = across < 0.0
    for g in range(groups):
        base = jnp.zeros((1, 1), jnp.float32)
        for other in range(groups):
            if other != g:
                before = jnp.where(sources[other] < sources[g], 1.0, 0.0)
                base = base + counts[other] * before
        rows = slice(g * cap, (g + 1) * cap)
        cell = base + step
        inside = (cell >= starts) & (cell < ends)
        place = cell - jnp.sum(jnp.where(inside, starts, 0.0), axis=1, keepdims=True)
        hot[rows, :] = jnp.where(lanes == place, 1.0, 0.0).astype(jnp.bfloat16)
        here = (across >= g * cap) & (across < (g + 1) * cap)
        cells = jnp.where(here, across - g * cap + base, cells)
        open_slots = open_slots | (here & (across - g * cap < counts[g]))
        value_ref[rows, :] = parts[g][:, HD:]
    low_edge, high_edge = edge_col[:, 0:1], edge_col[:, HD : HD + 1]
    mine = (cells >= low_edge) & (cells < high_edge) & open_slots
    bias_ref[...] = jnp.where(mine, 0.0, MASKED)
    trig = jnp.dot(hot[...], high_ref[...], preferred_element_type=jnp.float32)
    trig = trig + jnp.dot(hot[...], low_ref[...], preferred_element_type=jnp.float32)
    for g in range(groups):
        rows = slice(g * cap, (g + 1) * cap)
        keys = parts[g][:, :HD].astype(jnp.float32)
        keys = jnp.where(keys < EMPTY / 2, keys, 0.0)
        turned_keys = keys * trig[rows, :HD] + pltpu.roll(keys, HD // 2, 1) * trig[rows, HD:]
        key_ref[rows, :] = turned_keys.astype(jnp.bfloat16)


def settle(edge_row, edge_col, high, low, parts):
    slots = len(parts) * parts[0].shape[0]
    wide = jax.ShapeDtypeStruct((slots, HD), jnp.bfloat16)
    return pl.pallas_call(
        lambda *refs: settle_kernel(len(parts), *refs),
        out_shape=(wide, wide, jax.ShapeDtypeStruct((edge_col.shape[0], slots), jnp.float32)),
        scratch_shapes=[pltpu.VMEM((slots, HD), jnp.bfloat16)],
        compiler_params=params(8),
        name="settle",
    )(edge_row, edge_col, high, low, *parts)


def hold_kernel(count, *refs):
    sems = refs[-1]
    copies = [
        pltpu.make_async_copy(refs[i], refs[count + 1 + i], sems.at[i]) for i in range(count)
    ]
    for copy in copies:
        copy.start()
    for copy in copies:
        copy.wait()


def hold(arrays, dep):
    count = len(arrays)
    return pl.pallas_call(
        lambda *refs: hold_kernel(count, *refs),
        out_shape=tuple(jax.ShapeDtypeStruct(a.shape, a.dtype) for a in arrays),
        in_specs=[pl.BlockSpec(memory_space=pl.ANY)] * (count + 1),
        out_specs=(pl.BlockSpec(memory_space=pltpu.VMEM),) * count,
        scratch_shapes=[pltpu.SemaphoreType.DMA((count,))],
        compiler_params=params(10),
        name="hold",
    )(*arrays, dep)


def rotated(values, turn):
    return values * turn[:, :HD] + pltpu.roll(values, HD // 2, 1) * turn[:, HD:]


def attend_kernel(step, *refs):
    f32, bf16 = jnp.float32, jnp.bfloat16
    turn_ref, key_ref, cache_ref, bias_ref, out_weight, *rest = refs
    turn = turn_ref[step]
    olds = [(rest[2 * i], rest[2 * i + 1]) for i in range(step)]
    rest = rest[2 * step :]
    if step:
        row_ref, inverse_ref, wq_ref, wk_ref, wv_ref, term_ref, new_key_ref, new_value_ref = rest
        blocks, n, share = row_ref.shape
        squares = jnp.zeros((n, share), f32)
        for i in range(blocks):
            plain = row_ref[i].astype(f32) * inverse_ref[:, i * share : (i + 1) * share]
            squares = squares + plain * plain
        mean = jnp.sum(squares, axis=1, keepdims=True) * (1.0 / (blocks * share))
        factor = lax.rsqrt(mean + EPSILON)
        rows = jnp.concatenate([row_ref[i] for i in range(blocks)], axis=1)
        query = jnp.dot(rows, wq_ref[...], preferred_element_type=f32) * factor
        key = jnp.dot(rows, wk_ref[...], preferred_element_type=f32) * factor
        value = jnp.dot(rows, wv_ref[...], preferred_element_type=f32) * factor
    else:
        query_ref, first_key, first_value, _, _, _, term_ref, new_key_ref, new_value_ref = rest
        query, key, value = query_ref[...], first_key[...], first_value[...]
    query = rotated(query, turn).astype(bf16)
    key = rotated(key, turn).astype(bf16)
    value = value.astype(bf16)
    new_key_ref[...] = key
    new_value_ref[...] = value
    scale = HD ** (-0.5)
    scores = lax.dot_general(
        query, key_ref[...], (((1,), (1,)), ((), ())), preferred_element_type=f32
    )
    scores = scores * scale + bias_ref[...]
    wide = query.astype(f32)
    pairs = [(k[...], v[...]) for k, v in olds] + [(key, value)]
    fresh = [jnp.sum(wide * k.astype(f32), axis=1, keepdims=True) * scale for k, _ in pairs]
    peak = jnp.max(scores, axis=1, keepdims=True)
    for f in fresh:
        peak = jnp.maximum(peak, f)
    cache_exp = jnp.exp(scores - peak)
    fresh_exp = [jnp.exp(f - peak) for f in fresh]
    total = jnp.sum(cache_exp, axis=1, keepdims=True)
    for f in fresh_exp:
        total = total + f
    weights = (cache_exp / total).astype(bf16)
    attended = jnp.dot(weights, cache_ref[...], preferred_element_type=f32)
    for f, (_, v) in zip(fresh_exp, pairs):
        attended = attended + (f / total).astype(bf16).astype(f32) * v.astype(f32)
    attended = attended.astype(bf16)
    blocks, _, share = term_ref.shape
    wide_share = 4 * share
    for j in range(blocks // 4):
        term = jnp.dot(
            attended, out_weight[:, j * wide_share : (j + 1) * wide_share], preferred_element_type=f32
        ).astype(bf16)
        for i in range(4):
            term_ref[4 * j + i] = term[:, i * share : (i + 1) * share]


def attend(step, blocks, turns, keys, cache, bias, w_out, olds, extra):
    n = bias.shape[0]
    share = w_out.shape[1] // blocks
    flat = [x for pair in olds for x in pair]
    small = jax.ShapeDtypeStruct((n, HD), jnp.bfloat16)
    return pl.pallas_call(
        lambda *refs: attend_kernel(step, *refs),
        out_shape=(jax.ShapeDtypeStruct((blocks, n, share), jnp.bfloat16), small, small),
        compiler_params=params(10),
        name="attend",
    )(turns, keys, cache, bias, w_out, *flat, *extra)


def spread_kernel(last, part_ref, current_ref, gain_ref, *refs):
    next_ref, *out = refs[-1:] if last else refs[-2:]
    total = current_ref[...]
    for i in range(part_ref.shape[0]):
        total = total + part_ref[i].astype(jnp.float32)
    next_ref[...] = total
    if not last:
        piece = (total * gain_ref[...]).astype(jnp.bfloat16)
        for i in range(part_ref.shape[0]):
            out[0][i] = piece


def spread(last, parts, current, gain, held):
    shapes = [jax.ShapeDtypeStruct(current.shape, jnp.float32)]
    if not last:
        shapes.append(jax.ShapeDtypeStruct(parts.shape, jnp.bfloat16))
    return pl.pallas_call(
        lambda *refs: spread_kernel(last, *refs),
        out_shape=tuple(shapes),
        compiler_params=params(4),
        name="spread",
    )(parts, current, gain, *held)


def per_device(
    prefill_rows, row_group, lengths, decode_state, norm_gain, w_query, w_key, w_value, w_out
):
    groups = lax.axis_size("grp")
    heads = lax.axis_size("head")
    rows_local, width = prefill_rows.shape
    plane_rows = rows_local * heads
    cap = (rows_local // groups + rows_local // groups // 2) * heads
    requests = lengths.shape[1]
    my_group = lax.axis_index("grp")
    my_head = lax.axis_index("head")
    share = width // heads
    f32, bf16 = jnp.float32, jnp.bfloat16

    core = my_head % 2
    with jax.named_scope("rows"):
        kept, given = norm_split(row_group, prefill_rows, norm_gain)
        got = send(given, CORE)
        start = jnp.concatenate([kept, got])
        f2 = send(start, lane(2, 0))
        f1 = send(start, lane(1, 0))
        f3 = send(start, lane(3, 0))
        l0, l1 = lines(kept, got, f1, f2, f3)
        s11 = send(l1, lane(0, 1))
        s30 = send(l0, lane(0, 3))
        s10 = send(l0, lane(0, 1))
        s31 = send(l1, lane(0, 3))
        s20 = send(s30, lane(0, 1))
        s21 = send(s11, lane(0, 3))
    with jax.named_scope("weights"):
        their_half = send(other_half(w_key, w_value, f1), CORE)

    with jax.named_scope("places"):
        group_ids = jnp.arange(groups, dtype=jnp.int32)
        late_lengths = after(lengths, f1)
        my_lengths = jnp.sum(
            jnp.where((group_ids == my_group)[:, None], late_lengths, 0), axis=0
        )
        request = jnp.arange(requests, dtype=jnp.int32)
        my_ends = jnp.sum(jnp.where(request[None, :] <= request[:, None], my_lengths[None, :], 0), axis=1)
        my_starts = my_ends - my_lengths
        edges = jnp.stack([my_starts, my_ends]).astype(f32)
        edge_row = jnp.pad(edges, ((0, 0), (0, HD - requests)), constant_values=1e9)
        edge_col = jnp.repeat(edges, HD, axis=0).T.reshape(requests, 2 * HD)
        spots = jnp.arange(HD, dtype=jnp.int32) + 0 * my_lengths[0]
        table = jnp.concatenate(angles_of(spots), axis=1)
        table_high = table.astype(bf16)
        table_low = (table - table_high.astype(f32)).astype(bf16)

    with jax.named_scope("project"):
        own_a, other_a, ids_a, half_weights = project(
            [l0, l1, s10, s11, s30, s31], w_key, w_value, their_half
        )
        own_b, other_b, ids_b = project_last(s20, s21, half_weights)
        leaving = finish(
            groups, cap, own_a, own_b, send(other_a, CORE), send(other_b, CORE), ids_a, ids_b
        )
        arrived = [leaving[0]]
        for hop in range(1, groups):
            pairs = [(g, (g + hop) % groups) for g in range(groups)]
            arrived.append(lax.ppermute(leaving[hop], "grp", pairs))
        (w_out,) = hold([w_out], leaving[0])
        cache_keys, cache_values, bias = settle(edge_row, edge_col, table_high, table_low, arrived)

    with jax.named_scope("first"):
        late_state = after(decode_state, got)
        current = lax.dynamic_slice_in_dim(late_state, my_head * share, share, 1)
        late_gain = after(norm_gain, got)
        my_gain = lax.dynamic_slice_in_dim(late_gain, my_head * share, share, 0)[None, :]
        inverse = (1.0 / late_gain)[None, :]
        decode_rows = normed(late_state, norm_gain)
        extra = [
            jnp.dot(decode_rows, w, preferred_element_type=f32) for w in (w_query, w_key, w_value)
        ]
        at_step = my_lengths[None, :] + jnp.arange(STEPS, dtype=jnp.int32)[:, None]
        turns = jnp.concatenate(angles_of(at_step), axis=-1)
        extra += [current, my_gain, inverse]
    held = [w_query, w_key, w_value, w_out]
    olds = []
    for step in range(STEPS):
        term, new_key, new_value = attend(
            step, heads, turns, cache_keys, cache_values, bias, w_out, olds, extra
        )
        olds.append((new_key, new_value))
        parts = lax.all_to_all(term, "head", split_axis=0, concat_axis=0, tiled=True)
        last = step + 1 == STEPS
        current, *spreading = spread(last, parts, current, my_gain, [] if last else held)
        if not last:
            rows = lax.all_to_all(spreading[0], "head", split_axis=0, concat_axis=0, tiled=True)
            extra = [rows, inverse, w_query, w_key, w_value]
    return current


def solution(mesh):
    return jax.shard_map(
        per_device,
        mesh=mesh,
        in_specs=(
            P(("grp", "head"), None),
            P(("grp", "head")),
            P(),
            P("grp", None),
            P(),
            P(None, "head"),
            P(None, "head"),
            P(None, "head"),
            P("head", None),
        ),
        out_specs=P("grp", "head"),
        check_vma=False,
    )
```

```python
import math

import jax
import jax.numpy as jnp
from jax import lax
from jax.experimental import pallas as pl
from jax.experimental.pallas import tpu as pltpu
from jax.sharding import PartitionSpec as P

HD = 128
STEPS = 4
EPSILON = 1e-05
ROPE_BASE = 10000.0
MASKED = -1e30


def normed(values, norm_gain):
    widened = values.astype(jnp.float32)
    factor = lax.rsqrt(jnp.mean(widened * widened, axis=-1, keepdims=True) + EPSILON)
    return (widened * factor * norm_gain).astype(jnp.bfloat16)


def angles_of(positions):
    half = HD // 2
    frequency = jnp.exp(
        jnp.arange(half, dtype=jnp.float32) * (-2.0 * math.log(ROPE_BASE) / HD)
    )
    angles = positions.astype(jnp.float32)[..., None] * frequency
    cosine = jnp.cos(angles)
    sine = jnp.sin(angles)
    return (
        jnp.concatenate([cosine, cosine], axis=-1),
        jnp.concatenate([-sine, sine], axis=-1),
    )


def turned(values, cosine, sine):
    half = HD // 2
    swapped = jnp.concatenate([values[..., half:], values[..., :half]], axis=-1)
    return values * cosine + swapped * sine


NX = 4
NY = 4
EMPTY = 1e30


def head_pairs(move):
    pairs = []
    for y in range(NY):
        for x in range(NX):
            for c in range(2):
                ty, tx, tc = move(y, x, c)
                pairs.append(((y * NX + x) * 2 + c, (ty * NX + tx) * 2 + tc))
    return pairs


def lane(first, second):
    return head_pairs(
        lambda y, x, c: (y ^ second, x ^ first, c) if c == 0 else (y ^ first, x ^ second, c)
    )


CORE = head_pairs(lambda y, x, c: (y, x, c ^ 1))


def send(values, pairs):
    return lax.ppermute(values, "head", pairs)


def after(values, piece):
    return values + (piece[0, 0].astype(jnp.float32) * 0.0).astype(values.dtype)


def params(mib):
    return pltpu.CompilerParams(vmem_limit_bytes=mib * 1024 * 1024)


def norm_kernel(group_ref, rows_ref, gain_ref, out_ref):
    n, half = rows_ref.shape[0], rows_ref.shape[1] // 2
    rows = rows_ref[...].astype(jnp.float32)
    factor = lax.rsqrt(jnp.mean(rows * rows, axis=1, keepdims=True) + EPSILON)
    result = (rows * factor * gain_ref[...]).astype(jnp.bfloat16)
    row = lax.broadcasted_iota(jnp.int32, (n, HD), 0)
    ids = jnp.zeros((n, HD), jnp.int32)
    for j in range(n):
        ids = jnp.where(row == j, group_ref[j], ids)
    ids = ids.astype(jnp.float32).astype(jnp.bfloat16)
    for side in range(2):
        out_ref[side * n : (side + 1) * n, :half] = result[:, side * half : (side + 1) * half]
        out_ref[side * n : (side + 1) * n, half:] = ids


def norm_rows(groups, rows, gain):
    n, width = rows.shape
    whole = pl.BlockSpec(memory_space=pltpu.VMEM)
    return pl.pallas_call(
        norm_kernel,
        out_shape=jax.ShapeDtypeStruct((2 * n, width // 2 + HD), jnp.bfloat16),
        in_specs=[pl.BlockSpec(memory_space=pltpu.SMEM), whole, whole],
        compiler_params=params(56),
        name="norm_rows",
    )(groups, rows, gain.reshape(1, -1))


def lines_kernel(start, f1, f2, f3, *refs):
    l0_ref, l1_ref = refs[-2:]
    n = start.shape[0] // 2
    for i, f in enumerate((start, f1, f2, f3)):
        l0_ref[i * n : (i + 1) * n, :] = f[:n, :]
        l1_ref[i * n : (i + 1) * n, :] = f[n:, :]


def lines(start, f1, f2, f3, *deps):
    shape = jax.ShapeDtypeStruct((NX * start.shape[0] // 2, start.shape[1]), start.dtype)
    return pl.pallas_call(
        lines_kernel, out_shape=(shape, shape), compiler_params=params(6), name="lines"
    )(start, f1, f2, f3, *deps)


CHUNKS = 8


def project_kernel(count, *refs):
    pieces = refs[: 2 * count]
    weights = refs[2 * count : 2 * count + 4]
    own_ref, other_ref, ids_ref, w, x, total, piece_sems, weight_sems = refs[2 * count + 4 :]
    size = pieces[0].shape[0]
    rows = count * size
    depth = w.shape[0] // CHUNKS
    half = w.shape[0] // 2
    loads = []
    for k in range(CHUNKS):
        here = slice(k * depth, (k + 1) * depth)
        loads.append(
            [
                pltpu.make_async_copy(
                    weight.at[here], w.at[here, i * HD : (i + 1) * HD], weight_sems.at[k, i]
                )
                for i, weight in enumerate(weights)
            ]
        )
    fetches = [
        pltpu.make_async_copy(p, x.at[i * size : (i + 1) * size], piece_sems.at[i])
        for i, p in enumerate(pieces)
    ]
    for load in loads[0]:
        load.start()
    for fetch in fetches:
        fetch.start()
    for k in range(1, CHUNKS):
        for load in loads[k]:
            load.start()
    for fetch in fetches[:count]:
        fetch.wait()
    for k in range(CHUNKS):
        if k == CHUNKS // 2:
            for fetch in fetches[count:]:
                fetch.wait()
        for load in loads[k]:
            load.wait()
        here = slice(k * depth, (k + 1) * depth)
        side = 2 * k // CHUNKS
        columns = slice(k * depth - side * half, (k + 1) * depth - side * half)
        term = jnp.dot(
            x[side * rows : (side + 1) * rows, columns], w[here, :], preferred_element_type=jnp.float32
        )
        if k == 0:
            total[...] = term
        else:
            total[...] += term
    ids_ref[...] = x[:rows, half:]
    own_ref[...] = total[:, : 2 * HD].astype(jnp.bfloat16)
    other_ref[:, : 2 * HD] = total[:, 2 * HD :].astype(jnp.bfloat16)
    other_ref[:, 2 * HD :] = x[:rows, half:]


def projected_shapes(rows):
    return (
        jax.ShapeDtypeStruct((rows, 2 * HD), jnp.bfloat16),
        jax.ShapeDtypeStruct((rows, 3 * HD), jnp.bfloat16),
        jax.ShapeDtypeStruct((rows, HD), jnp.bfloat16),
    )


def project(lows, highs, weights):
    count = len(lows)
    size, wide = lows[0].shape
    rows, width = count * size, 2 * (wide - HD)
    return pl.pallas_call(
        lambda *refs: project_kernel(count, *refs),
        out_shape=projected_shapes(rows)
        + (jax.ShapeDtypeStruct((width, 4 * HD), jnp.bfloat16),),
        in_specs=[pl.BlockSpec(memory_space=pl.ANY)] * (2 * count + 4),
        scratch_shapes=[
            pltpu.VMEM((2 * rows, wide), jnp.bfloat16),
            pltpu.VMEM((rows, 4 * HD), jnp.float32),
            pltpu.SemaphoreType.DMA((2 * count,)),
            pltpu.SemaphoreType.DMA((CHUNKS, 4)),
        ],
        compiler_params=params(18),
        name="project",
    )(*lows, *highs, *weights)


def project_low_kernel(low, w, total_ref):
    half = w.shape[0] // 2
    total_ref[...] = jnp.dot(low[:, :half], w[:half, :], preferred_element_type=jnp.float32)


def project_high_kernel(high, w, low_ref, own_ref, other_ref, ids_ref):
    half = w.shape[0] // 2
    total = low_ref[...]
    total = total + jnp.dot(high[:, :half], w[half:, :], preferred_element_type=jnp.float32)
    ids_ref[...] = high[:, half:]
    own_ref[...] = total[:, : 2 * HD].astype(jnp.bfloat16)
    other_ref[:, : 2 * HD] = total[:, 2 * HD :].astype(jnp.bfloat16)
    other_ref[:, 2 * HD :] = high[:, half:]


def project_last(low, high, weights):
    rows = low.shape[0]
    total = pl.pallas_call(
        project_low_kernel,
        out_shape=jax.ShapeDtypeStruct((rows, weights.shape[1]), jnp.float32),
        compiler_params=params(10),
        name="project_low",
    )(low, weights)
    return pl.pallas_call(
        project_high_kernel,
        out_shape=projected_shapes(rows),
        compiler_params=params(10),
        name="project_high",
    )(high, weights, total)


def origin(shape, dim, head):
    at = lax.broadcasted_iota(jnp.int32, shape, dim)
    turn, d_first, row = (at >> 6) & 3, (at >> 4) & 3, at & 15
    d_second = turn ^ (turn >> 1)
    c = (head & 1) ^ (at >> 8)
    dy = jnp.where(c == 0, d_second, d_first)
    dx = jnp.where(c == 0, d_first, d_second)
    y, x = (head >> 3) ^ dy, ((head >> 1) & 3) ^ dx
    return (((y * NX + x) * 2 + c) << 4) + row


def finish_kernel(groups, cap, own_a, own_b, ids_a, ids_b, their_a, their_b, *refs):
    outs, packed = refs[:groups], refs[groups]
    total = packed.shape[0]
    early, half = own_a.shape[0], total // 2
    head = lax.axis_index("head")
    group = lax.axis_index("grp").astype(jnp.float32)
    packed[:early, :] = own_a[...]
    packed[early:half, :] = own_b[...]
    packed[half : half + early, :] = their_a[:, : 2 * HD]
    packed[half + early :, :] = their_b[:, : 2 * HD]
    ids = [ids_a[...], ids_b[...], their_a[:, 2 * HD :], their_b[:, 2 * HD :]]
    hop = jnp.concatenate(ids, axis=0).astype(jnp.float32) - group
    hop = jnp.where(hop < 0.0, hop + groups, hop)
    lanes = lax.broadcasted_iota(jnp.int32, (1, HD), 1).astype(jnp.float32)
    match = jnp.where(hop == lanes, 1.0, 0.0)
    earlier = origin((1, total), 1, head) < origin((total, 1), 0, head)
    ranks = jnp.dot(
        jnp.where(earlier, 1.0, 0.0).astype(jnp.bfloat16),
        match.astype(jnp.bfloat16),
        preferred_element_type=jnp.float32,
    )
    order = jnp.sum(ranks * match, axis=1, keepdims=True)
    slot = hop[:, :1] * cap + order
    slots = lax.broadcasted_iota(jnp.int32, (1, groups * cap), 1).astype(jnp.float32)
    pick = jnp.where(slots == slot, 1.0, 0.0).astype(jnp.bfloat16)
    routed = lax.dot_general(
        pick, packed[...], (((0,), (0,)), ((), ())), preferred_element_type=jnp.float32
    )
    counts = jnp.sum(match, axis=0, keepdims=True)
    step = lax.broadcasted_iota(jnp.int32, (cap, 1), 0).astype(jnp.float32)
    for g in range(groups):
        rows = slice(g * cap, (g + 1) * cap)
        filled = step < counts[:, g : g + 1]
        outs[g][:, :HD] = jnp.where(filled, routed[rows, :HD], EMPTY).astype(jnp.bfloat16)
        outs[g][:, HD:] = routed[rows, HD:].astype(jnp.bfloat16)


def finish(groups, cap, own_a, own_b, ids_a, ids_b, their_a, their_b):
    shape = jax.ShapeDtypeStruct((cap, 2 * HD), jnp.bfloat16)
    rows = 2 * (own_a.shape[0] + own_b.shape[0])
    return pl.pallas_call(
        lambda *refs: finish_kernel(groups, cap, *refs),
        out_shape=(shape,) * groups,
        scratch_shapes=[pltpu.VMEM((rows, 2 * HD), jnp.bfloat16)],
        compiler_params=params(12),
        name="finish",
    )(own_a, own_b, ids_a, ids_b, their_a, their_b)


def settle_kernel(groups, edge_row, edge_col, high_ref, low_ref, *refs):
    parts = refs[:groups]
    key_ref, value_ref, bias_ref, hot = refs[groups:]
    cap = parts[0].shape[0]
    slots = groups * cap
    me = lax.axis_index("grp")
    sources = [lax.rem(me + groups - g, groups) for g in range(groups)]
    starts, ends = edge_row[0:1, :], edge_row[1:2, :]
    lanes = lax.broadcasted_iota(jnp.int32, (1, HD), 1).astype(jnp.float32)
    step = lax.broadcasted_iota(jnp.int32, (cap, 1), 0).astype(jnp.float32)
    across = lax.broadcasted_iota(jnp.int32, (1, slots), 1).astype(jnp.float32)
    counts = []
    for part in parts:
        full = part[:, :HD].astype(jnp.float32) < EMPTY / 2
        counts.append(jnp.sum(jnp.where(full, 1.0, 0.0), axis=0, keepdims=True)[:, :1])
    cells = across
    open_slots = across < 0.0
    for g in range(groups):
        base = jnp.zeros((1, 1), jnp.float32)
        for other in range(groups):
            if other != g:
                before = jnp.where(sources[other] < sources[g], 1.0, 0.0)
                base = base + counts[other] * before
        rows = slice(g * cap, (g + 1) * cap)
        cell = base + step
        inside = (cell >= starts) & (cell < ends)
        place = cell - jnp.sum(jnp.where(inside, starts, 0.0), axis=1, keepdims=True)
        hot[rows, :] = jnp.where(lanes == place, 1.0, 0.0).astype(jnp.bfloat16)
        here = (across >= g * cap) & (across < (g + 1) * cap)
        cells = jnp.where(here, across - g * cap + base, cells)
        open_slots = open_slots | (here & (across - g * cap < counts[g]))
        value_ref[rows, :] = parts[g][:, HD:]
    low_edge, high_edge = edge_col[:, 0:1], edge_col[:, HD : HD + 1]
    mine = (cells >= low_edge) & (cells < high_edge) & open_slots
    bias_ref[...] = jnp.where(mine, 0.0, MASKED)
    trig = jnp.dot(hot[...], high_ref[...], preferred_element_type=jnp.float32)
    trig = trig + jnp.dot(hot[...], low_ref[...], preferred_element_type=jnp.float32)
    for g in range(groups):
        rows = slice(g * cap, (g + 1) * cap)
        keys = parts[g][:, :HD].astype(jnp.float32)
        keys = jnp.where(keys < EMPTY / 2, keys, 0.0)
        turned_keys = keys * trig[rows, :HD] + pltpu.roll(keys, HD // 2, 1) * trig[rows, HD:]
        key_ref[rows, :] = turned_keys.astype(jnp.bfloat16)


def settle(edge_row, edge_col, high, low, parts):
    slots = len(parts) * parts[0].shape[0]
    wide = jax.ShapeDtypeStruct((slots, HD), jnp.bfloat16)
    return pl.pallas_call(
        lambda *refs: settle_kernel(len(parts), *refs),
        out_shape=(wide, wide, jax.ShapeDtypeStruct((edge_col.shape[0], slots), jnp.float32)),
        scratch_shapes=[pltpu.VMEM((slots, HD), jnp.bfloat16)],
        compiler_params=params(8),
        name="settle",
    )(edge_row, edge_col, high, low, *parts)


def hold_kernel(count, *refs):
    sems = refs[-1]
    copies = [
        pltpu.make_async_copy(refs[i], refs[count + 1 + i], sems.at[i]) for i in range(count)
    ]
    for copy in copies:
        copy.start()
    for copy in copies:
        copy.wait()


def hold(arrays, dep):
    count = len(arrays)
    return pl.pallas_call(
        lambda *refs: hold_kernel(count, *refs),
        out_shape=tuple(jax.ShapeDtypeStruct(a.shape, a.dtype) for a in arrays),
        in_specs=[pl.BlockSpec(memory_space=pl.ANY)] * (count + 1),
        out_specs=(pl.BlockSpec(memory_space=pltpu.VMEM),) * count,
        scratch_shapes=[pltpu.SemaphoreType.DMA((count,))],
        compiler_params=params(10),
        name="hold",
    )(*arrays, dep)


def rotated(values, turn):
    return values * turn[:, :HD] + pltpu.roll(values, HD // 2, 1) * turn[:, HD:]


def first_kernel(state_ref, gain_ref, wq_ref, wk_ref, wv_ref, *refs):
    query_ref, key_ref, value_ref, current_ref, my_gain_ref, inverse_ref = refs[-6:]
    share = current_ref.shape[1]
    mine = pl.ds(pl.multiple_of(lax.axis_index("head") * share, share), share)
    state = state_ref[...]
    gain = gain_ref[...]
    factor = lax.rsqrt(jnp.mean(state * state, axis=1, keepdims=True) + EPSILON)
    rows = (state * factor * gain).astype(jnp.bfloat16)
    query_ref[...] = jnp.dot(rows, wq_ref[...], preferred_element_type=jnp.float32)
    key_ref[...] = jnp.dot(rows, wk_ref[...], preferred_element_type=jnp.float32)
    value_ref[...] = jnp.dot(rows, wv_ref[...], preferred_element_type=jnp.float32)
    current_ref[...] = state_ref[:, mine]
    my_gain_ref[...] = gain_ref[:, mine]
    inverse_ref[...] = 1.0 / gain


def first(state, gain, weights, share, *deps):
    n, width = state.shape
    small = jax.ShapeDtypeStruct((n, HD), jnp.float32)
    whole = pl.BlockSpec(memory_space=pltpu.VMEM)
    return pl.pallas_call(
        first_kernel,
        out_shape=(small,) * 3
        + tuple(jax.ShapeDtypeStruct(d, jnp.float32) for d in ((n, share), (1, share), (1, width))),
        in_specs=[whole] * 5 + [pl.BlockSpec(memory_space=pl.ANY)] * len(deps),
        compiler_params=params(54),
        name="first",
    )(state, gain.reshape(1, -1), *weights, *deps)


def attend_kernel(step, *refs):
    f32, bf16 = jnp.float32, jnp.bfloat16
    turn_ref, key_ref, cache_ref, bias_ref, out_weight, *rest = refs
    turn = turn_ref[step]
    olds = [(rest[2 * i], rest[2 * i + 1]) for i in range(step)]
    rest = rest[2 * step :]
    if step:
        row_ref, inverse_ref, wq_ref, wk_ref, wv_ref, term_ref, new_key_ref, new_value_ref = rest
        blocks, n, share = row_ref.shape
        squares = jnp.zeros((n, share), f32)
        for i in range(blocks):
            plain = row_ref[i].astype(f32) * inverse_ref[:, i * share : (i + 1) * share]
            squares = squares + plain * plain
        mean = jnp.sum(squares, axis=1, keepdims=True) * (1.0 / (blocks * share))
        factor = lax.rsqrt(mean + EPSILON)
        rows = jnp.concatenate([row_ref[i] for i in range(blocks)], axis=1)
        query = jnp.dot(rows, wq_ref[...], preferred_element_type=f32) * factor
        key = jnp.dot(rows, wk_ref[...], preferred_element_type=f32) * factor
        value = jnp.dot(rows, wv_ref[...], preferred_element_type=f32) * factor
    else:
        query_ref, first_key, first_value, _, _, _, term_ref, new_key_ref, new_value_ref = rest
        query, key, value = query_ref[...], first_key[...], first_value[...]
    query = rotated(query, turn).astype(bf16)
    key = rotated(key, turn).astype(bf16)
    value = value.astype(bf16)
    new_key_ref[...] = key
    new_value_ref[...] = value
    scale = HD ** (-0.5)
    scores = lax.dot_general(
        query, key_ref[...], (((1,), (1,)), ((), ())), preferred_element_type=f32
    )
    scores = scores * scale + bias_ref[...]
    wide = query.astype(f32)
    pairs = [(k[...], v[...]) for k, v in olds] + [(key, value)]
    fresh = [jnp.sum(wide * k.astype(f32), axis=1, keepdims=True) * scale for k, _ in pairs]
    peak = jnp.max(scores, axis=1, keepdims=True)
    for f in fresh:
        peak = jnp.maximum(peak, f)
    cache_exp = jnp.exp(scores - peak)
    fresh_exp = [jnp.exp(f - peak) for f in fresh]
    total = jnp.sum(cache_exp, axis=1, keepdims=True)
    for f in fresh_exp:
        total = total + f
    weights = (cache_exp / total).astype(bf16)
    attended = jnp.dot(weights, cache_ref[...], preferred_element_type=f32)
    for f, (_, v) in zip(fresh_exp, pairs):
        attended = attended + (f / total).astype(bf16).astype(f32) * v.astype(f32)
    attended = attended.astype(bf16)
    blocks, _, share = term_ref.shape
    wide_share = 4 * share
    for j in range(blocks // 4):
        term = jnp.dot(
            attended, out_weight[:, j * wide_share : (j + 1) * wide_share], preferred_element_type=f32
        ).astype(bf16)
        for i in range(4):
            term_ref[4 * j + i] = term[:, i * share : (i + 1) * share]


def attend(step, blocks, turns, keys, cache, bias, w_out, olds, extra):
    n = bias.shape[0]
    share = w_out.shape[1] // blocks
    flat = [x for pair in olds for x in pair]
    small = jax.ShapeDtypeStruct((n, HD), jnp.bfloat16)
    return pl.pallas_call(
        lambda *refs: attend_kernel(step, *refs),
        out_shape=(jax.ShapeDtypeStruct((blocks, n, share), jnp.bfloat16), small, small),
        compiler_params=params(10),
        name="attend",
    )(turns, keys, cache, bias, w_out, *flat, *extra)


def spread_kernel(last, part_ref, current_ref, gain_ref, *refs):
    next_ref, *out = refs[-1:] if last else refs[-2:]
    total = current_ref[...]
    for i in range(part_ref.shape[0]):
        total = total + part_ref[i].astype(jnp.float32)
    next_ref[...] = total
    if not last:
        piece = (total * gain_ref[...]).astype(jnp.bfloat16)
        for i in range(part_ref.shape[0]):
            out[0][i] = piece


def spread(last, parts, current, gain, held):
    shapes = [jax.ShapeDtypeStruct(current.shape, jnp.float32)]
    if not last:
        shapes.append(jax.ShapeDtypeStruct(parts.shape, jnp.bfloat16))
    return pl.pallas_call(
        lambda *refs: spread_kernel(last, *refs),
        out_shape=tuple(shapes),
        compiler_params=params(4),
        name="spread",
    )(parts, current, gain, *held)


def per_device(
    prefill_rows, row_group, lengths, decode_state, norm_gain, w_query, w_key, w_value, w_out
):
    groups = lax.axis_size("grp")
    heads = lax.axis_size("head")
    rows_local, width = prefill_rows.shape
    cap = (rows_local // groups + rows_local // groups // 2) * heads
    requests = lengths.shape[1]
    my_group = lax.axis_index("grp")
    my_head = lax.axis_index("head")
    share = width // heads
    f32, bf16 = jnp.float32, jnp.bfloat16

    with jax.named_scope("rows"):
        start = norm_rows(row_group, prefill_rows, norm_gain)
        f2 = send(start, lane(2, 0))
        f1 = send(start, lane(1, 0))
        f3 = send(start, lane(3, 0))
        both_weights = [w_key, w_value, send(w_key, CORE), send(w_value, CORE)]
        l0, l1 = lines(start, f1, f2, f3, both_weights[2][:16])
        s11 = send(l1, lane(0, 1))
        s30 = send(l0, lane(0, 3))
        s10 = send(l0, lane(0, 1))
        s31 = send(l1, lane(0, 3))
        s20 = send(s30, lane(0, 1))
        s21 = send(s11, lane(0, 3))
    with jax.named_scope("places"):
        group_ids = jnp.arange(groups, dtype=jnp.int32)
        late_lengths = after(lengths, f1)
        my_lengths = jnp.sum(
            jnp.where((group_ids == my_group)[:, None], late_lengths, 0), axis=0
        )
        request = jnp.arange(requests, dtype=jnp.int32)
        my_ends = jnp.sum(jnp.where(request[None, :] <= request[:, None], my_lengths[None, :], 0), axis=1)
        my_starts = my_ends - my_lengths
        edges = jnp.stack([my_starts, my_ends]).astype(f32)
        edge_row = jnp.pad(edges, ((0, 0), (0, HD - requests)), constant_values=1e9)
        edge_col = jnp.repeat(edges, HD, axis=0).T.reshape(requests, 2 * HD)
        spots = jnp.arange(HD, dtype=jnp.int32) + 0 * my_lengths[0]
        table = jnp.concatenate(angles_of(spots), axis=1)
        table_high = table.astype(bf16)
        table_low = (table - table_high.astype(f32)).astype(bf16)

    with jax.named_scope("project"):
        own_a, other_a, ids_a, wide_weights = project([l0, s10, s30], [l1, s11, s31], both_weights)
        own_b, other_b, ids_b = project_last(s20, s21, wide_weights)
        leaving = finish(
            groups, cap, own_a, own_b, ids_a, ids_b, send(other_a, CORE), send(other_b, CORE)
        )
        arrived = [leaving[0]]
        for hop in range(1, groups):
            pairs = [(g, (g + hop) % groups) for g in range(groups)]
            arrived.append(lax.ppermute(leaving[hop], "grp", pairs))
        (w_out,) = hold([w_out], leaving[0])
        cache_keys, cache_values, bias = settle(edge_row, edge_col, table_high, table_low, arrived)

    with jax.named_scope("first"):
        extra = first(decode_state, norm_gain, (w_query, w_key, w_value), share)
        current, my_gain, inverse = extra[3:]
        at_step = my_lengths[None, :] + jnp.arange(STEPS, dtype=jnp.int32)[:, None]
        turns = jnp.concatenate(angles_of(at_step), axis=-1)
    held = [w_query, w_key, w_value, w_out]
    olds = []
    for step in range(STEPS):
        term, new_key, new_value = attend(
            step, heads, turns, cache_keys, cache_values, bias, w_out, olds, extra
        )
        olds.append((new_key, new_value))
        parts = lax.all_to_all(term, "head", split_axis=0, concat_axis=0, tiled=True)
        last = step + 1 == STEPS
        current, *spreading = spread(last, parts, current, my_gain, [] if last else held)
        if not last:
            rows = lax.all_to_all(spreading[0], "head", split_axis=0, concat_axis=0, tiled=True)
            extra = [rows, inverse, w_query, w_key, w_value]
    return current


def solution(mesh):
    return jax.shard_map(
        per_device,
        mesh=mesh,
        in_specs=(
            P(("grp", "head"), None),
            P(("grp", "head")),
            P(),
            P("grp", None),
            P(),
            P(None, "head"),
            P(None, "head"),
            P(None, "head"),
            P("head", None),
        ),
        out_specs=P("grp", "head"),
        check_vma=False,
    )
```

```python
import math

import jax
import jax.numpy as jnp
from jax import lax
from jax.experimental import pallas as pl
from jax.experimental.pallas import tpu as pltpu
from jax.sharding import PartitionSpec as P

HD = 128
STEPS = 4
EPSILON = 1e-05
ROPE_BASE = 10000.0
MASKED = -1e30


def normed(values, norm_gain):
    widened = values.astype(jnp.float32)
    factor = lax.rsqrt(jnp.mean(widened * widened, axis=-1, keepdims=True) + EPSILON)
    return (widened * factor * norm_gain).astype(jnp.bfloat16)


def angles_of(positions):
    half = HD // 2
    frequency = jnp.exp(
        jnp.arange(half, dtype=jnp.float32) * (-2.0 * math.log(ROPE_BASE) / HD)
    )
    angles = positions.astype(jnp.float32)[..., None] * frequency
    cosine = jnp.cos(angles)
    sine = jnp.sin(angles)
    return (
        jnp.concatenate([cosine, cosine], axis=-1),
        jnp.concatenate([-sine, sine], axis=-1),
    )


def turned(values, cosine, sine):
    half = HD // 2
    swapped = jnp.concatenate([values[..., half:], values[..., :half]], axis=-1)
    return values * cosine + swapped * sine


NX = 4
NY = 4
EMPTY = 1e30
HOPS = (0, 4, 3, 5, 2, 6, 1, 7)


def head_pairs(move):
    pairs = []
    for y in range(NY):
        for x in range(NX):
            for c in range(2):
                ty, tx, tc = move(y, x, c)
                pairs.append(((y * NX + x) * 2 + c, (ty * NX + tx) * 2 + tc))
    return pairs


def lane(first, second):
    return head_pairs(
        lambda y, x, c: (y ^ second, x ^ first, c) if c == 0 else (y ^ first, x ^ second, c)
    )


CORE = head_pairs(lambda y, x, c: (y, x, c ^ 1))


def send(values, pairs):
    return lax.ppermute(values, "head", pairs)


def after(values, piece):
    return values + (piece[0, 0].astype(jnp.float32) * 0.0).astype(values.dtype)


def params(mib):
    return pltpu.CompilerParams(vmem_limit_bytes=mib * 1024 * 1024)


def norm_kernel(group_ref, rows_ref, gain_ref, out_ref):
    n, half = rows_ref.shape[0], rows_ref.shape[1] // 2
    rows = rows_ref[...].astype(jnp.float32)
    factor = lax.rsqrt(jnp.mean(rows * rows, axis=1, keepdims=True) + EPSILON)
    result = (rows * factor * gain_ref[...]).astype(jnp.bfloat16)
    row = lax.broadcasted_iota(jnp.int32, (n, HD), 0)
    ids = jnp.zeros((n, HD), jnp.int32)
    for j in range(n):
        ids = jnp.where(row == j, group_ref[j], ids)
    ids = ids.astype(jnp.float32).astype(jnp.bfloat16)
    for side in range(2):
        out_ref[side * n : (side + 1) * n, :half] = result[:, side * half : (side + 1) * half]
        out_ref[side * n : (side + 1) * n, half:] = ids


def norm_rows(groups, rows, gain):
    n, width = rows.shape
    whole = pl.BlockSpec(memory_space=pltpu.VMEM)
    return pl.pallas_call(
        norm_kernel,
        out_shape=jax.ShapeDtypeStruct((2 * n, width // 2 + HD), jnp.bfloat16),
        in_specs=[pl.BlockSpec(memory_space=pltpu.SMEM), whole, whole],
        compiler_params=params(56),
        name="norm_rows",
    )(groups, rows, gain.reshape(1, -1))


def lines_kernel(start, f1, f2, f3, *refs):
    l0_ref, l1_ref = refs[-2:]
    n = start.shape[0] // 2
    for i, f in enumerate((start, f1, f2, f3)):
        l0_ref[i * n : (i + 1) * n, :] = f[:n, :]
        l1_ref[i * n : (i + 1) * n, :] = f[n:, :]


def lines(start, f1, f2, f3, *deps):
    shape = jax.ShapeDtypeStruct((NX * start.shape[0] // 2, start.shape[1]), start.dtype)
    return pl.pallas_call(
        lines_kernel, out_shape=(shape, shape), compiler_params=params(6), name="lines"
    )(start, f1, f2, f3, *deps)


CHUNKS = 8


def project_kernel(count, *refs):
    pieces = refs[: 2 * count]
    weights = refs[2 * count : 2 * count + 4]
    own_ref, other_ref, ids_ref, w, x, total, piece_sems, weight_sems = refs[2 * count + 4 :]
    size = pieces[0].shape[0]
    rows = count * size
    depth = w.shape[0] // CHUNKS
    half = w.shape[0] // 2
    loads = []
    for k in range(CHUNKS):
        here = slice(k * depth, (k + 1) * depth)
        loads.append(
            [
                pltpu.make_async_copy(
                    weight.at[here], w.at[here, i * HD : (i + 1) * HD], weight_sems.at[k, i]
                )
                for i, weight in enumerate(weights)
            ]
        )
    fetches = [
        pltpu.make_async_copy(p, x.at[i * size : (i + 1) * size], piece_sems.at[i])
        for i, p in enumerate(pieces)
    ]
    for load in loads[0]:
        load.start()
    for fetch in fetches:
        fetch.start()
    for k in range(1, CHUNKS):
        for load in loads[k]:
            load.start()
    for fetch in fetches[:count]:
        fetch.wait()
    for k in range(CHUNKS):
        if k == CHUNKS // 2:
            for fetch in fetches[count:]:
                fetch.wait()
        for load in loads[k]:
            load.wait()
        here = slice(k * depth, (k + 1) * depth)
        side = 2 * k // CHUNKS
        columns = slice(k * depth - side * half, (k + 1) * depth - side * half)
        term = jnp.dot(
            x[side * rows : (side + 1) * rows, columns], w[here, :], preferred_element_type=jnp.float32
        )
        if k == 0:
            total[...] = term
        else:
            total[...] += term
    ids_ref[...] = x[:rows, half:]
    own_ref[...] = total[:, : 2 * HD].astype(jnp.bfloat16)
    other_ref[:, : 2 * HD] = total[:, 2 * HD :].astype(jnp.bfloat16)
    other_ref[:, 2 * HD :] = x[:rows, half:]


def projected_shapes(rows):
    return (
        jax.ShapeDtypeStruct((rows, 2 * HD), jnp.bfloat16),
        jax.ShapeDtypeStruct((rows, 3 * HD), jnp.bfloat16),
        jax.ShapeDtypeStruct((rows, HD), jnp.bfloat16),
    )


def project(lows, highs, weights):
    count = len(lows)
    size, wide = lows[0].shape
    rows, width = count * size, 2 * (wide - HD)
    return pl.pallas_call(
        lambda *refs: project_kernel(count, *refs),
        out_shape=projected_shapes(rows)
        + (jax.ShapeDtypeStruct((width, 4 * HD), jnp.bfloat16),),
        in_specs=[pl.BlockSpec(memory_space=pl.ANY)] * (2 * count + 4),
        scratch_shapes=[
            pltpu.VMEM((2 * rows, wide), jnp.bfloat16),
            pltpu.VMEM((rows, 4 * HD), jnp.float32),
            pltpu.SemaphoreType.DMA((2 * count,)),
            pltpu.SemaphoreType.DMA((CHUNKS, 4)),
        ],
        compiler_params=params(18),
        name="project",
    )(*lows, *highs, *weights)


def project_low_kernel(low, w, total_ref):
    half = w.shape[0] // 2
    total_ref[...] = jnp.dot(low[:, :half], w[:half, :], preferred_element_type=jnp.float32)


def project_high_kernel(high, w, low_ref, own_ref, other_ref, ids_ref):
    half = w.shape[0] // 2
    total = low_ref[...]
    total = total + jnp.dot(high[:, :half], w[half:, :], preferred_element_type=jnp.float32)
    ids_ref[...] = high[:, half:]
    own_ref[...] = total[:, : 2 * HD].astype(jnp.bfloat16)
    other_ref[:, : 2 * HD] = total[:, 2 * HD :].astype(jnp.bfloat16)
    other_ref[:, 2 * HD :] = high[:, half:]


def project_last(low, high, weights):
    rows = low.shape[0]
    total = pl.pallas_call(
        project_low_kernel,
        out_shape=jax.ShapeDtypeStruct((rows, weights.shape[1]), jnp.float32),
        compiler_params=params(10),
        name="project_low",
    )(low, weights)
    return pl.pallas_call(
        project_high_kernel,
        out_shape=projected_shapes(rows),
        compiler_params=params(10),
        name="project_high",
    )(high, weights, total)


def origin(shape, dim, head):
    at = lax.broadcasted_iota(jnp.int32, shape, dim)
    turn, d_first, row = (at >> 6) & 3, (at >> 4) & 3, at & 15
    d_second = turn ^ (turn >> 1)
    c = (head & 1) ^ (at >> 8)
    dy = jnp.where(c == 0, d_second, d_first)
    dx = jnp.where(c == 0, d_first, d_second)
    y, x = (head >> 3) ^ dy, ((head >> 1) & 3) ^ dx
    return (((y * NX + x) * 2 + c) << 4) + row


def finish_kernel(groups, cap, own_a, own_b, ids_a, ids_b, their_a, their_b, *refs):
    outs, packed = refs[:groups], refs[groups]
    total = packed.shape[0]
    early, half = own_a.shape[0], total // 2
    head = lax.axis_index("head")
    group = lax.axis_index("grp").astype(jnp.float32)
    packed[:early, :] = own_a[...]
    packed[early:half, :] = own_b[...]
    packed[half : half + early, :] = their_a[:, : 2 * HD]
    packed[half + early :, :] = their_b[:, : 2 * HD]
    ids = [ids_a[...], ids_b[...], their_a[:, 2 * HD :], their_b[:, 2 * HD :]]
    hop = jnp.concatenate(ids, axis=0).astype(jnp.float32) - group
    hop = jnp.where(hop < 0.0, hop + groups, hop)
    lanes = lax.broadcasted_iota(jnp.int32, (1, HD), 1).astype(jnp.float32)
    match = jnp.where(hop == lanes, 1.0, 0.0)
    earlier = origin((1, total), 1, head) < origin((total, 1), 0, head)
    ranks = jnp.dot(
        jnp.where(earlier, 1.0, 0.0).astype(jnp.bfloat16),
        match.astype(jnp.bfloat16),
        preferred_element_type=jnp.float32,
    )
    order = jnp.sum(ranks * match, axis=1, keepdims=True)
    slot = hop[:, :1] * cap + order
    slots = lax.broadcasted_iota(jnp.int32, (1, groups * cap), 1).astype(jnp.float32)
    pick = jnp.where(slots == slot, 1.0, 0.0).astype(jnp.bfloat16)
    routed = lax.dot_general(
        pick, packed[...], (((0,), (0,)), ((), ())), preferred_element_type=jnp.float32
    )
    counts = jnp.sum(match, axis=0, keepdims=True)
    step = lax.broadcasted_iota(jnp.int32, (cap, 1), 0).astype(jnp.float32)
    for g in range(groups):
        rows = slice(g * cap, (g + 1) * cap)
        filled = step < counts[:, g : g + 1]
        outs[g][:, :HD] = jnp.where(filled, routed[rows, :HD], EMPTY).astype(jnp.bfloat16)
        outs[g][:, HD:] = routed[rows, HD:].astype(jnp.bfloat16)


def finish(groups, cap, own_a, own_b, ids_a, ids_b, their_a, their_b):
    shape = jax.ShapeDtypeStruct((cap, 2 * HD), jnp.bfloat16)
    rows = 2 * (own_a.shape[0] + own_b.shape[0])
    return pl.pallas_call(
        lambda *refs: finish_kernel(groups, cap, *refs),
        out_shape=(shape,) * groups,
        scratch_shapes=[pltpu.VMEM((rows, 2 * HD), jnp.bfloat16)],
        compiler_params=params(12),
        name="finish",
    )(own_a, own_b, ids_a, ids_b, their_a, their_b)


def settle_kernel(groups, edge_row, edge_col, high_ref, low_ref, *refs):
    parts = [refs[HOPS.index(g)] for g in range(groups)]
    key_ref, value_ref, bias_ref, hot = refs[groups:]
    cap = parts[0].shape[0]
    slots = groups * cap
    me = lax.axis_index("grp")
    sources = [lax.rem(me + groups - g, groups) for g in range(groups)]
    starts, ends = edge_row[0:1, :], edge_row[1:2, :]
    lanes = lax.broadcasted_iota(jnp.int32, (1, HD), 1).astype(jnp.float32)
    step = lax.broadcasted_iota(jnp.int32, (cap, 1), 0).astype(jnp.float32)
    across = lax.broadcasted_iota(jnp.int32, (1, slots), 1).astype(jnp.float32)
    counts = []
    for part in parts:
        full = part[:, :HD].astype(jnp.float32) < EMPTY / 2
        counts.append(jnp.sum(jnp.where(full, 1.0, 0.0), axis=0, keepdims=True)[:, :1])
    cells = across
    open_slots = across < 0.0
    for g in range(groups):
        base = jnp.zeros((1, 1), jnp.float32)
        for other in range(groups):
            if other != g:
                before = jnp.where(sources[other] < sources[g], 1.0, 0.0)
                base = base + counts[other] * before
        rows = slice(g * cap, (g + 1) * cap)
        cell = base + step
        inside = (cell >= starts) & (cell < ends)
        place = cell - jnp.sum(jnp.where(inside, starts, 0.0), axis=1, keepdims=True)
        hot[rows, :] = jnp.where(lanes == place, 1.0, 0.0).astype(jnp.bfloat16)
        here = (across >= g * cap) & (across < (g + 1) * cap)
        cells = jnp.where(here, across - g * cap + base, cells)
        open_slots = open_slots | (here & (across - g * cap < counts[g]))
        value_ref[rows, :] = parts[g][:, HD:]
    low_edge, high_edge = edge_col[:, 0:1], edge_col[:, HD : HD + 1]
    mine = (cells >= low_edge) & (cells < high_edge) & open_slots
    bias_ref[...] = jnp.where(mine, 0.0, MASKED)
    trig = jnp.dot(hot[...], high_ref[...], preferred_element_type=jnp.float32)
    trig = trig + jnp.dot(hot[...], low_ref[...], preferred_element_type=jnp.float32)
    for g in range(groups):
        rows = slice(g * cap, (g + 1) * cap)
        keys = parts[g][:, :HD].astype(jnp.float32)
        keys = jnp.where(keys < EMPTY / 2, keys, 0.0)
        turned_keys = keys * trig[rows, :HD] + pltpu.roll(keys, HD // 2, 1) * trig[rows, HD:]
        key_ref[rows, :] = turned_keys.astype(jnp.bfloat16)


def settle(edge_row, edge_col, high, low, parts):
    slots = len(parts) * parts[0].shape[0]
    wide = jax.ShapeDtypeStruct((slots, HD), jnp.bfloat16)
    return pl.pallas_call(
        lambda *refs: settle_kernel(len(parts), *refs),
        out_shape=(wide, wide, jax.ShapeDtypeStruct((edge_col.shape[0], slots), jnp.float32)),
        scratch_shapes=[pltpu.VMEM((slots, HD), jnp.bfloat16)],
        compiler_params=params(8),
        name="settle",
    )(edge_row, edge_col, high, low, *parts)


def hold_kernel(count, *refs):
    sems = refs[-1]
    copies = [
        pltpu.make_async_copy(refs[i], refs[count + 1 + i], sems.at[i]) for i in range(count)
    ]
    for copy in copies:
        copy.start()
    for copy in copies:
        copy.wait()


def hold(arrays, dep):
    count = len(arrays)
    return pl.pallas_call(
        lambda *refs: hold_kernel(count, *refs),
        out_shape=tuple(jax.ShapeDtypeStruct(a.shape, a.dtype) for a in arrays),
        in_specs=[pl.BlockSpec(memory_space=pl.ANY)] * (count + 1),
        out_specs=(pl.BlockSpec(memory_space=pltpu.VMEM),) * count,
        scratch_shapes=[pltpu.SemaphoreType.DMA((count,))],
        compiler_params=params(10),
        name="hold",
    )(*arrays, dep)


def rotated(values, turn):
    return values * turn[:, :HD] + pltpu.roll(values, HD // 2, 1) * turn[:, HD:]


def first_kernel(state_ref, gain_ref, wq_ref, wk_ref, wv_ref, *refs):
    query_ref, key_ref, value_ref, current_ref, my_gain_ref, inverse_ref = refs[-6:]
    share = current_ref.shape[1]
    mine = pl.ds(pl.multiple_of(lax.axis_index("head") * share, share), share)
    state = state_ref[...]
    gain = gain_ref[...]
    factor = lax.rsqrt(jnp.mean(state * state, axis=1, keepdims=True) + EPSILON)
    rows = (state * factor * gain).astype(jnp.bfloat16)
    query_ref[...] = jnp.dot(rows, wq_ref[...], preferred_element_type=jnp.float32)
    key_ref[...] = jnp.dot(rows, wk_ref[...], preferred_element_type=jnp.float32)
    value_ref[...] = jnp.dot(rows, wv_ref[...], preferred_element_type=jnp.float32)
    current_ref[...] = state_ref[:, mine]
    my_gain_ref[...] = gain_ref[:, mine]
    inverse_ref[...] = 1.0 / gain


def first(state, gain, weights, share, *deps):
    n, width = state.shape
    small = jax.ShapeDtypeStruct((n, HD), jnp.float32)
    whole = pl.BlockSpec(memory_space=pltpu.VMEM)
    return pl.pallas_call(
        first_kernel,
        out_shape=(small,) * 3
        + tuple(jax.ShapeDtypeStruct(d, jnp.float32) for d in ((n, share), (1, share), (1, width))),
        in_specs=[whole] * 5 + [pl.BlockSpec(memory_space=pl.ANY)] * len(deps),
        compiler_params=params(54),
        name="first",
    )(state, gain.reshape(1, -1), *weights, *deps)


def attend_kernel(step, *refs):
    f32, bf16 = jnp.float32, jnp.bfloat16
    turn_ref, key_ref, cache_ref, bias_ref, out_weight, *rest = refs
    turn = turn_ref[step]
    olds = [(rest[2 * i], rest[2 * i + 1]) for i in range(step)]
    rest = rest[2 * step :]
    if step:
        row_ref, inverse_ref, wq_ref, wk_ref, wv_ref, term_ref, new_key_ref, new_value_ref = rest
        blocks, n, share = row_ref.shape
        squares = jnp.zeros((n, share), f32)
        for i in range(blocks):
            plain = row_ref[i].astype(f32) * inverse_ref[:, i * share : (i + 1) * share]
            squares = squares + plain * plain
        mean = jnp.sum(squares, axis=1, keepdims=True) * (1.0 / (blocks * share))
        factor = lax.rsqrt(mean + EPSILON)
        rows = jnp.concatenate([row_ref[i] for i in range(blocks)], axis=1)
        query = jnp.dot(rows, wq_ref[...], preferred_element_type=f32) * factor
        key = jnp.dot(rows, wk_ref[...], preferred_element_type=f32) * factor
        value = jnp.dot(rows, wv_ref[...], preferred_element_type=f32) * factor
    else:
        query_ref, first_key, first_value, _, _, _, term_ref, new_key_ref, new_value_ref = rest
        query, key, value = query_ref[...], first_key[...], first_value[...]
    query = rotated(query, turn).astype(bf16)
    key = rotated(key, turn).astype(bf16)
    value = value.astype(bf16)
    new_key_ref[...] = key
    new_value_ref[...] = value
    scale = HD ** (-0.5)
    scores = lax.dot_general(
        query, key_ref[...], (((1,), (1,)), ((), ())), preferred_element_type=f32
    )
    scores = scores * scale + bias_ref[...]
    wide = query.astype(f32)
    pairs = [(k[...], v[...]) for k, v in olds] + [(key, value)]
    fresh = [jnp.sum(wide * k.astype(f32), axis=1, keepdims=True) * scale for k, _ in pairs]
    peak = jnp.max(scores, axis=1, keepdims=True)
    for f in fresh:
        peak = jnp.maximum(peak, f)
    cache_exp = jnp.exp(scores - peak)
    fresh_exp = [jnp.exp(f - peak) for f in fresh]
    total = jnp.sum(cache_exp, axis=1, keepdims=True)
    for f in fresh_exp:
        total = total + f
    weights = (cache_exp / total).astype(bf16)
    attended = jnp.dot(weights, cache_ref[...], preferred_element_type=f32)
    for f, (_, v) in zip(fresh_exp, pairs):
        attended = attended + (f / total).astype(bf16).astype(f32) * v.astype(f32)
    attended = attended.astype(bf16)
    blocks, _, share = term_ref.shape
    wide_share = 4 * share
    for j in range(blocks // 4):
        term = jnp.dot(
            attended, out_weight[:, j * wide_share : (j + 1) * wide_share], preferred_element_type=f32
        ).astype(bf16)
        for i in range(4):
            term_ref[4 * j + i] = term[:, i * share : (i + 1) * share]


def attend(step, blocks, turns, keys, cache, bias, w_out, olds, extra):
    n = bias.shape[0]
    share = w_out.shape[1] // blocks
    flat = [x for pair in olds for x in pair]
    small = jax.ShapeDtypeStruct((n, HD), jnp.bfloat16)
    return pl.pallas_call(
        lambda *refs: attend_kernel(step, *refs),
        out_shape=(jax.ShapeDtypeStruct((blocks, n, share), jnp.bfloat16), small, small),
        compiler_params=params(10),
        name="attend",
    )(turns, keys, cache, bias, w_out, *flat, *extra)


def spread_kernel(last, part_ref, current_ref, gain_ref, *refs):
    next_ref, *out = refs[-1:] if last else refs[-2:]
    total = current_ref[...]
    for i in range(part_ref.shape[0]):
        total = total + part_ref[i].astype(jnp.float32)
    next_ref[...] = total
    if not last:
        piece = (total * gain_ref[...]).astype(jnp.bfloat16)
        for i in range(part_ref.shape[0]):
            out[0][i] = piece


def spread(last, parts, current, gain, held):
    shapes = [jax.ShapeDtypeStruct(current.shape, jnp.float32)]
    if not last:
        shapes.append(jax.ShapeDtypeStruct(parts.shape, jnp.bfloat16))
    return pl.pallas_call(
        lambda *refs: spread_kernel(last, *refs),
        out_shape=tuple(shapes),
        compiler_params=params(4),
        name="spread",
    )(parts, current, gain, *held)


def per_device(
    prefill_rows, row_group, lengths, decode_state, norm_gain, w_query, w_key, w_value, w_out
):
    groups = lax.axis_size("grp")
    heads = lax.axis_size("head")
    rows_local, width = prefill_rows.shape
    cap = (rows_local // groups + rows_local // groups // 2) * heads
    requests = lengths.shape[1]
    my_group = lax.axis_index("grp")
    my_head = lax.axis_index("head")
    share = width // heads
    f32, bf16 = jnp.float32, jnp.bfloat16

    with jax.named_scope("rows"):
        start = norm_rows(row_group, prefill_rows, norm_gain)
        f2 = send(start, lane(2, 0))
        f1 = send(start, lane(1, 0))
        f3 = send(start, lane(3, 0))
        both_weights = [w_key, w_value, send(w_key, CORE), send(w_value, CORE)]
        l0, l1 = lines(start, f1, f2, f3, both_weights[2][:16])
        s11 = send(l1, lane(0, 1))
        s30 = send(l0, lane(0, 3))
        s10 = send(l0, lane(0, 1))
        s31 = send(l1, lane(0, 3))
        s20 = send(s30, lane(0, 1))
        s21 = send(s11, lane(0, 3))
    with jax.named_scope("places"):
        group_ids = jnp.arange(groups, dtype=jnp.int32)
        late_lengths = after(lengths, f1)
        my_lengths = jnp.sum(
            jnp.where((group_ids == my_group)[:, None], late_lengths, 0), axis=0
        )
        request = jnp.arange(requests, dtype=jnp.int32)
        my_ends = jnp.sum(jnp.where(request[None, :] <= request[:, None], my_lengths[None, :], 0), axis=1)
        my_starts = my_ends - my_lengths
        edges = jnp.stack([my_starts, my_ends]).astype(f32)
        edge_row = jnp.pad(edges, ((0, 0), (0, HD - requests)), constant_values=1e9)
        edge_col = jnp.repeat(edges, HD, axis=0).T.reshape(requests, 2 * HD)
        spots = jnp.arange(HD, dtype=jnp.int32) + 0 * my_lengths[0]
        table = jnp.concatenate(angles_of(spots), axis=1)
        table_high = table.astype(bf16)
        table_low = (table - table_high.astype(f32)).astype(bf16)

    with jax.named_scope("project"):
        own_a, other_a, ids_a, wide_weights = project([l0, s10, s30], [l1, s11, s31], both_weights)
        own_b, other_b, ids_b = project_last(s20, s21, wide_weights)
        leaving = finish(
            groups, cap, own_a, own_b, ids_a, ids_b, send(other_a, CORE), send(other_b, CORE)
        )
        arrived = [leaving[0]]
        for hop in HOPS[1:]:
            pairs = [(g, (g + hop) % groups) for g in range(groups)]
            arrived.append(lax.ppermute(leaving[hop], "grp", pairs))
        (w_out,) = hold([w_out], leaving[0])
        cache_keys, cache_values, bias = settle(edge_row, edge_col, table_high, table_low, arrived)

    with jax.named_scope("first"):
        extra = first(decode_state, norm_gain, (w_query, w_key, w_value), share)
        current, my_gain, inverse = extra[3:]
        at_step = my_lengths[None, :] + jnp.arange(STEPS, dtype=jnp.int32)[:, None]
        turns = jnp.concatenate(angles_of(at_step), axis=-1)
    held = [w_query, w_key, w_value, w_out]
    olds = []
    for step in range(STEPS):
        term, new_key, new_value = attend(
            step, heads, turns, cache_keys, cache_values, bias, w_out, olds, extra
        )
        olds.append((new_key, new_value))
        parts = lax.all_to_all(term, "head", split_axis=0, concat_axis=0, tiled=True)
        last = step + 1 == STEPS
        current, *spreading = spread(last, parts, current, my_gain, [] if last else held)
        if not last:
            rows = lax.all_to_all(spreading[0], "head", split_axis=0, concat_axis=0, tiled=True)
            extra = [rows, inverse, w_query, w_key, w_value]
    return current


def solution(mesh):
    return jax.shard_map(
        per_device,
        mesh=mesh,
        in_specs=(
            P(("grp", "head"), None),
            P(("grp", "head")),
            P(),
            P("grp", None),
            P(),
            P(None, "head"),
            P(None, "head"),
            P(None, "head"),
            P("head", None),
        ),
        out_specs=P("grp", "head"),
        check_vma=False,
    )
```

```python
import math

import jax
import jax.numpy as jnp
from jax import lax
from jax.experimental import pallas as pl
from jax.experimental.pallas import tpu as pltpu
from jax.sharding import PartitionSpec as P

HD = 128
STEPS = 4
EPSILON = 1e-05
ROPE_BASE = 10000.0
MASKED = -1e30


def normed(values, norm_gain):
    widened = values.astype(jnp.float32)
    factor = lax.rsqrt(jnp.mean(widened * widened, axis=-1, keepdims=True) + EPSILON)
    return (widened * factor * norm_gain).astype(jnp.bfloat16)


def angles_of(positions):
    half = HD // 2
    frequency = jnp.exp(
        jnp.arange(half, dtype=jnp.float32) * (-2.0 * math.log(ROPE_BASE) / HD)
    )
    angles = positions.astype(jnp.float32)[..., None] * frequency
    cosine = jnp.cos(angles)
    sine = jnp.sin(angles)
    return (
        jnp.concatenate([cosine, cosine], axis=-1),
        jnp.concatenate([-sine, sine], axis=-1),
    )


def turned(values, cosine, sine):
    half = HD // 2
    swapped = jnp.concatenate([values[..., half:], values[..., :half]], axis=-1)
    return values * cosine + swapped * sine


NX = 4
NY = 4
EMPTY = 1e30
HOPS = (0, 4, 3, 5, 2, 6, 1, 7)


def head_pairs(move):
    pairs = []
    for y in range(NY):
        for x in range(NX):
            for c in range(2):
                ty, tx, tc = move(y, x, c)
                pairs.append(((y * NX + x) * 2 + c, (ty * NX + tx) * 2 + tc))
    return pairs


def lane(first, second):
    return head_pairs(
        lambda y, x, c: (y ^ second, x ^ first, c) if c == 0 else (y ^ first, x ^ second, c)
    )


CORE = head_pairs(lambda y, x, c: (y, x, c ^ 1))


def send(values, pairs):
    return lax.ppermute(values, "head", pairs)


def after(values, piece):
    return values + (piece[0, 0].astype(jnp.float32) * 0.0).astype(values.dtype)


def params(mib):
    return pltpu.CompilerParams(vmem_limit_bytes=mib * 1024 * 1024)


def norm_kernel(group_ref, rows_ref, gain_ref, out_ref):
    n, half = rows_ref.shape[0], rows_ref.shape[1] // 2
    rows = rows_ref[...].astype(jnp.float32)
    factor = lax.rsqrt(jnp.mean(rows * rows, axis=1, keepdims=True) + EPSILON)
    result = (rows * factor * gain_ref[...]).astype(jnp.bfloat16)
    row = lax.broadcasted_iota(jnp.int32, (n, HD), 0)
    ids = jnp.zeros((n, HD), jnp.int32)
    for j in range(n):
        ids = jnp.where(row == j, group_ref[j], ids)
    ids = ids.astype(jnp.float32).astype(jnp.bfloat16)
    for side in range(2):
        out_ref[side * n : (side + 1) * n, :half] = result[:, side * half : (side + 1) * half]
        out_ref[side * n : (side + 1) * n, half:] = ids


def norm_rows(groups, rows, gain):
    n, width = rows.shape
    whole = pl.BlockSpec(memory_space=pltpu.VMEM)
    return pl.pallas_call(
        norm_kernel,
        out_shape=jax.ShapeDtypeStruct((2 * n, width // 2 + HD), jnp.bfloat16),
        in_specs=[pl.BlockSpec(memory_space=pltpu.SMEM), whole, whole],
        compiler_params=params(56),
        name="norm_rows",
    )(groups, rows, gain.reshape(1, -1))


def lines_kernel(start, f1, f2, f3, *refs):
    l0_ref, l1_ref = refs[-2:]
    n = start.shape[0] // 2
    for i, f in enumerate((start, f1, f2, f3)):
        l0_ref[i * n : (i + 1) * n, :] = f[:n, :]
        l1_ref[i * n : (i + 1) * n, :] = f[n:, :]


def lines(start, f1, f2, f3, *deps):
    shape = jax.ShapeDtypeStruct((NX * start.shape[0] // 2, start.shape[1]), start.dtype)
    return pl.pallas_call(
        lines_kernel, out_shape=(shape, shape), compiler_params=params(6), name="lines"
    )(start, f1, f2, f3, *deps)


CHUNKS = 8


def project_kernel(count, *refs):
    pieces = refs[: 2 * count]
    weights = refs[2 * count : 2 * count + 4]
    own_ref, other_ref, ids_ref, w, x, total, piece_sems, weight_sems = refs[2 * count + 4 :]
    size = pieces[0].shape[0]
    rows = count * size
    depth = w.shape[0] // CHUNKS
    half = w.shape[0] // 2
    loads = []
    for k in range(CHUNKS):
        here = slice(k * depth, (k + 1) * depth)
        loads.append(
            [
                pltpu.make_async_copy(
                    weight.at[here], w.at[here, i * HD : (i + 1) * HD], weight_sems.at[k, i]
                )
                for i, weight in enumerate(weights)
            ]
        )
    fetches = [
        pltpu.make_async_copy(p, x.at[i * size : (i + 1) * size], piece_sems.at[i])
        for i, p in enumerate(pieces)
    ]
    for load in loads[0]:
        load.start()
    for fetch in fetches:
        fetch.start()
    for k in range(1, CHUNKS):
        for load in loads[k]:
            load.start()
    for fetch in fetches[:count]:
        fetch.wait()
    for k in range(CHUNKS):
        if k == CHUNKS // 2:
            for fetch in fetches[count:]:
                fetch.wait()
        for load in loads[k]:
            load.wait()
        here = slice(k * depth, (k + 1) * depth)
        side = 2 * k // CHUNKS
        columns = slice(k * depth - side * half, (k + 1) * depth - side * half)
        term = jnp.dot(
            x[side * rows : (side + 1) * rows, columns], w[here, :], preferred_element_type=jnp.float32
        )
        if k == 0:
            total[...] = term
        else:
            total[...] += term
    ids_ref[...] = x[:rows, half:]
    own_ref[...] = total[:, : 2 * HD].astype(jnp.bfloat16)
    other_ref[:, : 2 * HD] = total[:, 2 * HD :].astype(jnp.bfloat16)
    other_ref[:, 2 * HD :] = x[:rows, half:]


def projected_shapes(rows):
    return (
        jax.ShapeDtypeStruct((rows, 2 * HD), jnp.bfloat16),
        jax.ShapeDtypeStruct((rows, 3 * HD), jnp.bfloat16),
        jax.ShapeDtypeStruct((rows, HD), jnp.bfloat16),
    )


def project(lows, highs, weights):
    count = len(lows)
    size, wide = lows[0].shape
    rows, width = count * size, 2 * (wide - HD)
    return pl.pallas_call(
        lambda *refs: project_kernel(count, *refs),
        out_shape=projected_shapes(rows)
        + (jax.ShapeDtypeStruct((width, 4 * HD), jnp.bfloat16),),
        in_specs=[pl.BlockSpec(memory_space=pl.ANY)] * (2 * count + 4),
        scratch_shapes=[
            pltpu.VMEM((2 * rows, wide), jnp.bfloat16),
            pltpu.VMEM((rows, 4 * HD), jnp.float32),
            pltpu.SemaphoreType.DMA((2 * count,)),
            pltpu.SemaphoreType.DMA((CHUNKS, 4)),
        ],
        compiler_params=params(18),
        name="project",
    )(*lows, *highs, *weights)


def project_low_kernel(low, w, total_ref):
    half = w.shape[0] // 2
    total_ref[...] = jnp.dot(low[:, :half], w[:half, :], preferred_element_type=jnp.float32)


def project_high_kernel(high, w, low_ref, own_ref, other_ref, ids_ref):
    half = w.shape[0] // 2
    total = low_ref[...]
    total = total + jnp.dot(high[:, :half], w[half:, :], preferred_element_type=jnp.float32)
    ids_ref[...] = high[:, half:]
    own_ref[...] = total[:, : 2 * HD].astype(jnp.bfloat16)
    other_ref[:, : 2 * HD] = total[:, 2 * HD :].astype(jnp.bfloat16)
    other_ref[:, 2 * HD :] = high[:, half:]


def project_last(low, high, weights):
    rows = low.shape[0]
    total = pl.pallas_call(
        project_low_kernel,
        out_shape=jax.ShapeDtypeStruct((rows, weights.shape[1]), jnp.float32),
        compiler_params=params(10),
        name="project_low",
    )(low, weights)
    return pl.pallas_call(
        project_high_kernel,
        out_shape=projected_shapes(rows),
        compiler_params=params(10),
        name="project_high",
    )(high, weights, total)


def origin(shape, dim, head):
    at = lax.broadcasted_iota(jnp.int32, shape, dim)
    turn, d_first, row = (at >> 6) & 3, (at >> 4) & 3, at & 15
    d_second = turn ^ (turn >> 1)
    c = (head & 1) ^ (at >> 8)
    dy = jnp.where(c == 0, d_second, d_first)
    dx = jnp.where(c == 0, d_first, d_second)
    y, x = (head >> 3) ^ dy, ((head >> 1) & 3) ^ dx
    return (((y * NX + x) * 2 + c) << 4) + row


def finish_kernel(groups, cap, own_a, own_b, ids_a, ids_b, their_a, their_b, *refs):
    outs, packed = refs[:groups], refs[groups]
    total = packed.shape[0]
    early, half = own_a.shape[0], total // 2
    head = lax.axis_index("head")
    group = lax.axis_index("grp").astype(jnp.float32)
    packed[:early, :] = own_a[...]
    packed[early:half, :] = own_b[...]
    packed[half : half + early, :] = their_a[:, : 2 * HD]
    packed[half + early :, :] = their_b[:, : 2 * HD]
    ids = [ids_a[...], ids_b[...], their_a[:, 2 * HD :], their_b[:, 2 * HD :]]
    hop = jnp.concatenate(ids, axis=0).astype(jnp.float32) - group
    hop = jnp.where(hop < 0.0, hop + groups, hop)
    lanes = lax.broadcasted_iota(jnp.int32, (1, HD), 1).astype(jnp.float32)
    match = jnp.where(hop == lanes, 1.0, 0.0)
    earlier = origin((1, total), 1, head) < origin((total, 1), 0, head)
    ranks = jnp.dot(
        jnp.where(earlier, 1.0, 0.0).astype(jnp.bfloat16),
        match.astype(jnp.bfloat16),
        preferred_element_type=jnp.float32,
    )
    order = jnp.sum(ranks * match, axis=1, keepdims=True)
    slot = hop[:, :1] * cap + order
    slots = lax.broadcasted_iota(jnp.int32, (1, groups * cap), 1).astype(jnp.float32)
    pick = jnp.where(slots == slot, 1.0, 0.0).astype(jnp.bfloat16)
    routed = lax.dot_general(
        pick, packed[...], (((0,), (0,)), ((), ())), preferred_element_type=jnp.float32
    )
    counts = jnp.sum(match, axis=0, keepdims=True)
    step = lax.broadcasted_iota(jnp.int32, (cap, 1), 0).astype(jnp.float32)
    for g in range(groups):
        rows = slice(g * cap, (g + 1) * cap)
        filled = step < counts[:, g : g + 1]
        outs[g][:, :HD] = jnp.where(filled, routed[rows, :HD], EMPTY).astype(jnp.bfloat16)
        outs[g][:, HD:] = routed[rows, HD:].astype(jnp.bfloat16)


def finish(groups, cap, own_a, own_b, ids_a, ids_b, their_a, their_b):
    shape = jax.ShapeDtypeStruct((cap, 2 * HD), jnp.bfloat16)
    rows = 2 * (own_a.shape[0] + own_b.shape[0])
    return pl.pallas_call(
        lambda *refs: finish_kernel(groups, cap, *refs),
        out_shape=(shape,) * groups,
        scratch_shapes=[pltpu.VMEM((rows, 2 * HD), jnp.bfloat16)],
        compiler_params=params(12),
        name="finish",
    )(own_a, own_b, ids_a, ids_b, their_a, their_b)


def settle_kernel(groups, edge_row, edge_col, high_ref, low_ref, *refs):
    parts = [refs[HOPS.index(g)] for g in range(groups)]
    key_ref, value_ref, bias_ref, hot = refs[groups:]
    cap = parts[0].shape[0]
    slots = groups * cap
    me = lax.axis_index("grp")
    sources = [lax.rem(me + groups - g, groups) for g in range(groups)]
    starts, ends = edge_row[0:1, :], edge_row[1:2, :]
    lanes = lax.broadcasted_iota(jnp.int32, (1, HD), 1).astype(jnp.float32)
    step = lax.broadcasted_iota(jnp.int32, (cap, 1), 0).astype(jnp.float32)
    across = lax.broadcasted_iota(jnp.int32, (1, slots), 1).astype(jnp.float32)
    counts = []
    for part in parts:
        full = part[:, :HD].astype(jnp.float32) < EMPTY / 2
        counts.append(jnp.sum(jnp.where(full, 1.0, 0.0), axis=0, keepdims=True)[:, :1])
    cells = across
    open_slots = across < 0.0
    for g in range(groups):
        base = jnp.zeros((1, 1), jnp.float32)
        for other in range(groups):
            if other != g:
                before = jnp.where(sources[other] < sources[g], 1.0, 0.0)
                base = base + counts[other] * before
        rows = slice(g * cap, (g + 1) * cap)
        cell = base + step
        inside = (cell >= starts) & (cell < ends)
        place = cell - jnp.sum(jnp.where(inside, starts, 0.0), axis=1, keepdims=True)
        hot[rows, :] = jnp.where(lanes == place, 1.0, 0.0).astype(jnp.bfloat16)
        here = (across >= g * cap) & (across < (g + 1) * cap)
        cells = jnp.where(here, across - g * cap + base, cells)
        open_slots = open_slots | (here & (across - g * cap < counts[g]))
        value_ref[rows, :] = parts[g][:, HD:]
    low_edge, high_edge = edge_col[:, 0:1], edge_col[:, HD : HD + 1]
    mine = (cells >= low_edge) & (cells < high_edge) & open_slots
    bias_ref[...] = jnp.where(mine, 0.0, MASKED)
    trig = jnp.dot(hot[...], high_ref[...], preferred_element_type=jnp.float32)
    trig = trig + jnp.dot(hot[...], low_ref[...], preferred_element_type=jnp.float32)
    for g in range(groups):
        rows = slice(g * cap, (g + 1) * cap)
        keys = parts[g][:, :HD].astype(jnp.float32)
        keys = jnp.where(keys < EMPTY / 2, keys, 0.0)
        turned_keys = keys * trig[rows, :HD] + pltpu.roll(keys, HD // 2, 1) * trig[rows, HD:]
        key_ref[rows, :] = turned_keys.astype(jnp.bfloat16)


def settle(edge_row, edge_col, high, low, parts):
    slots = len(parts) * parts[0].shape[0]
    wide = jax.ShapeDtypeStruct((slots, HD), jnp.bfloat16)
    return pl.pallas_call(
        lambda *refs: settle_kernel(len(parts), *refs),
        out_shape=(wide, wide, jax.ShapeDtypeStruct((edge_col.shape[0], slots), jnp.float32)),
        scratch_shapes=[pltpu.VMEM((slots, HD), jnp.bfloat16)],
        compiler_params=params(8),
        name="settle",
    )(edge_row, edge_col, high, low, *parts)


def hold_kernel(count, *refs):
    sems = refs[-1]
    copies = [
        pltpu.make_async_copy(refs[i], refs[count + 1 + i], sems.at[i]) for i in range(count)
    ]
    for copy in copies:
        copy.start()
    for copy in copies:
        copy.wait()


def hold(arrays, dep):
    count = len(arrays)
    return pl.pallas_call(
        lambda *refs: hold_kernel(count, *refs),
        out_shape=tuple(jax.ShapeDtypeStruct(a.shape, a.dtype) for a in arrays),
        in_specs=[pl.BlockSpec(memory_space=pl.ANY)] * (count + 1),
        out_specs=(pl.BlockSpec(memory_space=pltpu.VMEM),) * count,
        scratch_shapes=[pltpu.SemaphoreType.DMA((count,))],
        compiler_params=params(10),
        name="hold",
    )(*arrays, dep)


def rotated(values, turn):
    return values * turn[:, :HD] + pltpu.roll(values, HD // 2, 1) * turn[:, HD:]


def first_kernel(state_ref, gain_ref, wq_ref, wk_ref, wv_ref, *refs):
    query_ref, key_ref, value_ref, current_ref, my_gain_ref, inverse_ref = refs[-6:]
    share = current_ref.shape[1]
    mine = pl.ds(pl.multiple_of(lax.axis_index("head") * share, share), share)
    state = state_ref[...]
    gain = gain_ref[...]
    factor = lax.rsqrt(jnp.mean(state * state, axis=1, keepdims=True) + EPSILON)
    rows = (state * factor * gain).astype(jnp.bfloat16)
    query_ref[...] = jnp.dot(rows, wq_ref[...], preferred_element_type=jnp.float32)
    key_ref[...] = jnp.dot(rows, wk_ref[...], preferred_element_type=jnp.float32)
    value_ref[...] = jnp.dot(rows, wv_ref[...], preferred_element_type=jnp.float32)
    current_ref[...] = state_ref[:, mine]
    my_gain_ref[...] = gain_ref[:, mine]
    inverse_ref[...] = 1.0 / gain


def first(state, gain, weights, share, *deps):
    n, width = state.shape
    small = jax.ShapeDtypeStruct((n, HD), jnp.float32)
    whole = pl.BlockSpec(memory_space=pltpu.VMEM)
    return pl.pallas_call(
        first_kernel,
        out_shape=(small,) * 3
        + tuple(jax.ShapeDtypeStruct(d, jnp.float32) for d in ((n, share), (1, share), (1, width))),
        in_specs=[whole] * 5 + [pl.BlockSpec(memory_space=pl.ANY)] * len(deps),
        compiler_params=params(60),
        name="first",
    )(state, gain.reshape(1, -1), *weights, *deps)


def attend_kernel(step, *refs):
    f32, bf16 = jnp.float32, jnp.bfloat16
    turn_ref, key_ref, cache_ref, bias_ref, out_weight, *rest = refs
    turn = turn_ref[step]
    olds = [(rest[2 * i], rest[2 * i + 1]) for i in range(step)]
    rest = rest[2 * step :]
    if step:
        row_ref, inverse_ref, wq_ref, wk_ref, wv_ref, term_ref, new_key_ref, new_value_ref = rest
        blocks, n, share = row_ref.shape
        squares = jnp.zeros((n, share), f32)
        for i in range(blocks):
            plain = row_ref[i].astype(f32) * inverse_ref[:, i * share : (i + 1) * share]
            squares = squares + plain * plain
        mean = jnp.sum(squares, axis=1, keepdims=True) * (1.0 / (blocks * share))
        factor = lax.rsqrt(mean + EPSILON)
        rows = jnp.concatenate([row_ref[i] for i in range(blocks)], axis=1)
        query = jnp.dot(rows, wq_ref[...], preferred_element_type=f32) * factor
        key = jnp.dot(rows, wk_ref[...], preferred_element_type=f32) * factor
        value = jnp.dot(rows, wv_ref[...], preferred_element_type=f32) * factor
    else:
        query_ref, first_key, first_value, _, _, _, term_ref, new_key_ref, new_value_ref = rest
        query, key, value = query_ref[...], first_key[...], first_value[...]
    query = rotated(query, turn).astype(bf16)
    key = rotated(key, turn).astype(bf16)
    value = value.astype(bf16)
    new_key_ref[...] = key
    new_value_ref[...] = value
    scale = HD ** (-0.5)
    scores = lax.dot_general(
        query, key_ref[...], (((1,), (1,)), ((), ())), preferred_element_type=f32
    )
    scores = scores * scale + bias_ref[...]
    wide = query.astype(f32)
    pairs = [(k[...], v[...]) for k, v in olds] + [(key, value)]
    fresh = [jnp.sum(wide * k.astype(f32), axis=1, keepdims=True) * scale for k, _ in pairs]
    peak = jnp.max(scores, axis=1, keepdims=True)
    for f in fresh:
        peak = jnp.maximum(peak, f)
    cache_exp = jnp.exp(scores - peak)
    fresh_exp = [jnp.exp(f - peak) for f in fresh]
    total = jnp.sum(cache_exp, axis=1, keepdims=True)
    for f in fresh_exp:
        total = total + f
    weights = (cache_exp / total).astype(bf16)
    attended = jnp.dot(weights, cache_ref[...], preferred_element_type=f32)
    for f, (_, v) in zip(fresh_exp, pairs):
        attended = attended + (f / total).astype(bf16).astype(f32) * v.astype(f32)
    attended = attended.astype(bf16)
    blocks, _, share = term_ref.shape
    wide_share = 4 * share
    for j in range(blocks // 4):
        term = jnp.dot(
            attended, out_weight[:, j * wide_share : (j + 1) * wide_share], preferred_element_type=f32
        ).astype(bf16)
        for i in range(4):
            term_ref[4 * j + i] = term[:, i * share : (i + 1) * share]


def attend(step, blocks, turns, keys, cache, bias, w_out, olds, extra):
    n = bias.shape[0]
    share = w_out.shape[1] // blocks
    flat = [x for pair in olds for x in pair]
    small = jax.ShapeDtypeStruct((n, HD), jnp.bfloat16)
    return pl.pallas_call(
        lambda *refs: attend_kernel(step, *refs),
        out_shape=(jax.ShapeDtypeStruct((blocks, n, share), jnp.bfloat16), small, small),
        compiler_params=params(10),
        name="attend",
    )(turns, keys, cache, bias, w_out, *flat, *extra)


def spread_kernel(last, part_ref, current_ref, gain_ref, *refs):
    next_ref, *out = refs[-1:] if last else refs[-2:]
    total = current_ref[...]
    for i in range(part_ref.shape[0]):
        total = total + part_ref[i].astype(jnp.float32)
    next_ref[...] = total
    if not last:
        piece = (total * gain_ref[...]).astype(jnp.bfloat16)
        for i in range(part_ref.shape[0]):
            out[0][i] = piece


def spread(last, parts, current, gain, held):
    shapes = [jax.ShapeDtypeStruct(current.shape, jnp.float32)]
    if not last:
        shapes.append(jax.ShapeDtypeStruct(parts.shape, jnp.bfloat16))
    return pl.pallas_call(
        lambda *refs: spread_kernel(last, *refs),
        out_shape=tuple(shapes),
        compiler_params=params(4),
        name="spread",
    )(parts, current, gain, *held)


def per_device(
    prefill_rows, row_group, lengths, decode_state, norm_gain, w_query, w_key, w_value, w_out
):
    groups = lax.axis_size("grp")
    heads = lax.axis_size("head")
    rows_local, width = prefill_rows.shape
    cap = (rows_local // groups + rows_local // groups // 2) * heads
    requests = lengths.shape[1]
    my_group = lax.axis_index("grp")
    my_head = lax.axis_index("head")
    share = width // heads
    f32, bf16 = jnp.float32, jnp.bfloat16

    with jax.named_scope("rows"):
        start = norm_rows(row_group, prefill_rows, norm_gain)
        f2 = send(start, lane(2, 0))
        f1 = send(start, lane(1, 0))
        f3 = send(start, lane(3, 0))
        both_weights = [w_key, w_value, send(w_key, CORE), send(w_value, CORE)]
        l0, l1 = lines(start, f1, f2, f3, both_weights[2][:16])
        s11 = send(l1, lane(0, 1))
        s30 = send(l0, lane(0, 3))
        s10 = send(l0, lane(0, 1))
        s31 = send(l1, lane(0, 3))
        s20 = send(s30, lane(0, 1))
        s21 = send(s11, lane(0, 3))
    with jax.named_scope("places"):
        group_ids = jnp.arange(groups, dtype=jnp.int32)
        late_lengths = after(lengths, f1)
        my_lengths = jnp.sum(
            jnp.where((group_ids == my_group)[:, None], late_lengths, 0), axis=0
        )
        request = jnp.arange(requests, dtype=jnp.int32)
        my_ends = jnp.sum(jnp.where(request[None, :] <= request[:, None], my_lengths[None, :], 0), axis=1)
        my_starts = my_ends - my_lengths
        edges = jnp.stack([my_starts, my_ends]).astype(f32)
        edge_row = jnp.pad(edges, ((0, 0), (0, HD - requests)), constant_values=1e9)
        edge_col = jnp.repeat(edges, HD, axis=0).T.reshape(requests, 2 * HD)
        spots = jnp.arange(HD, dtype=jnp.int32) + 0 * my_lengths[0]
        table = jnp.concatenate(angles_of(spots), axis=1)
        table_high = table.astype(bf16)
        table_low = (table - table_high.astype(f32)).astype(bf16)

    with jax.named_scope("project"):
        own_a, other_a, ids_a, wide_weights = project([l0, s10, s30], [l1, s11, s31], both_weights)
        own_b, other_b, ids_b = project_last(s20, s21, wide_weights)
        leaving = finish(
            groups, cap, own_a, own_b, ids_a, ids_b, send(other_a, CORE), send(other_b, CORE)
        )
        arrived = [leaving[0]]
        for hop in HOPS[1:]:
            pairs = [(g, (g + hop) % groups) for g in range(groups)]
            arrived.append(lax.ppermute(leaving[hop], "grp", pairs))
        (w_out,) = hold([w_out], leaving[0])
        cache_keys, cache_values, bias = settle(edge_row, edge_col, table_high, table_low, arrived)

    with jax.named_scope("first"):
        extra = first(decode_state, norm_gain, (w_query, w_key, w_value), share)
        current, my_gain, inverse = extra[3:]
        at_step = my_lengths[None, :] + jnp.arange(STEPS, dtype=jnp.int32)[:, None]
        turns = jnp.concatenate(angles_of(at_step), axis=-1)
    held = [w_query, w_key, w_value, w_out]
    olds = []
    for step in range(STEPS):
        term, new_key, new_value = attend(
            step, heads, turns, cache_keys, cache_values, bias, w_out, olds, extra
        )
        olds.append((new_key, new_value))
        parts = lax.all_to_all(term, "head", split_axis=0, concat_axis=0, tiled=True)
        last = step + 1 == STEPS
        current, *spreading = spread(last, parts, current, my_gain, [] if last else held)
        if not last:
            rows = lax.all_to_all(spreading[0], "head", split_axis=0, concat_axis=0, tiled=True)
            extra = [rows, inverse, w_query, w_key, w_value]
    return current


def solution(mesh):
    return jax.shard_map(
        per_device,
        mesh=mesh,
        in_specs=(
            P(("grp", "head"), None),
            P(("grp", "head")),
            P(),
            P("grp", None),
            P(),
            P(None, "head"),
            P(None, "head"),
            P(None, "head"),
            P("head", None),
        ),
        out_specs=P("grp", "head"),
        check_vma=False,
    )
```
